512 devices in a mesh: px: 32 (over x_hi, y, core), py: 16 (over x_lo, z).
Axes of the slice: x: 4 (x_hi: 2, x_lo: 2; x = x_hi * 2 + x_lo), y: 8, z: 8, core: 2. Of those that a mesh axis runs over, the one named last changes fastest.
Arguments:
- trial_block: float32 [32, 16, 2, 8, 8192], P('px', 'py'), may hold values from -12 to 12
- stiff_coef: float32 [32, 16, 1024], P('px', 'py'), may hold values from 0.3 to 3
- mass_coef: float32 [32, 16, 1024], P('px', 'py'), may hold values from 1 to 12
- elem_count: int32 [32, 16], P('px', 'py'), may hold values from 256 to 1024, as said below
- elem_dofs: int32 [32, 16, 1024, 20], P('px', 'py'), may hold values from 0 to 12287, as said below
- pairing: int32 [2048], replicated, may hold values from 0 to 2047, each once
- bloch_fraction: int32 [2], replicated, may hold values from 1 to 16, as said below
- stiff_ref: float32 [20, 20], replicated, may hold values from -16 to 17, as said below
- mass_ref: float32 [20, 20], replicated, may hold values from -16 to 17, as said below
Outputs:
- curl_image: float32 [32, 16, 2, 8, 8192], P('px', 'py')
- mass_image: float32 [32, 16, 2, 8, 8192], P('px', 'py')
- gram: float32 [2, 2, 8, 8], replicated
The draws below stay inside these ranges and needn't reach their ends.
Inputs may be any that keep to these rules, and one draw needn't show every extreme that they name: `elem_count`: element slots below 128 are the only ones that name indices of 8192 or more; each part's count is at least 256, and each part of a 2-by-2 block of parts has exactly 1024 in every draw. `elem_dofs`: indices into the extended layout; slots at or above 128 name only indices below 8192. bloch_fraction[1] is 16 and 0 < bloch_fraction[0] < bloch_fraction[1]. `stiff_ref`: symmetric positive definite. `mass_ref`: symmetric positive definite.
All inputs are finite; a program needn't handle non-finite values.
Results may differ from the reference program's by a relative error of at most 0.0003.
Values sent between devices are 32-bit elements; how exact they have to be, the bound alone decides.
A program may use at most 64 MiB of HBM per device.

```python
import math
import jax
import jax.numpy as jnp
from jax import lax

NVEC = 8
NLOC = 20
INTERIOR = 4096
FACE = 2048
ELEM_CAP = 1024
OWNED = 8192
EXTENDED = 12288
N_PX = 32
N_PY = 16


def draw_trial_block(key, part):
    shape = (N_PX, N_PY, 2, NVEC, OWNED)
    row_pos = jnp.arange(N_PX, dtype=jnp.float32).reshape(N_PX, 1, 1, 1, 1) / max(N_PX - 1, 1)
    scale = 1.0 + 2.0 * row_pos
    values = jax.random.truncated_normal(key, -4.0, 4.0, shape, jnp.float32) * scale
    return values


def draw_elem_count(key, part):
    base_key = jax.random.fold_in(key, 21)
    row_key = jax.random.fold_in(key, 22)
    col_key = jax.random.fold_in(key, 23)
    base = jax.random.randint(base_key, (N_PX, N_PY), ELEM_CAP // 4, ELEM_CAP // 2 + 1)
    row_start = jax.random.randint(row_key, (), 0, N_PX)
    col_start = jax.random.randint(col_key, (), 0, N_PY - 1)
    row_ids = jnp.arange(N_PX, dtype=jnp.int32).reshape(N_PX, 1)
    col_ids = jnp.arange(N_PY, dtype=jnp.int32).reshape(1, N_PY)
    in_rows = (row_ids == row_start) | (row_ids == (row_start + 1) % N_PX)
    in_cols = (col_ids == col_start) | (col_ids == col_start + 1)
    return jnp.where(in_rows & in_cols, ELEM_CAP, base).astype(jnp.int32)


def draw_elem_dofs(key, part):
    shape = (N_PX, N_PY, ELEM_CAP, NLOC)
    owned_pick = jax.random.randint(jax.random.fold_in(key, 31), shape, 0, OWNED)
    face_pick = jax.random.randint(jax.random.fold_in(key, 32), shape, OWNED, EXTENDED)
    slot_ids = jnp.arange(ELEM_CAP, dtype=jnp.int32).reshape(1, 1, ELEM_CAP, 1)
    local_ids = jnp.arange(NLOC, dtype=jnp.int32).reshape(1, 1, 1, NLOC)
    use_face = (slot_ids < ELEM_CAP // 8) & (local_ids < 8)
    return jnp.where(use_face, face_pick, owned_pick).astype(jnp.int32)


def draw_bloch_fraction(key, part):
    denominator = jnp.full((), 16, jnp.int32)
    numerator = jax.random.randint(jax.random.fold_in(key, 42), (), 1, 16)
    return jnp.stack([numerator, denominator]).astype(jnp.int32)


def symmetric_matrix(key, diag_shift):
    shape = (NLOC, NLOC)
    factor = jax.random.truncated_normal(key, -4.0, 4.0, shape, jnp.float32)
    product = jnp.dot(factor, factor.T, precision=lax.Precision.HIGHEST) / NLOC
    return product + diag_shift * jnp.eye(NLOC, dtype=jnp.float32)


def draw_stiff_ref(key, part):
    return symmetric_matrix(jax.random.fold_in(key, 51), 0.5)


def draw_mass_ref(key, part):
    return symmetric_matrix(jax.random.fold_in(key, 52), 1.0)


def level_of(key, shape, pieces, low, top_value):
    gain, own = 1.0, jax.random.fold_in(key, 6)
    for axis_at, shards_of in pieces:
        draws = jnp.exp(jax.random.uniform(jax.random.fold_in(own, axis_at), (shards_of,), jnp.float32, low / len(pieces), top_value / len(pieces)))
        gain = gain * jnp.repeat(draws, shape[axis_at] // shards_of).reshape([-1 if axis == axis_at else 1 for axis in range(len(shape))])
    return gain


def setup_inputs(seed: int = 0) -> dict:
    splits = jax.random.split(jax.random.key(seed), 10)
    trial_block = draw_trial_block(jax.random.fold_in(splits[9], 71), 0)
    stiff_coef = jnp.clip(jnp.exp(math.log(3.0) - 2.3025851 * jax.random.uniform(splits[1], (N_PX, N_PY, ELEM_CAP), jnp.float32) ** level_of(splits[1], (N_PX, N_PY, ELEM_CAP), ((0, 32), (1, 16)), -0.2, 0.2)), 0.3, 3.0)
    mass_coef = jnp.clip(jnp.exp(math.log(12.0) - 2.4849066 * jax.random.uniform(splits[2], (N_PX, N_PY, ELEM_CAP), jnp.float32) ** level_of(splits[2], (N_PX, N_PY, ELEM_CAP), ((0, 32), (1, 16)), -0.2, 0.2)), 1.0, 12.0)
    elem_count = draw_elem_count(jax.random.fold_in(splits[9], 71), 0)
    elem_dofs = draw_elem_dofs(jax.random.fold_in(splits[9], 71), 0)
    pairing = jax.random.permutation(splits[5], FACE).astype(jnp.int32)
    bloch_fraction = draw_bloch_fraction(jax.random.fold_in(splits[9], 71), 0)
    stiff_ref = draw_stiff_ref(jax.random.fold_in(splits[9], 71), 0)
    mass_ref = draw_mass_ref(jax.random.fold_in(splits[9], 71), 0)
    return {"trial_block": trial_block, "stiff_coef": stiff_coef, "mass_coef": mass_coef, "elem_count": elem_count, "elem_dofs": elem_dofs, "pairing": pairing, "bloch_fraction": bloch_fraction, "stiff_ref": stiff_ref, "mass_ref": mass_ref}


HIGH = lax.Precision.HIGHEST


def extended_all(trial_block, pairing, cosine, sine_part):
    low_x = trial_block[..., INTERIOR:INTERIOR + FACE]
    low_y = trial_block[..., INTERIOR + FACE:OWNED]
    high_x = jnp.roll(low_x, -1, axis=0)
    wrapped = low_x[0][..., pairing]
    turned = jnp.stack([cosine * wrapped[:, 0] - sine_part * wrapped[:, 1], sine_part * wrapped[:, 0] + cosine * wrapped[:, 1]], axis=1)
    high_x = high_x.at[N_PX - 1].set(turned)
    high_y = jnp.concatenate([low_y[:, 1:], jnp.zeros_like(low_y[:, :1])], axis=1)
    return jnp.concatenate([trial_block, high_x, high_y], axis=-1)


def part_images(ext_part, stiff_part, mass_part, live_total, slot_dofs, stiff_ref, mass_ref):
    flat_rows = ext_part.reshape(2 * NVEC, EXTENDED)
    index_t = slot_dofs.T
    gathered = flat_rows[:, index_t]
    live_mask = (jnp.arange(ELEM_CAP, dtype=jnp.int32) < live_total).astype(jnp.float32)
    curl_terms = jnp.einsum("ji,rie->rje", stiff_ref, gathered, precision=HIGH, preferred_element_type=jnp.float32) * (stiff_part * live_mask)
    mass_terms = jnp.einsum("ji,rie->rje", mass_ref, gathered, precision=HIGH, preferred_element_type=jnp.float32) * (mass_part * live_mask)
    zero_rows = jnp.zeros((2 * NVEC, EXTENDED), jnp.float32)
    curl_ext = zero_rows.at[:, index_t].add(curl_terms)
    mass_ext = zero_rows.at[:, index_t].add(mass_terms)
    return curl_ext.reshape(2, NVEC, EXTENDED), mass_ext.reshape(2, NVEC, EXTENDED)


def assemble(images, pairing, cosine, sine_part):
    owned_part = images[..., :OWNED]
    side_x = images[..., OWNED:OWNED + FACE]
    side_y = images[..., OWNED + FACE:]
    back_x = jnp.roll(side_x, 1, axis=0)
    source = side_x[N_PX - 1]
    turned = jnp.stack([cosine * source[:, 0] + sine_part * source[:, 1], cosine * source[:, 1] - sine_part * source[:, 0]], axis=1)
    placed = jnp.zeros_like(turned).at[..., pairing].set(turned)
    back_x = back_x.at[0].set(placed)
    back_y = jnp.concatenate([jnp.zeros_like(side_y[:, :1]), side_y[:, :-1]], axis=1)
    owned_part = owned_part.at[..., INTERIOR:INTERIOR + FACE].add(back_x)
    owned_part = owned_part.at[..., INTERIOR + FACE:OWNED].add(back_y)
    return owned_part


def gram_of(left_vec, right_vec):
    real_part = jnp.dot(left_vec[0], right_vec[0].T, precision=HIGH, preferred_element_type=jnp.float32) + jnp.dot(left_vec[1], right_vec[1].T, precision=HIGH, preferred_element_type=jnp.float32)
    imag_part = jnp.dot(left_vec[0], right_vec[1].T, precision=HIGH, preferred_element_type=jnp.float32) - jnp.dot(left_vec[1], right_vec[0].T, precision=HIGH, preferred_element_type=jnp.float32)
    return jnp.stack([real_part, imag_part])


def reference(trial_block, stiff_coef, mass_coef, elem_count, elem_dofs, pairing, bloch_fraction, stiff_ref, mass_ref):
    phase_angle = 2.0 * jnp.pi * bloch_fraction[0].astype(jnp.float32) / bloch_fraction[1].astype(jnp.float32)
    cosine = jnp.cos(phase_angle)
    sine_part = jnp.sin(phase_angle)
    parts_all = N_PX * N_PY
    extended = extended_all(trial_block, pairing, cosine, sine_part)

    def one_part(items):
        return part_images(items[0], items[1], items[2], items[3], items[4], stiff_ref, mass_ref)

    curl_ext, mass_ext = lax.map(one_part, (extended.reshape(parts_all, 2, NVEC, EXTENDED), stiff_coef.reshape(parts_all, ELEM_CAP), mass_coef.reshape(parts_all, ELEM_CAP), elem_count.reshape(parts_all), elem_dofs.reshape(parts_all, ELEM_CAP, NLOC)))
    curl_ext = curl_ext.reshape(N_PX, N_PY, 2, NVEC, EXTENDED)
    mass_ext = mass_ext.reshape(N_PX, N_PY, 2, NVEC, EXTENDED)
    curl_image = assemble(curl_ext, pairing, cosine, sine_part)
    mass_image = assemble(mass_ext, pairing, cosine, sine_part)

    def flatten(values):
        return jnp.moveaxis(values.reshape(parts_all, 2, NVEC, OWNED), 0, 2).reshape(2, NVEC, parts_all * OWNED)

    left_vec = flatten(trial_block)
    gram = jnp.stack([gram_of(left_vec, flatten(curl_image)), gram_of(left_vec, flatten(mass_image))]) / (parts_all * OWNED)
    return curl_image, mass_image, gram
```

```python
import functools
import math

import jax
import jax.numpy as jnp
from jax import lax
from jax.experimental import pallas as pl
from jax.experimental.pallas import tpu as pltpu
from jax.sharding import PartitionSpec as P

HIGH = lax.Precision.HIGHEST
LANES = 128
ROWS = 16
NLOC = 20
HALO_SLOTS = 128
BLOCK = 128
TILES = 5
GTILES = 3
LANE_SETS = 4

VMEM = pl.BlockSpec(memory_space=pltpu.VMEM)
SMEM = pl.BlockSpec(memory_space=pltpu.SMEM)


def split_bf16(value):
    high = value.astype(jnp.bfloat16)
    low = (value - high.astype(jnp.float32)).astype(jnp.bfloat16)
    return high, low


def dot_split(a, b):
    (ah, al), (bh, bl) = a, b
    dot = functools.partial(jnp.dot, preferred_element_type=jnp.float32)
    return dot(ah, bh) + (dot(al, bh) + dot(ah, bl))


def prepare_kernel(wrap_ref, dofs_ref, pairing_ref, stiff_ref, mass_ref, idx_out, kh_out, kl_out):
    face = pairing_ref.shape[0] * LANES
    owned = 4 * face
    idx_out[...] = dofs_ref[...]
    head = dofs_ref[:, :HALO_SLOTS]
    spot = head - owned
    local = spot & (LANES - 1)
    found = jnp.zeros_like(head)
    for row in range(pairing_ref.shape[0]):
        values = jnp.broadcast_to(pairing_ref[row : row + 1, :], head.shape)
        here = jnp.take_along_axis(values, local, axis=1)
        found = jnp.where((spot >> 7) == row, here + owned, found)
    wraps = (spot >= 0) & (spot < face) & (wrap_ref[0] == 1)
    idx_out[:, :HALO_SLOTS] = jnp.where(wraps, found, head)

    grow = lax.broadcasted_iota(jnp.int32, (GTILES * LANES, NLOC), 0)
    gcol = lax.broadcasted_iota(jnp.int32, (GTILES * LANES, NLOC), 1)
    spread_i = ((grow >> 4) == gcol).astype(jnp.float32)
    trow = lax.broadcasted_iota(jnp.int32, (NLOC, TILES * LANES), 0)
    tcol = lax.broadcasted_iota(jnp.int32, (NLOC, TILES * LANES), 1)
    spread_j = ((tcol >> 5) == trow).astype(jnp.float32)
    dot = functools.partial(jnp.dot, precision=HIGH, preferred_element_type=jnp.float32)
    stiff = dot(dot(spread_i, stiff_ref[...].T), spread_j)
    mass = dot(dot(spread_i, mass_ref[...].T), spread_j)
    krow = lax.broadcasted_iota(jnp.int32, (GTILES * LANES, TILES * LANES), 0)
    kcol = lax.broadcasted_iota(jnp.int32, (GTILES * LANES, TILES * LANES), 1)
    both = jnp.where(((kcol >> 4) & 1) == 0, stiff, mass)
    both = jnp.where((krow & 15) == (kcol & 15), both, 0.0)
    kh_out[...], kl_out[...] = split_bf16(both)


def part_kernel(
    count_ref,
    phase_ref,
    idx_s,
    idx_v,
    own_ref,
    high_x_ref,
    high_y_ref,
    stiff_ref,
    mass_ref,
    kh_ref,
    kl_ref,
    curl_out,
    mass_out,
    side_x_out,
    side_y_out,
    gram_out,
    ext,
    acc0,
    acc1,
    acc2,
    acc3,
    gathered,
    terms,
    gram,
):
    accs = (acc0, acc1, acc2, acc3)
    owned = own_ref.shape[1]
    face = high_x_ref.shape[1]
    cosine, sine = phase_ref[0], phase_ref[1]
    count = count_ref[0, 0]

    def put_rows(at, block):
        ext[pl.ds(at, LANES), :] = jnp.concatenate([block] * (LANES // ROWS), axis=0).T

    @pl.loop(0, owned // LANES)
    def _(b):
        at = pl.multiple_of(b * LANES, LANES)
        put_rows(at, own_ref[:, pl.ds(at, LANES)])

    @pl.loop(0, face // LANES)
    def _(b):
        at = pl.multiple_of(b * LANES, LANES)
        got = high_x_ref[:, pl.ds(at, LANES)]
        real, imag = got[: ROWS // 2], got[ROWS // 2 :]
        turned = jnp.concatenate([cosine * real - sine * imag, sine * real + cosine * imag], axis=0)
        put_rows(owned + at, turned)
        put_rows(owned + face + at, high_y_ref[:, pl.ds(at, LANES)])

    zero_rows = jnp.zeros((LANES, LANES), jnp.float32)

    @pl.loop(0, ext.shape[0] // LANES)
    def _(b):
        at = pl.multiple_of(b * LANES, LANES)
        for acc in accs:
            acc[pl.ds(at, LANES), :] = zero_rows

    gram[...] = jnp.zeros_like(gram)
    lane_set = lax.broadcasted_iota(jnp.int32, (1, LANES), 1) >> 4

    @pl.loop(0, (count + BLOCK - 1) // BLOCK)
    def _(block_id):
        first = pl.multiple_of(block_id * BLOCK, BLOCK)

        @pl.loop(0, BLOCK, unroll=4)
        def _(e):
            slot = first + e
            for tile in range(GTILES):
                inside = range(8 * tile, min(8 * tile + 8, NLOC))
                row = None
                for i in inside:
                    got = ext[pl.ds(idx_s[i, slot], 1), :]
                    row = got if row is None else jnp.where(lane_set == i % 8, got, row)
                gathered[tile, pl.ds(e, 1), :] = row

        values = jnp.concatenate([gathered[tile] for tile in range(GTILES)], axis=1)
        pieces = split_bf16(values)
        products = dot_split(pieces, (kh_ref[...], kl_ref[...]))
        slots = first + lax.broadcasted_iota(jnp.int32, (1, BLOCK), 1)
        live = slots < count
        stiff = jnp.where(live, stiff_ref[:, pl.ds(first, BLOCK)], 0.0)
        mass = jnp.where(live, mass_ref[:, pl.ds(first, BLOCK)], 0.0)
        pair = [jnp.broadcast_to(stiff, (ROWS, BLOCK)), jnp.broadcast_to(mass, (ROWS, BLOCK))]
        coef = jnp.concatenate(pair * LANE_SETS, axis=0).T
        scaled = [products[:, t * LANES : (t + 1) * LANES] * coef for t in range(TILES)]

        turned = split_bf16(values.T)
        for t in range(TILES):
            gram[:, t * LANES : (t + 1) * LANES] += dot_split(turned, split_bf16(scaled[t]))

        names = []
        for t in range(TILES):
            rows = [
                jnp.broadcast_to(idx_v[j : j + 1, pl.ds(first, BLOCK)], (LANES // LANE_SETS, BLOCK))
                for j in range(LANE_SETS * t, LANE_SETS * t + LANE_SETS)
            ]
            names.append(jnp.concatenate(rows, axis=0).astype(jnp.float32).T)
        for t in range(TILES):
            total = scaled[t]
            for s in range(t):
                total = total + jnp.where(names[s] == names[t], scaled[s], 0.0)
            terms[t] = total

        @pl.loop(0, BLOCK, unroll=2)
        def _(e):
            slot = first + e
            added = [terms[t, pl.ds(e, 1), :] for t in range(TILES)]
            places = [[idx_s[LANE_SETS * t + g, slot] for t in range(TILES)] for g in range(LANE_SETS)]
            held = [[accs[g][pl.ds(places[g][t], 1), :] for t in range(TILES)] for g in range(LANE_SETS)]
            for t in range(TILES):
                for g in range(LANE_SETS):
                    accs[g][pl.ds(places[g][t], 1), :] = held[g][t] + added[t]

    quarter = lax.broadcasted_iota(jnp.int32, (LANES, LANES), 1) >> 5

    def summed(at):
        rows = accs[0][pl.ds(at, LANES), :]
        for g in range(1, LANE_SETS):
            rows = jnp.where(quarter == g, accs[g][pl.ds(at, LANES), :], rows)
        rows = rows.T
        return (rows[:32] + rows[32:64]) + (rows[64:96] + rows[96:])

    @pl.loop(0, owned // LANES)
    def _(b):
        at = pl.multiple_of(b * LANES, LANES)
        both = summed(at)
        curl_out[:, pl.ds(at, LANES)] = both[:ROWS]
        mass_out[:, pl.ds(at, LANES)] = both[ROWS:]

    @pl.loop(0, face // LANES)
    def _(b):
        at = pl.multiple_of(b * LANES, LANES)
        both = summed(owned + at)
        for op in range(2):
            real, imag = both[ROWS * op : ROWS * op + 8], both[ROWS * op + 8 : ROWS * op + ROWS]
            side_x_out[ROWS * op : ROWS * op + 8, pl.ds(at, LANES)] = cosine * real + sine * imag
            side_x_out[ROWS * op + 8 : ROWS * op + ROWS, pl.ds(at, LANES)] = cosine * imag - sine * real
        side_y_out[:, pl.ds(at, LANES)] = summed(owned + face + at)

    total = jnp.zeros((ROWS, LANES), jnp.float32)
    for j in range(NLOC):
        t = j // LANE_SETS
        piece = gram[j * ROWS : (j + 1) * ROWS, t * LANES : (t + 1) * LANES]
        lanes = lax.broadcasted_iota(jnp.int32, (ROWS, LANES), 1) >> 5
        total = total + jnp.where(lanes == j % LANE_SETS, piece, 0.0)
    gram_out[...] = total


def prepare(wraps, dofs, pairing, stiff_mat, mass_mat):
    shape = jax.ShapeDtypeStruct
    wide = (GTILES * LANES, TILES * LANES)
    return pl.pallas_call(
        prepare_kernel,
        out_shape=(
            shape(dofs.shape, jnp.int32),
            shape(wide, jnp.bfloat16),
            shape(wide, jnp.bfloat16),
        ),
        in_specs=[SMEM, VMEM, VMEM, VMEM, VMEM],
        out_specs=(VMEM, VMEM, VMEM),
        compiler_params=pltpu.CompilerParams(vmem_limit_bytes=16 * 2**20),
        name="prepare",
    )(wraps, dofs, pairing, stiff_mat, mass_mat)


def part_images(count, phase, idx, own, high_x, high_y, stiff, mass, kh, kl):
    shape = jax.ShapeDtypeStruct
    owned, face = own.shape[1], high_x.shape[1]
    extent = owned + 2 * face
    f32 = jnp.float32
    return pl.pallas_call(
        part_kernel,
        out_shape=(
            shape((ROWS, owned), f32),
            shape((ROWS, owned), f32),
            shape((2 * ROWS, face), f32),
            shape((2 * ROWS, face), f32),
            shape((ROWS, LANES), f32),
        ),
        in_specs=[SMEM, SMEM, SMEM] + [VMEM] * 8,
        out_specs=(VMEM,) * 5,
        scratch_shapes=[pltpu.VMEM((extent, LANES), f32)] * 5
        + [
            pltpu.VMEM((GTILES, BLOCK, LANES), f32),
            pltpu.VMEM((TILES, BLOCK, LANES), f32),
            pltpu.VMEM((GTILES * LANES, TILES * LANES), f32),
        ],
        compiler_params=pltpu.CompilerParams(vmem_limit_bytes=56 * 2**20),
        name="part_images",
    )(count, phase, idx, idx, own, high_x, high_y, stiff, mass, kh, kl)


def on_device(
    trial_block,
    stiff_coef,
    mass_coef,
    elem_count,
    elem_dofs,
    pairing,
    bloch_fraction,
    stiff_mat,
    mass_mat,
):
    owned = trial_block.shape[-1]
    face = pairing.shape[0]
    interior = owned - 2 * face
    own = trial_block.reshape(ROWS, owned)
    n_px, n_py = lax.axis_size("px"), lax.axis_size("py")
    down_x = [((a + 1) % n_px, a) for a in range(n_px)]
    down_y = [(b + 1, b) for b in range(n_py - 1)]
    high_x = lax.ppermute(own[:, interior : interior + face], "px", down_x)
    high_y = lax.ppermute(own[:, interior + face :], "py", down_y)

    angle = 2.0 * math.pi * bloch_fraction[0].astype(jnp.float32) / bloch_fraction[1].astype(jnp.float32)
    at_end = lax.axis_index("px") == n_px - 1
    phase = jnp.stack([jnp.where(at_end, jnp.cos(angle), 1.0), jnp.where(at_end, jnp.sin(angle), 0.0)])
    wraps = at_end.astype(jnp.int32).reshape(1)
    idx, kh, kl = prepare(
        wraps, elem_dofs[0, 0].T, pairing.reshape(-1, LANES), stiff_mat, mass_mat
    )
    curl, mass, side_x, side_y, gram = part_images(
        elem_count, phase, idx, own, high_x, high_y, stiff_coef[0], mass_coef[0], kh, kl
    )
    back_x = lax.ppermute(side_x, "px", [(a, (a + 1) % n_px) for a in range(n_px)])
    back_y = lax.ppermute(side_y, "py", [(b, b + 1) for b in range(n_py - 1)])

    def finish(image, add_x, add_y):
        low_x = image[:, interior : interior + face] + add_x
        low_y = image[:, interior + face :] + add_y
        whole = jnp.concatenate([image[:, :interior], low_x, low_y], axis=1)
        return whole.reshape(trial_block.shape)

    curl = finish(curl, back_x[:ROWS], back_y[:ROWS])
    mass = finish(mass, back_x[ROWS:], back_y[ROWS:])

    gram = lax.psum(gram, ("px", "py")) / float(n_px * n_py * owned)
    gram = gram.reshape(2, 8, LANE_SETS, 2, 2, 8).sum(2)
    real = gram[0, :, :, 0] + gram[1, :, :, 1]
    imag = gram[0, :, :, 1] - gram[1, :, :, 0]
    return curl, mass, jnp.stack([real, imag]).transpose(2, 0, 1, 3)


def solution(mesh):
    return jax.shard_map(
        on_device,
        mesh=mesh,
        in_specs=(
            P("px", "py", None, None, None),
            P("px", "py", None),
            P("px", "py", None),
            P("px", "py"),
            P("px", "py", None, None),
            P(),
            P(),
            P(),
            P(),
        ),
        out_specs=(P("px", "py", None, None, None), P("px", "py", None, None, None), P()),
        check_vma=False,
    )
```

```python
import functools
import math

import jax
import jax.numpy as jnp
from jax import lax
from jax.experimental import pallas as pl
from jax.experimental.pallas import tpu as pltpu
from jax.sharding import PartitionSpec as P

HIGH = lax.Precision.HIGHEST
LANES = 128
ROWS = 16
NLOC = 20
HALO_SLOTS = 128
BLOCK = 128
TILES = 5
GTILES = 3
LANE_SETS = 4

VMEM = pl.BlockSpec(memory_space=pltpu.VMEM)
SMEM = pl.BlockSpec(memory_space=pltpu.SMEM)


def split_bf16(value):
    high = value.astype(jnp.bfloat16)
    low = (value - high.astype(jnp.float32)).astype(jnp.bfloat16)
    return high, low


def dot_split(a, b):
    (ah, al), (bh, bl) = a, b
    dot = functools.partial(jnp.dot, preferred_element_type=jnp.float32)
    return dot(ah, bh) + (dot(al, bh) + dot(ah, bl))


def prepare_kernel(wrap_ref, dofs_ref, pairing_ref, stiff_ref, mass_ref, idx_out, kh_out, kl_out):
    face = pairing_ref.shape[0] * LANES
    owned = 4 * face
    blocks = dofs_ref.shape[0] // NLOC
    idx_out[...] = dofs_ref[...]
    heads = pl.ds(0, NLOC, stride=blocks)
    head = dofs_ref[heads, :]
    spot = head - owned
    local = spot & (LANES - 1)
    found = jnp.zeros_like(head)
    for row in range(pairing_ref.shape[0]):
        values = jnp.broadcast_to(pairing_ref[row : row + 1, :], head.shape)
        here = jnp.take_along_axis(values, local, axis=1)
        found = jnp.where((spot >> 7) == row, here + owned, found)
    wraps = (spot >= 0) & (spot < face) & (wrap_ref[0] == 1)
    idx_out[heads, :] = jnp.where(wraps, found, head)

    grow = lax.broadcasted_iota(jnp.int32, (GTILES * LANES, NLOC), 0)
    gcol = lax.broadcasted_iota(jnp.int32, (GTILES * LANES, NLOC), 1)
    spread_i = ((grow >> 4) == gcol).astype(jnp.float32)
    trow = lax.broadcasted_iota(jnp.int32, (NLOC, TILES * LANES), 0)
    tcol = lax.broadcasted_iota(jnp.int32, (NLOC, TILES * LANES), 1)
    spread_j = ((tcol >> 5) == trow).astype(jnp.float32)
    dot = functools.partial(jnp.dot, precision=HIGH, preferred_element_type=jnp.float32)
    stiff = dot(dot(spread_i, stiff_ref[...].T), spread_j)
    mass = dot(dot(spread_i, mass_ref[...].T), spread_j)
    krow = lax.broadcasted_iota(jnp.int32, (GTILES * LANES, TILES * LANES), 0)
    kcol = lax.broadcasted_iota(jnp.int32, (GTILES * LANES, TILES * LANES), 1)
    both = jnp.where(((kcol >> 4) & 1) == 0, stiff, mass)
    both = jnp.where((krow & 15) == (kcol & 15), both, 0.0)
    kh_out[...], kl_out[...] = split_bf16(both)


def part_kernel(
    count_ref,
    phase_ref,
    idx_s,
    idx_v,
    own_ref,
    high_x_ref,
    high_y_ref,
    stiff_ref,
    mass_ref,
    kh_ref,
    kl_ref,
    curl_out,
    mass_out,
    side_x_out,
    side_y_out,
    gram_out,
    ext,
    acc0,
    acc1,
    acc2,
    acc3,
    gathered,
    terms,
    gram,
):
    accs = (acc0, acc1, acc2, acc3)
    owned = own_ref.shape[1]
    face = high_x_ref.shape[1]
    cosine, sine = phase_ref[0], phase_ref[1]
    count = count_ref[0, 0]
    capacity = stiff_ref.shape[1]
    blocks = capacity // BLOCK

    def put_rows(at, block):
        ext[pl.ds(at, LANES), :] = jnp.concatenate([block] * (LANES // ROWS), axis=0).T

    @pl.loop(0, owned // LANES, unroll=8)
    def _(b):
        at = pl.multiple_of(b * LANES, LANES)
        put_rows(at, own_ref[:, pl.ds(at, LANES)])

    @pl.loop(0, face // LANES, unroll=4)
    def _(b):
        at = pl.multiple_of(b * LANES, LANES)
        got = high_x_ref[:, pl.ds(at, LANES)]
        real, imag = got[: ROWS // 2], got[ROWS // 2 :]
        turned = jnp.concatenate([cosine * real - sine * imag, sine * real + cosine * imag], axis=0)
        put_rows(owned + at, turned)
        put_rows(owned + face + at, high_y_ref[:, pl.ds(at, LANES)])

    zero_rows = jnp.zeros((LANES, LANES), jnp.float32)

    @pl.loop(0, ext.shape[0] // LANES)
    def _(b):
        at = pl.multiple_of(b * LANES, LANES)
        for acc in accs:
            acc[pl.ds(at, LANES), :] = zero_rows

    gram[...] = jnp.zeros_like(gram)
    lane_set = lax.broadcasted_iota(jnp.int32, (1, LANES), 1) >> 4

    @pl.loop(0, (count + BLOCK - 1) // BLOCK)
    def _(block_id):
        first = pl.multiple_of(block_id * BLOCK, BLOCK)

        @pl.loop(0, BLOCK, unroll=4)
        def _(e):
            slot = first + e
            for tile in range(GTILES):
                inside = range(8 * tile, min(8 * tile + 8, NLOC))
                row = None
                for i in inside:
                    got = ext[pl.ds(idx_s[slot + i * capacity], 1), :]
                    row = got if row is None else jnp.where(lane_set == i % 8, got, row)
                gathered[tile, pl.ds(e, 1), :] = row

        values = jnp.concatenate([gathered[tile] for tile in range(GTILES)], axis=1)
        pieces = split_bf16(values)
        products = dot_split(pieces, (kh_ref[...], kl_ref[...]))
        slots = first + lax.broadcasted_iota(jnp.int32, (1, BLOCK), 1)
        live = slots < count
        stiff = jnp.where(live, stiff_ref[:, pl.ds(first, BLOCK)], 0.0)
        mass = jnp.where(live, mass_ref[:, pl.ds(first, BLOCK)], 0.0)
        pair = [jnp.broadcast_to(stiff, (ROWS, BLOCK)), jnp.broadcast_to(mass, (ROWS, BLOCK))]
        coef = jnp.concatenate(pair * LANE_SETS, axis=0).T
        scaled = [products[:, t * LANES : (t + 1) * LANES] * coef for t in range(TILES)]

        turned = split_bf16(values.T)
        for t in range(TILES):
            gram[:, t * LANES : (t + 1) * LANES] += dot_split(turned, split_bf16(scaled[t]))

        names = []
        for t in range(TILES):
            rows = [
                jnp.broadcast_to(idx_v[pl.ds(j * blocks + block_id, 1), :], (LANES // LANE_SETS, BLOCK))
                for j in range(LANE_SETS * t, LANE_SETS * t + LANE_SETS)
            ]
            names.append(jnp.concatenate(rows, axis=0).astype(jnp.float32).T)
        for t in range(TILES):
            total = scaled[t]
            for s in range(t):
                total = total + jnp.where(names[s] == names[t], scaled[s], 0.0)
            terms[t] = total

        @pl.loop(0, BLOCK, unroll=2)
        def _(e):
            slot = first + e
            added = [terms[t, pl.ds(e, 1), :] for t in range(TILES)]
            places = [[idx_s[slot + (LANE_SETS * t + g) * capacity] for t in range(TILES)] for g in range(LANE_SETS)]
            held = [[accs[g][pl.ds(places[g][t], 1), :] for t in range(TILES)] for g in range(LANE_SETS)]
            for t in range(TILES):
                for g in range(LANE_SETS):
                    accs[g][pl.ds(places[g][t], 1), :] = held[g][t] + added[t]

    quarter = lax.broadcasted_iota(jnp.int32, (LANES, LANES), 1) >> 5

    def summed(at):
        rows = accs[0][pl.ds(at, LANES), :]
        for g in range(1, LANE_SETS):
            rows = jnp.where(quarter == g, accs[g][pl.ds(at, LANES), :], rows)
        rows = rows.T
        return (rows[:32] + rows[32:64]) + (rows[64:96] + rows[96:])

    @pl.loop(0, owned // LANES, unroll=4)
    def _(b):
        at = pl.multiple_of(b * LANES, LANES)
        both = summed(at)
        curl_out[:, pl.ds(at, LANES)] = both[:ROWS]
        mass_out[:, pl.ds(at, LANES)] = both[ROWS:]

    @pl.loop(0, face // LANES, unroll=2)
    def _(b):
        at = pl.multiple_of(b * LANES, LANES)
        both = summed(owned + at)
        for op in range(2):
            real, imag = both[ROWS * op : ROWS * op + 8], both[ROWS * op + 8 : ROWS * op + ROWS]
            side_x_out[ROWS * op : ROWS * op + 8, pl.ds(at, LANES)] = cosine * real + sine * imag
            side_x_out[ROWS * op + 8 : ROWS * op + ROWS, pl.ds(at, LANES)] = cosine * imag - sine * real
        side_y_out[:, pl.ds(at, LANES)] = summed(owned + face + at)

    total = jnp.zeros((ROWS, LANES), jnp.float32)
    for j in range(NLOC):
        t = j // LANE_SETS
        piece = gram[j * ROWS : (j + 1) * ROWS, t * LANES : (t + 1) * LANES]
        lanes = lax.broadcasted_iota(jnp.int32, (ROWS, LANES), 1) >> 5
        total = total + jnp.where(lanes == j % LANE_SETS, piece, 0.0)
    for shift in (LANES // 2, LANES // 4):
        total = total + pltpu.roll(total, shift, 1)
    of_real, of_imag = total[:8], total[8:]
    odd = ((lax.broadcasted_iota(jnp.int32, (8, LANES), 1) >> 3) & 1) == 1
    gram_out[...] = jnp.where(
        odd, of_real - pltpu.roll(of_imag, 8, 1), of_real + pltpu.roll(of_imag, LANES - 8, 1)
    )


def exchange_kernel(
    side_x_ref,
    side_y_ref,
    gram_ref,
    back_x,
    back_y,
    gram_out,
    along_x,
    row_sum,
    along_y,
    side_send,
    side_recv,
    send_x,
    recv_x,
    send_y,
    recv_y,
):
    n_px, n_py = along_x.shape[0], along_y.shape[0]
    a, b = lax.axis_index("px"), lax.axis_index("py")

    barrier = pltpu.get_barrier_semaphore()

    def greet(axis, me, n):
        @pl.loop(1, n)
        def _(k):
            other = lax.rem(me + k, n)
            pl.semaphore_signal(barrier, 1, device_id={axis: other}, device_id_type=pl.DeviceIdType.MESH)

    greet("px", a, n_px)
    greet("py", b, n_py)
    pl.semaphore_wait(barrier, n_px + n_py - 2)

    def tile_copy(axis, to, source, held, at, send, recv):
        return pltpu.make_async_remote_copy(
            src_ref=source,
            dst_ref=held.at[at],
            send_sem=send.at[to],
            recv_sem=recv.at[at],
            device_id={axis: to},
            device_id_type=pl.DeviceIdType.MESH,
        )

    def send_all(axis, me, n, source, held, send, recv):
        @pl.loop(1, n)
        def _(k):
            tile_copy(axis, lax.rem(me + k, n), source, held, me, send, recv).start()

    def sum_all(axis, me, n, source, held, send, recv):
        held[pl.ds(me, 1)] = source[...][None]

        @pl.loop(1, n)
        def _(k):
            other = lax.rem(me + k, n)
            tile_copy(axis, other, source, held, other, send, recv).wait_recv()

        total = held[0]
        for at in range(1, n):
            total = total + held[at]
        return total

    def sent_all(axis, me, n, source, held, send, recv):
        @pl.loop(1, n)
        def _(k):
            tile_copy(axis, lax.rem(me + k, n), source, held, me, send, recv).wait_send()

    def side_copy(source, held, at, axis, to):
        return pltpu.make_async_remote_copy(
            src_ref=source,
            dst_ref=held,
            send_sem=side_send.at[at],
            recv_sem=side_recv.at[at],
            device_id={axis: to},
            device_id_type=pl.DeviceIdType.MESH,
        )

    over_x = ("px", a, n_px, gram_ref, along_x, send_x, recv_x)
    over_y = ("py", b, n_py, row_sum, along_y, send_y, recv_y)
    to_x = side_copy(side_x_ref, back_x, 0, "px", lax.rem(a + 1, n_px))
    to_y = side_copy(side_y_ref, back_y, 1, "py", lax.rem(b + 1, n_py))
    send_all(*over_x)
    to_x.start()

    @pl.when(b < n_py - 1)
    def _():
        to_y.start()

    row_sum[...] = sum_all(*over_x)
    send_all(*over_y)
    whole = sum_all(*over_y)
    for op in range(2):
        for part in range(2):
            at = 16 * op + 8 * part
            gram_out[op, part] = whole[:, at : at + 8] / gram_scale(n_px, n_py, side_x_ref)
    to_x.wait_recv()

    @pl.when(b > 0)
    def _():
        to_y.wait_recv()

    @pl.when(b == 0)
    def _():
        back_y[...] = jnp.zeros_like(back_y)

    to_x.wait_send()

    @pl.when(b < n_py - 1)
    def _():
        to_y.wait_send()

    sent_all(*over_x)
    sent_all(*over_y)


def gram_scale(n_px, n_py, side_ref):
    return float(n_px * n_py * 4 * side_ref.shape[1])


def exchange(side_x, side_y, gram, n_px, n_py):
    shape = jax.ShapeDtypeStruct
    f32 = jnp.float32
    dma = pltpu.SemaphoreType.DMA
    return pl.pallas_call(
        exchange_kernel,
        out_shape=(shape(side_x.shape, f32), shape(side_y.shape, f32), shape((2, 2, 8, 8), f32)),
        in_specs=[VMEM] * 3,
        out_specs=(VMEM,) * 3,
        scratch_shapes=[
            pltpu.VMEM((n_px, 8, LANES), f32),
            pltpu.VMEM((8, LANES), f32),
            pltpu.VMEM((n_py, 8, LANES), f32),
            dma((2,)),
            dma((2,)),
            dma((n_px,)),
            dma((n_px,)),
            dma((n_py,)),
            dma((n_py,)),
        ],
        compiler_params=pltpu.CompilerParams(
            collective_id=0, has_side_effects=True, vmem_limit_bytes=16 * 2**20
        ),
        name="exchange",
    )(side_x, side_y, gram)


def prepare(wraps, dofs, pairing, stiff_mat, mass_mat):
    shape = jax.ShapeDtypeStruct
    wide = (GTILES * LANES, TILES * LANES)
    return pl.pallas_call(
        prepare_kernel,
        out_shape=(
            shape(dofs.shape, jnp.int32),
            shape(wide, jnp.bfloat16),
            shape(wide, jnp.bfloat16),
        ),
        in_specs=[SMEM, VMEM, VMEM, VMEM, VMEM],
        out_specs=(VMEM, VMEM, VMEM),
        compiler_params=pltpu.CompilerParams(vmem_limit_bytes=16 * 2**20),
        name="prepare",
    )(wraps, dofs, pairing, stiff_mat, mass_mat)


def part_images(count, phase, idx, own, high_x, high_y, stiff, mass, kh, kl):
    shape = jax.ShapeDtypeStruct
    owned, face = own.shape[1], high_x.shape[1]
    extent = owned + 2 * face
    f32 = jnp.float32
    return pl.pallas_call(
        part_kernel,
        out_shape=(
            shape((ROWS, owned), f32),
            shape((ROWS, owned), f32),
            shape((2 * ROWS, face), f32),
            shape((2 * ROWS, face), f32),
            shape((8, LANES), f32),
        ),
        in_specs=[SMEM, SMEM, SMEM] + [VMEM] * 8,
        out_specs=(VMEM,) * 5,
        scratch_shapes=[pltpu.VMEM((extent, LANES), f32)] * 5
        + [
            pltpu.VMEM((GTILES, BLOCK, LANES), f32),
            pltpu.VMEM((TILES, BLOCK, LANES), f32),
            pltpu.VMEM((GTILES * LANES, TILES * LANES), f32),
        ],
        compiler_params=pltpu.CompilerParams(vmem_limit_bytes=56 * 2**20),
        name="part_images",
    )(count, phase, idx.reshape(-1), idx, own, high_x, high_y, stiff, mass, kh, kl)


def on_device(
    trial_block,
    stiff_coef,
    mass_coef,
    elem_count,
    elem_dofs,
    pairing,
    bloch_fraction,
    stiff_mat,
    mass_mat,
):
    owned = trial_block.shape[-1]
    face = pairing.shape[0]
    interior = owned - 2 * face
    own = trial_block.reshape(ROWS, owned)
    n_px, n_py = lax.axis_size("px"), lax.axis_size("py")
    down_x = [((a + 1) % n_px, a) for a in range(n_px)]
    down_y = [(b + 1, b) for b in range(n_py - 1)]
    high_x = lax.ppermute(own[:, interior : interior + face], "px", down_x)
    high_y = lax.ppermute(own[:, interior + face :], "py", down_y)

    angle = 2.0 * math.pi * bloch_fraction[0].astype(jnp.float32) / bloch_fraction[1].astype(jnp.float32)
    at_end = lax.axis_index("px") == n_px - 1
    phase = jnp.stack([jnp.where(at_end, jnp.cos(angle), 1.0), jnp.where(at_end, jnp.sin(angle), 0.0)])
    wraps = at_end.astype(jnp.int32).reshape(1)
    idx, kh, kl = prepare(
        wraps, elem_dofs[0, 0].T.reshape(-1, LANES), pairing.reshape(-1, LANES), stiff_mat, mass_mat
    )
    curl, mass, side_x, side_y, gram = part_images(
        elem_count, phase, idx, own, high_x, high_y, stiff_coef[0], mass_coef[0], kh, kl
    )
    back_x, back_y, gram = exchange(side_x, side_y, gram, n_px, n_py)

    def finish(image, add_x, add_y):
        low_x = image[:, interior : interior + face] + add_x
        low_y = image[:, interior + face :] + add_y
        whole = jnp.concatenate([image[:, :interior], low_x, low_y], axis=1)
        return whole.reshape(trial_block.shape)

    curl = finish(curl, back_x[:ROWS], back_y[:ROWS])
    mass = finish(mass, back_x[ROWS:], back_y[ROWS:])
    return curl, mass, gram


def solution(mesh):
    return jax.shard_map(
        on_device,
        mesh=mesh,
        in_specs=(
            P("px", "py", None, None, None),
            P("px", "py", None),
            P("px", "py", None),
            P("px", "py"),
            P("px", "py", None, None),
            P(),
            P(),
            P(),
            P(),
        ),
        out_specs=(P("px", "py", None, None, None), P("px", "py", None, None, None), P()),
        check_vma=False,
    )
```

```python
import functools
import math

import jax
import jax.numpy as jnp
from jax import lax
from jax.experimental import pallas as pl
from jax.experimental.pallas import tpu as pltpu
from jax.sharding import PartitionSpec as P

HIGH = lax.Precision.HIGHEST
LANES = 128
ROWS = 16
NLOC = 20
HALO_SLOTS = 128
BLOCK = 256
TILES = 5
GTILES = 3
LANE_SETS = 4

VMEM = pl.BlockSpec(memory_space=pltpu.VMEM)
SMEM = pl.BlockSpec(memory_space=pltpu.SMEM)
ANY = pl.BlockSpec(memory_space=pl.ANY)
VMEM_BYTES = 56 * 2**20
OUT_CHUNKS = 2


def split_bf16(value):
    high = value.astype(jnp.bfloat16)
    low = (value - high.astype(jnp.float32)).astype(jnp.bfloat16)
    return high, low


def dot_split(a, b):
    (ah, al), (bh, bl) = a, b
    dot = functools.partial(jnp.dot, preferred_element_type=jnp.float32)
    both = dot(jnp.concatenate([ah, al], axis=0), bh)
    rows = ah.shape[0]
    return both[:rows] + (both[rows:] + dot(ah, bl))


def begin_kernel(
    fraction_ref,
    own_hbm,
    dofs_ref,
    pairing_ref,
    stiff_ref,
    mass_ref,
    high_x,
    high_y,
    phase_out,
    idx_out,
    kh_out,
    kl_out,
    zeros,
    sems,
):
    face = pairing_ref.shape[0] * LANES
    owned = own_hbm.shape[1]
    n_px, n_py = lax.axis_size("px"), lax.axis_size("py")
    a, b = lax.axis_index("px"), lax.axis_index("py")
    below_x, above_x = lax.rem(a + n_px - 1, n_px), lax.rem(a + 1, n_px)
    below_y, above_y = lax.rem(b + n_py - 1, n_py), lax.rem(b + 1, n_py)

    barrier = pltpu.get_barrier_semaphore()

    def greet(axis, to):
        pl.semaphore_signal(barrier, 1, device_id={axis: to}, device_id_type=pl.DeviceIdType.MESH)

    greet("px", below_x)
    greet("px", above_x)

    @pl.when(b > 0)
    def _():
        greet("py", below_y)

    @pl.when(b < n_py - 1)
    def _():
        greet("py", above_y)

    pl.semaphore_wait(barrier, 2 + jnp.minimum(b, 1) + jnp.minimum(n_py - 1 - b, 1))

    def face_copy(first, target, at, axis, to):
        return pltpu.make_async_remote_copy(
            src_ref=own_hbm.at[:, pl.ds(first, face)],
            dst_ref=target,
            send_sem=sems.at[2 * at],
            recv_sem=sems.at[2 * at + 1],
            device_id={axis: to},
            device_id_type=pl.DeviceIdType.MESH,
        )

    to_x = face_copy(owned - 2 * face, high_x, 0, "px", below_x)
    to_y = face_copy(owned - face, high_y, 1, "py", below_y)
    no_y = pltpu.make_async_copy(zeros, high_y, sems.at[4])
    to_x.start()

    @pl.when(b > 0)
    def _():
        to_y.start()

    @pl.when(b == n_py - 1)
    def _():
        zeros[...] = jnp.zeros_like(zeros)
        no_y.start()

    at_end = jnp.broadcast_to(a, (1, LANES)) == n_px - 1
    above = jnp.broadcast_to(fraction_ref[0], (1, LANES)).astype(jnp.float32)
    below = jnp.broadcast_to(fraction_ref[1], (1, LANES)).astype(jnp.float32)
    angle = 2.0 * math.pi * above / below
    phase_out[0:1, :] = jnp.where(at_end, jnp.cos(angle), 1.0)
    phase_out[1:2, :] = jnp.where(at_end, jnp.sin(angle), 0.0)

    blocks = dofs_ref.shape[0] // NLOC
    idx_out[...] = dofs_ref[...]
    heads = pl.ds(0, NLOC, stride=blocks)
    head = dofs_ref[heads, :]
    spot = head - owned
    local = spot & (LANES - 1)
    found = jnp.zeros_like(head)
    for row in range(pairing_ref.shape[0]):
        values = jnp.broadcast_to(pairing_ref[row : row + 1, :], head.shape)
        here = jnp.take_along_axis(values, local, axis=1)
        found = jnp.where((spot >> 7) == row, here + owned, found)
    wraps = (spot >= 0) & (spot < face) & (jnp.broadcast_to(a, head.shape) == n_px - 1)
    idx_out[heads, :] = jnp.where(wraps, found, head)

    grow = lax.broadcasted_iota(jnp.int32, (GTILES * LANES, NLOC), 0)
    gcol = lax.broadcasted_iota(jnp.int32, (GTILES * LANES, NLOC), 1)
    spread_i = ((grow >> 4) == gcol).astype(jnp.float32)
    trow = lax.broadcasted_iota(jnp.int32, (NLOC, TILES * LANES), 0)
    tcol = lax.broadcasted_iota(jnp.int32, (NLOC, TILES * LANES), 1)
    spread_j = ((tcol >> 5) == trow).astype(jnp.float32)
    dot = functools.partial(jnp.dot, precision=HIGH, preferred_element_type=jnp.float32)
    stiff = dot(dot(spread_i, stiff_ref[...].T), spread_j)
    mass = dot(dot(spread_i, mass_ref[...].T), spread_j)
    krow = lax.broadcasted_iota(jnp.int32, (GTILES * LANES, TILES * LANES), 0)
    kcol = lax.broadcasted_iota(jnp.int32, (GTILES * LANES, TILES * LANES), 1)
    both = jnp.where(((kcol >> 4) & 1) == 0, stiff, mass)
    both = jnp.where((krow & 15) == (kcol & 15), both, 0.0)
    kh_out[...], kl_out[...] = split_bf16(both)

    to_x.wait()

    @pl.when(b > 0)
    def _():
        to_y.wait_send()

    @pl.when(b < n_py - 1)
    def _():
        to_y.wait_recv()

    @pl.when(b == n_py - 1)
    def _():
        no_y.wait()


def begin(fraction, own, dofs, pairing, stiff_mat, mass_mat):
    shape = jax.ShapeDtypeStruct
    high = shape((ROWS, pairing.size), jnp.float32)
    spread = shape((GTILES * LANES, TILES * LANES), jnp.bfloat16)
    return pl.pallas_call(
        begin_kernel,
        out_shape=(high, high, shape((2, LANES), jnp.float32), shape(dofs.shape, jnp.int32), spread, spread),
        in_specs=[SMEM, ANY, VMEM, VMEM, VMEM, VMEM],
        out_specs=(ANY, ANY, VMEM, VMEM, VMEM, VMEM),
        scratch_shapes=[
            pltpu.VMEM(high.shape, jnp.float32),
            pltpu.SemaphoreType.DMA((5,)),
        ],
        compiler_params=pltpu.CompilerParams(
            collective_id=1, has_side_effects=True, vmem_limit_bytes=VMEM_BYTES
        ),
        name="begin",
    )(fraction, own, dofs, pairing, stiff_mat, mass_mat)


def part_kernel(
    count_ref,
    idx_hbm,
    own_hbm,
    high_x_hbm,
    high_y_hbm,
    phase_ref,
    idx_v,
    stiff_ref,
    mass_ref,
    kh_ref,
    kl_ref,
    curl_out,
    mass_out,
    side_x_out,
    side_y_out,
    gram_out,
    ext,
    acc0,
    acc1,
    acc2,
    acc3,
    gathered,
    terms,
    gram,
    idx_all,
    own_v,
    high_v,
    images,
    in_sems,
    out_sems,
):
    accs = (acc0, acc1, acc2, acc3)
    owned = own_v.shape[1]
    face = high_v.shape[2]
    cosine, sine = phase_ref[0:1, :], phase_ref[1:2, :]
    count = count_ref[0, 0]
    capacity = stiff_ref.shape[1]
    idx_s = [idx_all.at[pl.ds(j * capacity, capacity)] for j in range(NLOC)]

    own_in = pltpu.make_async_copy(own_hbm, own_v, in_sems.at[0])
    high_x_in = pltpu.make_async_copy(high_x_hbm, high_v.at[0], in_sems.at[1])
    high_y_in = pltpu.make_async_copy(high_y_hbm, high_v.at[1], in_sems.at[2])
    idx_in = pltpu.make_async_copy(idx_hbm, idx_all, in_sems.at[3])
    own_in.start()
    idx_in.start()
    high_x_in.start()
    high_y_in.start()

    zero_rows = jnp.zeros((LANES, LANES), jnp.float32)

    @pl.loop(0, ext.shape[0] // LANES)
    def _(b):
        at = pl.multiple_of(b * LANES, LANES)
        for acc in accs:
            acc[pl.ds(at, LANES), :] = zero_rows

    gram[...] = jnp.zeros_like(gram)

    def put_rows(at, block):
        ext[pl.ds(at, LANES), :] = jnp.concatenate([block] * (LANES // ROWS), axis=0).T

    own_in.wait()

    @pl.loop(0, owned // LANES, unroll=8)
    def _(b):
        at = pl.multiple_of(b * LANES, LANES)
        put_rows(at, own_v[:, pl.ds(at, LANES)])

    high_x_in.wait()
    high_y_in.wait()

    @pl.loop(0, face // LANES, unroll=4)
    def _(b):
        at = pl.multiple_of(b * LANES, LANES)
        got = high_v[0, :, pl.ds(at, LANES)]
        real, imag = got[: ROWS // 2], got[ROWS // 2 :]
        turned = jnp.concatenate([cosine * real - sine * imag, sine * real + cosine * imag], axis=0)
        high_v[0, :, pl.ds(at, LANES)] = turned
        put_rows(owned + at, turned)
        put_rows(owned + face + at, high_v[1, :, pl.ds(at, LANES)])

    def idx_row(j, block_id, part):
        row = j * (capacity // LANES) + block_id * (BLOCK // LANES) + part
        return jnp.broadcast_to(idx_v[pl.ds(row, 1), :], (LANES // LANE_SETS, LANES))

    lane_set = lax.broadcasted_iota(jnp.int32, (1, LANES), 1) >> 4
    idx_in.wait()

    @pl.loop(0, (count + BLOCK - 1) // BLOCK)
    def _(block_id):
        first = pl.multiple_of(block_id * BLOCK, BLOCK)

        @pl.loop(0, BLOCK, unroll=4)
        def _(e):
            slot = first + e
            for tile in range(GTILES):
                inside = range(8 * tile, min(8 * tile + 8, NLOC))
                row = None
                for i in inside:
                    got = ext[pl.ds(idx_s[i][slot], 1), :]
                    row = got if row is None else jnp.where(lane_set == i % 8, got, row)
                gathered[tile, pl.ds(e, 1), :] = row

        values = jnp.concatenate([gathered[tile] for tile in range(GTILES)], axis=1)
        products = dot_split(split_bf16(values), (kh_ref[...], kl_ref[...]))
        slots = first + lax.broadcasted_iota(jnp.int32, (1, BLOCK), 1)
        live = slots < count
        stiff = jnp.where(live, stiff_ref[:, pl.ds(first, BLOCK)], 0.0)
        mass = jnp.where(live, mass_ref[:, pl.ds(first, BLOCK)], 0.0)
        pair = [jnp.broadcast_to(stiff, (ROWS, BLOCK)), jnp.broadcast_to(mass, (ROWS, BLOCK))]
        coef = jnp.concatenate(pair * LANE_SETS, axis=0).T
        scaled = [products[:, t * LANES : (t + 1) * LANES] * coef for t in range(TILES)]

        names = []
        for t in range(TILES):
            rows = [
                jnp.concatenate([idx_row(j, block_id, part) for part in range(BLOCK // LANES)], axis=1)
                for j in range(LANE_SETS * t, LANE_SETS * t + LANE_SETS)
            ]
            names.append(jnp.concatenate(rows, axis=0).astype(jnp.float32).T)
        for t in range(TILES):
            total = scaled[t]
            for s in range(t):
                total = total + jnp.where(names[s] == names[t], scaled[s], 0.0)
            terms[t] = total

        @pl.loop(0, BLOCK, unroll=4)
        def _(e):
            slot = first + e
            added = [terms[t, pl.ds(e, 1), :] for t in range(TILES)]
            places = [[idx_s[LANE_SETS * t + g][slot] for t in range(TILES)] for g in range(LANE_SETS)]
            held = [[accs[g][pl.ds(places[g][t], 1), :] for t in range(TILES)] for g in range(LANE_SETS)]
            for t in range(TILES):
                for g in range(LANE_SETS):
                    accs[g][pl.ds(places[g][t], 1), :] = held[g][t] + added[t]

    quarter = lax.broadcasted_iota(jnp.int32, (LANES, LANES), 1) >> 5

    def summed(at):
        rows = accs[0][pl.ds(at, LANES), :]
        for g in range(1, LANE_SETS):
            rows = jnp.where(quarter == g, accs[g][pl.ds(at, LANES), :], rows)
        rows = rows.T
        return (rows[:32] + rows[32:64]) + (rows[64:96] + rows[96:])

    def wide(at):
        return jnp.concatenate([summed(at), summed(at + LANES)], axis=1)

    across = (((1,), (1,)), ((), ()))
    dot = functools.partial(lax.dot_general, dimension_numbers=across, preferred_element_type=jnp.float32)

    def add_gram(left, both):
        (lh, ll), (bh, bl) = split_bf16(left), split_bf16(both)
        pieces = dot(jnp.concatenate([lh, ll], axis=0), bh)
        gram[:, : 2 * ROWS] += pieces[:ROWS] + (pieces[ROWS:] + dot(lh, bl))

    step = 2 * LANES

    @pl.loop(0, face // step, unroll=2)
    def _(b):
        at = pl.multiple_of(b * step, step)
        both = wide(owned + at)
        add_gram(high_v[0, :, pl.ds(at, step)], both)
        cos2, sin2 = (jnp.concatenate([row, row], axis=1) for row in (cosine, sine))
        for op in range(2):
            real, imag = both[ROWS * op : ROWS * op + 8], both[ROWS * op + 8 : ROWS * op + ROWS]
            side_x_out[ROWS * op : ROWS * op + 8, pl.ds(at, step)] = cos2 * real + sin2 * imag
            side_x_out[ROWS * op + 8 : ROWS * op + ROWS, pl.ds(at, step)] = cos2 * imag - sin2 * real
        both = wide(owned + face + at)
        add_gram(high_v[1, :, pl.ds(at, step)], both)
        side_y_out[:, pl.ds(at, step)] = both

    chunk = owned // OUT_CHUNKS

    def out_copies(c):
        cols = pl.ds(c * chunk, chunk)
        return (
            pltpu.make_async_copy(images.at[pl.ds(0, ROWS), cols], curl_out.at[:, cols], out_sems.at[0, c]),
            pltpu.make_async_copy(images.at[pl.ds(ROWS, ROWS), cols], mass_out.at[:, cols], out_sems.at[1, c]),
        )

    for c in range(OUT_CHUNKS):

        @pl.loop(0, chunk // step, unroll=4)
        def _(b):
            at = pl.multiple_of(c * chunk + b * step, step)
            both = wide(at)
            add_gram(own_v[:, pl.ds(at, step)], both)
            images[:, pl.ds(at, step)] = both

        for copy in out_copies(c):
            copy.start()

    total = gram[...]
    of_real, of_imag = total[:8], total[8:]
    odd = ((lax.broadcasted_iota(jnp.int32, (8, LANES), 1) >> 3) & 1) == 1
    gram_out[...] = jnp.where(
        odd, of_real - pltpu.roll(of_imag, 8, 1), of_real + pltpu.roll(of_imag, LANES - 8, 1)
    )
    for c in range(OUT_CHUNKS):
        for copy in out_copies(c):
            copy.wait()


def part_images(count, phase, idx, own, high_x, high_y, stiff, mass, kh, kl):
    shape = jax.ShapeDtypeStruct
    owned, face = own.shape[1], high_x.shape[1]
    extent = owned + 2 * face
    f32 = jnp.float32
    dma = pltpu.SemaphoreType.DMA
    return pl.pallas_call(
        part_kernel,
        out_shape=(
            shape((ROWS, owned), f32),
            shape((ROWS, owned), f32),
            shape((2 * ROWS, face), f32),
            shape((2 * ROWS, face), f32),
            shape((8, LANES), f32),
        ),
        in_specs=[SMEM, ANY, ANY, ANY, ANY] + [VMEM] * 6,
        out_specs=(ANY, ANY, VMEM, VMEM, VMEM),
        scratch_shapes=[pltpu.VMEM((extent, LANES), f32)] * 5
        + [
            pltpu.VMEM((GTILES, BLOCK, LANES), f32),
            pltpu.VMEM((TILES, BLOCK, LANES), f32),
            pltpu.VMEM((ROWS, LANES), f32),
            pltpu.SMEM((idx.size,), jnp.int32),
            pltpu.VMEM((ROWS, owned), f32),
            pltpu.VMEM((2, ROWS, face), f32),
            pltpu.VMEM((2 * ROWS, owned), f32),
            dma((4,)),
            dma((2, OUT_CHUNKS)),
        ],
        compiler_params=pltpu.CompilerParams(vmem_limit_bytes=VMEM_BYTES),
        name="part_images",
    )(count, idx.reshape(-1), own, high_x, high_y, phase, idx, stiff, mass, kh, kl)


def exchange_kernel(
    side_x_ref,
    side_y_ref,
    gram_ref,
    back_x,
    back_y,
    gram_out,
    along_x,
    row_sum,
    along_y,
    side_send,
    side_recv,
    send_x,
    recv_x,
    send_y,
    recv_y,
):
    n_px, n_py = along_x.shape[0], along_y.shape[0]
    a, b = lax.axis_index("px"), lax.axis_index("py")

    barrier = pltpu.get_barrier_semaphore()

    def greet(axis, me, n):
        @pl.loop(1, n)
        def _(k):
            other = lax.rem(me + k, n)
            pl.semaphore_signal(barrier, 1, device_id={axis: other}, device_id_type=pl.DeviceIdType.MESH)

    greet("px", a, n_px)
    greet("py", b, n_py)
    pl.semaphore_wait(barrier, n_px + n_py - 2)

    def tile_copy(axis, to, source, held, at, send, recv):
        return pltpu.make_async_remote_copy(
            src_ref=source,
            dst_ref=held.at[at],
            send_sem=send.at[to],
            recv_sem=recv.at[at],
            device_id={axis: to},
            device_id_type=pl.DeviceIdType.MESH,
        )

    def send_all(axis, me, n, source, held, send, recv):
        @pl.loop(1, n)
        def _(k):
            tile_copy(axis, lax.rem(me + k, n), source, held, me, send, recv).start()

    def sum_all(axis, me, n, source, held, send, recv):
        held[pl.ds(me, 1)] = source[...][None]

        @pl.loop(1, n)
        def _(k):
            other = lax.rem(me + k, n)
            tile_copy(axis, other, source, held, other, send, recv).wait_recv()

        total = held[0]
        for at in range(1, n):
            total = total + held[at]
        return total

    def sent_all(axis, me, n, source, held, send, recv):
        @pl.loop(1, n)
        def _(k):
            tile_copy(axis, lax.rem(me + k, n), source, held, me, send, recv).wait_send()

    def side_copy(source, held, at, axis, to):
        return pltpu.make_async_remote_copy(
            src_ref=source,
            dst_ref=held,
            send_sem=side_send.at[at],
            recv_sem=side_recv.at[at],
            device_id={axis: to},
            device_id_type=pl.DeviceIdType.MESH,
        )

    over_x = ("px", a, n_px, gram_ref, along_x, send_x, recv_x)
    over_y = ("py", b, n_py, row_sum, along_y, send_y, recv_y)
    to_x = side_copy(side_x_ref, back_x, 0, "px", lax.rem(a + 1, n_px))
    to_y = side_copy(side_y_ref, back_y, 1, "py", lax.rem(b + 1, n_py))
    send_all(*over_x)
    to_x.start()

    @pl.when(b < n_py - 1)
    def _():
        to_y.start()

    row_sum[...] = sum_all(*over_x)
    send_all(*over_y)
    whole = sum_all(*over_y)
    for op in range(2):
        for part in range(2):
            at = 16 * op + 8 * part
            gram_out[op, part] = whole[:, at : at + 8] / gram_scale(n_px, n_py, side_x_ref)
    to_x.wait_recv()

    @pl.when(b > 0)
    def _():
        to_y.wait_recv()

    @pl.when(b == 0)
    def _():
        back_y[...] = jnp.zeros_like(back_y)

    to_x.wait_send()

    @pl.when(b < n_py - 1)
    def _():
        to_y.wait_send()

    sent_all(*over_x)
    sent_all(*over_y)


def gram_scale(n_px, n_py, side_ref):
    return float(n_px * n_py * 4 * side_ref.shape[1])


def exchange(side_x, side_y, gram, n_px, n_py):
    shape = jax.ShapeDtypeStruct
    f32 = jnp.float32
    dma = pltpu.SemaphoreType.DMA
    return pl.pallas_call(
        exchange_kernel,
        out_shape=(shape(side_x.shape, f32), shape(side_y.shape, f32), shape((2, 2, 8, 8), f32)),
        in_specs=[VMEM] * 3,
        out_specs=(VMEM,) * 3,
        scratch_shapes=[
            pltpu.VMEM((n_px, 8, LANES), f32),
            pltpu.VMEM((8, LANES), f32),
            pltpu.VMEM((n_py, 8, LANES), f32),
            dma((2,)),
            dma((2,)),
            dma((n_px,)),
            dma((n_px,)),
            dma((n_py,)),
            dma((n_py,)),
        ],
        compiler_params=pltpu.CompilerParams(
            collective_id=0, has_side_effects=True, vmem_limit_bytes=VMEM_BYTES
        ),
        name="exchange",
    )(side_x, side_y, gram)


def finish_kernel(curl_in, mass_in, back_x, back_y, gram_ref, curl_out, mass_out, gram_out, low, sems):
    face = back_x.shape[1]
    lows = pl.ds(curl_out.shape[1] - 2 * face, 2 * face)
    images = (curl_out, mass_out)
    reads = [pltpu.make_async_copy(images[op].at[:, lows], low.at[op], sems.at[op]) for op in range(2)]
    writes = [pltpu.make_async_copy(low.at[op], images[op].at[:, lows], sems.at[2 + op]) for op in range(2)]
    for read in reads:
        read.start()
    gram_out[...] = gram_ref[...]
    for op in range(2):
        reads[op].wait()
        low[op, :, :face] += back_x[ROWS * op : ROWS * op + ROWS, :]
        low[op, :, face:] += back_y[ROWS * op : ROWS * op + ROWS, :]
        writes[op].start()
    for write in writes:
        write.wait()


def finish(curl, mass, back_x, back_y, gram):
    shape = jax.ShapeDtypeStruct
    return pl.pallas_call(
        finish_kernel,
        out_shape=tuple(shape(value.shape, jnp.float32) for value in (curl, mass, gram)),
        in_specs=[ANY, ANY, VMEM, VMEM, VMEM],
        out_specs=(ANY, ANY, VMEM),
        scratch_shapes=[
            pltpu.VMEM((2, ROWS, 2 * back_x.shape[1]), jnp.float32),
            pltpu.SemaphoreType.DMA((4,)),
        ],
        input_output_aliases={0: 0, 1: 1},
        compiler_params=pltpu.CompilerParams(vmem_limit_bytes=VMEM_BYTES),
        name="finish",
    )(curl, mass, back_x, back_y, gram)


def on_device(
    trial_block,
    stiff_coef,
    mass_coef,
    elem_count,
    elem_dofs,
    pairing,
    bloch_fraction,
    stiff_mat,
    mass_mat,
):
    owned = trial_block.shape[-1]
    own = trial_block.reshape(ROWS, owned)
    n_px, n_py = lax.axis_size("px"), lax.axis_size("py")
    high_x, high_y, phase, idx, kh, kl = begin(
        bloch_fraction,
        own,
        elem_dofs[0, 0].T.reshape(-1, LANES),
        pairing.reshape(-1, LANES),
        stiff_mat,
        mass_mat,
    )
    curl, mass, side_x, side_y, gram = part_images(
        elem_count, phase, idx, own, high_x, high_y, stiff_coef[0], mass_coef[0], kh, kl
    )
    back_x, back_y, gram = exchange(side_x, side_y, gram, n_px, n_py)
    curl, mass, gram = finish(curl, mass, back_x, back_y, gram)
    return curl.reshape(trial_block.shape), mass.reshape(trial_block.shape), gram


def solution(mesh):
    return jax.shard_map(
        on_device,
        mesh=mesh,
        in_specs=(
            P("px", "py", None, None, None),
            P("px", "py", None),
            P("px", "py", None),
            P("px", "py"),
            P("px", "py", None, None),
            P(),
            P(),
            P(),
            P(),
        ),
        out_specs=(P("px", "py", None, None, None), P("px", "py", None, None, None), P()),
        check_vma=False,
    )
```

```python
import functools
import math

import jax
import jax.numpy as jnp
from jax import lax
from jax.experimental import pallas as pl
from jax.experimental.pallas import tpu as pltpu
from jax.sharding import PartitionSpec as P

HIGH = lax.Precision.HIGHEST
LANES = 128
ROWS = 16
NLOC = 20
HALO_SLOTS = 128
BLOCK = 256
TILES = 5
GTILES = 3
LANE_SETS = 4

VMEM = pl.BlockSpec(memory_space=pltpu.VMEM)
SMEM = pl.BlockSpec(memory_space=pltpu.SMEM)
ANY = pl.BlockSpec(memory_space=pl.ANY)
VMEM_BYTES = 56 * 2**20
OUT_CHUNKS = 2
GROUP = 8


def split_bf16(value):
    high = value.astype(jnp.bfloat16)
    low = (value - high.astype(jnp.float32)).astype(jnp.bfloat16)
    return high, low


def dot_split(a, b):
    (ah, al), (bh, bl) = a, b
    dot = functools.partial(jnp.dot, preferred_element_type=jnp.float32)
    both = dot(jnp.concatenate([ah, al], axis=0), bh)
    rows = ah.shape[0]
    return both[:rows] + (both[rows:] + dot(ah, bl))


def begin_kernel(
    fraction_ref,
    own_hbm,
    dofs_ref,
    pairing_ref,
    stiff_ref,
    mass_ref,
    high_x,
    high_y,
    phase_out,
    idx_out,
    kh_out,
    kl_out,
    zeros,
    sems,
):
    face = pairing_ref.shape[0] * LANES
    owned = own_hbm.shape[1]
    n_px, n_py = lax.axis_size("px"), lax.axis_size("py")
    a, b = lax.axis_index("px"), lax.axis_index("py")
    below_x, above_x = lax.rem(a + n_px - 1, n_px), lax.rem(a + 1, n_px)
    below_y, above_y = lax.rem(b + n_py - 1, n_py), lax.rem(b + 1, n_py)

    barrier = pltpu.get_barrier_semaphore()

    def greet(axis, to):
        pl.semaphore_signal(barrier, 1, device_id={axis: to}, device_id_type=pl.DeviceIdType.MESH)

    greet("px", below_x)
    greet("px", above_x)

    @pl.when(b > 0)
    def _():
        greet("py", below_y)

    @pl.when(b < n_py - 1)
    def _():
        greet("py", above_y)

    pl.semaphore_wait(barrier, 2 + jnp.minimum(b, 1) + jnp.minimum(n_py - 1 - b, 1))

    def face_copy(first, target, at, axis, to):
        return pltpu.make_async_remote_copy(
            src_ref=own_hbm.at[:, pl.ds(first, face)],
            dst_ref=target,
            send_sem=sems.at[2 * at],
            recv_sem=sems.at[2 * at + 1],
            device_id={axis: to},
            device_id_type=pl.DeviceIdType.MESH,
        )

    to_x = face_copy(owned - 2 * face, high_x, 0, "px", below_x)
    to_y = face_copy(owned - face, high_y, 1, "py", below_y)
    no_y = pltpu.make_async_copy(zeros, high_y, sems.at[4])
    to_x.start()

    @pl.when(b > 0)
    def _():
        to_y.start()

    @pl.when(b == n_py - 1)
    def _():
        zeros[...] = jnp.zeros_like(zeros)
        no_y.start()

    at_end = jnp.broadcast_to(a, (1, LANES)) == n_px - 1
    above = jnp.broadcast_to(fraction_ref[0], (1, LANES)).astype(jnp.float32)
    below = jnp.broadcast_to(fraction_ref[1], (1, LANES)).astype(jnp.float32)
    angle = 2.0 * math.pi * above / below
    phase_out[0:1, :] = jnp.where(at_end, jnp.cos(angle), 1.0)
    phase_out[1:2, :] = jnp.where(at_end, jnp.sin(angle), 0.0)

    blocks = dofs_ref.shape[0] // NLOC
    idx_out[...] = dofs_ref[...]
    heads = pl.ds(0, NLOC, stride=blocks)
    head = dofs_ref[heads, :]
    spot = head - owned
    local = spot & (LANES - 1)
    found = jnp.zeros_like(head)
    for row in range(pairing_ref.shape[0]):
        values = jnp.broadcast_to(pairing_ref[row : row + 1, :], head.shape)
        here = jnp.take_along_axis(values, local, axis=1)
        found = jnp.where((spot >> 7) == row, here + owned, found)
    wraps = (spot >= 0) & (spot < face) & (jnp.broadcast_to(a, head.shape) == n_px - 1)
    idx_out[heads, :] = jnp.where(wraps, found, head)

    grow = lax.broadcasted_iota(jnp.int32, (GTILES * LANES, NLOC), 0)
    gcol = lax.broadcasted_iota(jnp.int32, (GTILES * LANES, NLOC), 1)
    spread_i = ((grow >> 4) == gcol).astype(jnp.float32)
    trow = lax.broadcasted_iota(jnp.int32, (NLOC, TILES * LANES), 0)
    tcol = lax.broadcasted_iota(jnp.int32, (NLOC, TILES * LANES), 1)
    spread_j = ((tcol >> 5) == trow).astype(jnp.float32)
    dot = functools.partial(jnp.dot, precision=HIGH, preferred_element_type=jnp.float32)
    stiff = dot(dot(spread_i, stiff_ref[...].T), spread_j)
    mass = dot(dot(spread_i, mass_ref[...].T), spread_j)
    krow = lax.broadcasted_iota(jnp.int32, (GTILES * LANES, TILES * LANES), 0)
    kcol = lax.broadcasted_iota(jnp.int32, (GTILES * LANES, TILES * LANES), 1)
    both = jnp.where(((kcol >> 4) & 1) == 0, stiff, mass)
    both = jnp.where((krow & 15) == (kcol & 15), both, 0.0)
    kh_out[...], kl_out[...] = split_bf16(both)

    to_x.wait()

    @pl.when(b > 0)
    def _():
        to_y.wait_send()

    @pl.when(b < n_py - 1)
    def _():
        to_y.wait_recv()

    @pl.when(b == n_py - 1)
    def _():
        no_y.wait()


def begin(fraction, own, dofs, pairing, stiff_mat, mass_mat):
    shape = jax.ShapeDtypeStruct
    high = shape((ROWS, pairing.size), jnp.float32)
    spread = shape((GTILES * LANES, TILES * LANES), jnp.bfloat16)
    return pl.pallas_call(
        begin_kernel,
        out_shape=(high, high, shape((2, LANES), jnp.float32), shape(dofs.shape, jnp.int32), spread, spread),
        in_specs=[SMEM, ANY, VMEM, VMEM, VMEM, VMEM],
        out_specs=(ANY, ANY, VMEM, VMEM, VMEM, VMEM),
        scratch_shapes=[
            pltpu.VMEM(high.shape, jnp.float32),
            pltpu.SemaphoreType.DMA((5,)),
        ],
        compiler_params=pltpu.CompilerParams(
            collective_id=1, has_side_effects=True, vmem_limit_bytes=VMEM_BYTES
        ),
        name="begin",
    )(fraction, own, dofs, pairing, stiff_mat, mass_mat)


def part_kernel(
    count_ref,
    idx_hbm,
    own_hbm,
    high_x_hbm,
    high_y_hbm,
    phase_ref,
    idx_v,
    stiff_ref,
    mass_ref,
    kh_ref,
    kl_ref,
    curl_out,
    mass_out,
    side_x_out,
    side_y_out,
    gram_out,
    ext,
    acc0,
    acc1,
    acc2,
    acc3,
    gathered,
    terms,
    gram,
    idx_all,
    own_v,
    high_v,
    images,
    in_sems,
    out_sems,
):
    accs = (acc0, acc1, acc2, acc3)
    owned = own_v.shape[1]
    face = high_v.shape[2]
    cosine, sine = phase_ref[0:1, :], phase_ref[1:2, :]
    count = count_ref[0, 0]
    capacity = stiff_ref.shape[1]
    idx_s = [idx_all.at[pl.ds(j * capacity, capacity)] for j in range(NLOC)]

    own_in = pltpu.make_async_copy(own_hbm, own_v, in_sems.at[0])
    high_x_in = pltpu.make_async_copy(high_x_hbm, high_v.at[0], in_sems.at[1])
    high_y_in = pltpu.make_async_copy(high_y_hbm, high_v.at[1], in_sems.at[2])
    idx_in = pltpu.make_async_copy(idx_hbm, idx_all, in_sems.at[3])
    own_in.start()
    idx_in.start()
    high_x_in.start()
    high_y_in.start()

    zero_rows = jnp.zeros((LANES, LANES), jnp.float32)

    @pl.loop(0, ext.shape[0] // LANES)
    def _(b):
        at = pl.multiple_of(b * LANES, LANES)
        for acc in accs:
            acc[pl.ds(at, LANES), :] = zero_rows

    gram[...] = jnp.zeros_like(gram)

    def put_rows(at, block):
        ext[pl.ds(at, LANES), :] = jnp.concatenate([block] * (LANES // ROWS), axis=0).T

    own_in.wait()

    @pl.loop(0, owned // LANES, unroll=8)
    def _(b):
        at = pl.multiple_of(b * LANES, LANES)
        put_rows(at, own_v[:, pl.ds(at, LANES)])

    high_x_in.wait()
    high_y_in.wait()

    @pl.loop(0, face // LANES, unroll=4)
    def _(b):
        at = pl.multiple_of(b * LANES, LANES)
        got = high_v[0, :, pl.ds(at, LANES)]
        real, imag = got[: ROWS // 2], got[ROWS // 2 :]
        turned = jnp.concatenate([cosine * real - sine * imag, sine * real + cosine * imag], axis=0)
        high_v[0, :, pl.ds(at, LANES)] = turned
        put_rows(owned + at, turned)
        put_rows(owned + face + at, high_v[1, :, pl.ds(at, LANES)])

    def idx_row(j, block_id, part):
        row = j * (capacity // LANES) + block_id * (BLOCK // LANES) + part
        return jnp.broadcast_to(idx_v[pl.ds(row, 1), :], (LANES // LANE_SETS, LANES))

    lane_set = lax.broadcasted_iota(jnp.int32, (1, LANES), 1) >> 4
    idx_in.wait()

    @pl.loop(0, (count + BLOCK - 1) // BLOCK)
    def _(block_id):
        first = pl.multiple_of(block_id * BLOCK, BLOCK)

        @pl.loop(0, BLOCK, unroll=4)
        def _(e):
            slot = first + e
            for tile in range(GTILES):
                inside = range(8 * tile, min(8 * tile + 8, NLOC))
                row = None
                for i in inside:
                    got = ext[pl.ds(idx_s[i][slot], 1), :]
                    row = got if row is None else jnp.where(lane_set == i % 8, got, row)
                gathered[tile, pl.ds(e, 1), :] = row

        values = jnp.concatenate([gathered[tile] for tile in range(GTILES)], axis=1)
        products = dot_split(split_bf16(values), (kh_ref[...], kl_ref[...]))
        slots = first + lax.broadcasted_iota(jnp.int32, (1, BLOCK), 1)
        live = slots < count
        stiff = jnp.where(live, stiff_ref[:, pl.ds(first, BLOCK)], 0.0)
        mass = jnp.where(live, mass_ref[:, pl.ds(first, BLOCK)], 0.0)
        pair = [jnp.broadcast_to(stiff, (ROWS, BLOCK)), jnp.broadcast_to(mass, (ROWS, BLOCK))]
        coef = jnp.concatenate(pair * LANE_SETS, axis=0).T
        scaled = [products[:, t * LANES : (t + 1) * LANES] * coef for t in range(TILES)]

        names = []
        for t in range(TILES):
            rows = [
                jnp.concatenate([idx_row(j, block_id, part) for part in range(BLOCK // LANES)], axis=1)
                for j in range(LANE_SETS * t, LANE_SETS * t + LANE_SETS)
            ]
            names.append(jnp.concatenate(rows, axis=0).astype(jnp.float32).T)
        for t in range(TILES):
            total = scaled[t]
            for s in range(t):
                total = total + jnp.where(names[s] == names[t], scaled[s], 0.0)
            terms[t] = total

        @pl.loop(0, BLOCK, unroll=4)
        def _(e):
            slot = first + e
            added = [terms[t, pl.ds(e, 1), :] for t in range(TILES)]
            places = [[idx_s[LANE_SETS * t + g][slot] for t in range(TILES)] for g in range(LANE_SETS)]
            held = [[accs[g][pl.ds(places[g][t], 1), :] for t in range(TILES)] for g in range(LANE_SETS)]
            for t in range(TILES):
                for g in range(LANE_SETS):
                    accs[g][pl.ds(places[g][t], 1), :] = held[g][t] + added[t]

    quarter = lax.broadcasted_iota(jnp.int32, (LANES, LANES), 1) >> 5

    def summed(at):
        rows = accs[0][pl.ds(at, LANES), :]
        for g in range(1, LANE_SETS):
            rows = jnp.where(quarter == g, accs[g][pl.ds(at, LANES), :], rows)
        rows = rows.T
        return (rows[:32] + rows[32:64]) + (rows[64:96] + rows[96:])

    def wide(at):
        return jnp.concatenate([summed(at), summed(at + LANES)], axis=1)

    across = (((1,), (1,)), ((), ()))
    dot = functools.partial(lax.dot_general, dimension_numbers=across, preferred_element_type=jnp.float32)

    def add_gram(left, both):
        (lh, ll), (bh, bl) = split_bf16(left), split_bf16(both)
        pieces = dot(jnp.concatenate([lh, ll], axis=0), bh)
        gram[:, : 2 * ROWS] += pieces[:ROWS] + (pieces[ROWS:] + dot(lh, bl))

    step = 2 * LANES

    @pl.loop(0, face // step, unroll=2)
    def _(b):
        at = pl.multiple_of(b * step, step)
        both = wide(owned + at)
        add_gram(high_v[0, :, pl.ds(at, step)], both)
        cos2, sin2 = (jnp.concatenate([row, row], axis=1) for row in (cosine, sine))
        for op in range(2):
            real, imag = both[ROWS * op : ROWS * op + 8], both[ROWS * op + 8 : ROWS * op + ROWS]
            side_x_out[ROWS * op : ROWS * op + 8, pl.ds(at, step)] = cos2 * real + sin2 * imag
            side_x_out[ROWS * op + 8 : ROWS * op + ROWS, pl.ds(at, step)] = cos2 * imag - sin2 * real
        both = wide(owned + face + at)
        add_gram(high_v[1, :, pl.ds(at, step)], both)
        side_y_out[:, pl.ds(at, step)] = both

    chunk = owned // OUT_CHUNKS

    def out_copies(c):
        cols = pl.ds(c * chunk, chunk)
        return (
            pltpu.make_async_copy(images.at[pl.ds(0, ROWS), cols], curl_out.at[:, cols], out_sems.at[0, c]),
            pltpu.make_async_copy(images.at[pl.ds(ROWS, ROWS), cols], mass_out.at[:, cols], out_sems.at[1, c]),
        )

    for c in range(OUT_CHUNKS):

        @pl.loop(0, chunk // step, unroll=4)
        def _(b):
            at = pl.multiple_of(c * chunk + b * step, step)
            both = wide(at)
            add_gram(own_v[:, pl.ds(at, step)], both)
            images[:, pl.ds(at, step)] = both

        for copy in out_copies(c):
            copy.start()

    total = gram[...]
    of_real, of_imag = total[:8], total[8:]
    odd = ((lax.broadcasted_iota(jnp.int32, (8, LANES), 1) >> 3) & 1) == 1
    gram_out[...] = jnp.where(
        odd, of_real - pltpu.roll(of_imag, 8, 1), of_real + pltpu.roll(of_imag, LANES - 8, 1)
    )
    for c in range(OUT_CHUNKS):
        for copy in out_copies(c):
            copy.wait()


def part_images(count, phase, idx, own, high_x, high_y, stiff, mass, kh, kl):
    shape = jax.ShapeDtypeStruct
    owned, face = own.shape[1], high_x.shape[1]
    extent = owned + 2 * face
    f32 = jnp.float32
    dma = pltpu.SemaphoreType.DMA
    return pl.pallas_call(
        part_kernel,
        out_shape=(
            shape((ROWS, owned), f32),
            shape((ROWS, owned), f32),
            shape((2 * ROWS, face), f32),
            shape((2 * ROWS, face), f32),
            shape((8, LANES), f32),
        ),
        in_specs=[SMEM, ANY, ANY, ANY, ANY] + [VMEM] * 6,
        out_specs=(ANY, ANY, VMEM, VMEM, VMEM),
        scratch_shapes=[pltpu.VMEM((extent, LANES), f32)] * 5
        + [
            pltpu.VMEM((GTILES, BLOCK, LANES), f32),
            pltpu.VMEM((TILES, BLOCK, LANES), f32),
            pltpu.VMEM((ROWS, LANES), f32),
            pltpu.SMEM((idx.size,), jnp.int32),
            pltpu.VMEM((ROWS, owned), f32),
            pltpu.VMEM((2, ROWS, face), f32),
            pltpu.VMEM((2 * ROWS, owned), f32),
            dma((4,)),
            dma((2, OUT_CHUNKS)),
        ],
        compiler_params=pltpu.CompilerParams(vmem_limit_bytes=VMEM_BYTES),
        name="part_images",
    )(count, idx.reshape(-1), own, high_x, high_y, phase, idx, stiff, mass, kh, kl)


def exchange_kernel(
    side_x_hbm,
    side_y_hbm,
    curl_hbm,
    mass_hbm,
    gram_ref,
    lows_out,
    gram_out,
    back,
    low,
    held,
    sums,
    low_sems,
    side_sems,
    send_sems,
    recv_sems,
):
    face = side_x_hbm.shape[1]
    owned = curl_hbm.shape[1]
    n_px, n_py = lax.axis_size("px"), lax.axis_size("py")
    a, b = lax.axis_index("px"), lax.axis_index("py")
    core, at_y, high = lax.rem(a, 2), lax.rem(a // 2, GROUP), a // (2 * GROUP)
    at_z, side = lax.rem(b, GROUP), b // GROUP

    def along_y(k):
        return {"px": high * (2 * GROUP) + k * 2 + core}

    def along_z(k):
        return {"py": side * GROUP + k}

    def over_rest(k):
        return {"px": (k // 4) * (2 * GROUP) + at_y * 2 + lax.rem(k, 2), "py": lax.rem(k // 2, 2) * GROUP + at_z}

    groups = ((along_y, at_y), (along_z, at_z), (over_rest, high * 4 + side * 2 + core))
    next_x, last_x = {"px": lax.rem(a + 1, n_px)}, {"px": lax.rem(a + n_px - 1, n_px)}
    next_y, last_y = {"py": lax.rem(b + 1, n_py)}, {"py": lax.rem(b + n_py - 1, n_py)}
    barrier = pltpu.get_barrier_semaphore()

    def greet(device):
        pl.semaphore_signal(barrier, 1, device_id=device, device_id_type=pl.DeviceIdType.MESH)

    for place, me in groups:
        for k in range(1, GROUP):
            greet(place(lax.rem(me + k, GROUP)))
    greet(next_x)
    greet(last_x)

    @pl.when(b < n_py - 1)
    def _():
        greet(next_y)

    @pl.when(b > 0)
    def _():
        greet(last_y)

    reads = [
        pltpu.make_async_copy(image.at[:, pl.ds(owned - 2 * face, 2 * face)], low.at[op], low_sems.at[op])
        for op, image in enumerate((curl_hbm, mass_hbm))
    ]
    write = pltpu.make_async_copy(low, lows_out, low_sems.at[2])
    for read in reads:
        read.start()
    peers = 3 * (GROUP - 1) + 2
    pl.semaphore_wait(barrier, peers + jnp.minimum(b, 1) + jnp.minimum(n_py - 1 - b, 1))

    def tile_copy(phase, source, to, at):
        return pltpu.make_async_remote_copy(
            src_ref=source,
            dst_ref=held.at[phase, at],
            send_sem=send_sems.at[phase, to],
            recv_sem=recv_sems.at[phase, at],
            device_id=groups[phase][0](to),
            device_id_type=pl.DeviceIdType.MESH,
        )

    def others(me):
        return [lax.rem(me + k, GROUP) for k in range(1, GROUP)]

    def send_all(phase, source):
        me = groups[phase][1]
        for to in others(me):
            tile_copy(phase, source, to, me).start()
        held[phase, pl.ds(me, 1)] = source[...][None]

    def sum_all(phase, source):
        me = groups[phase][1]
        for other in others(me):
            tile_copy(phase, source, other, other).wait_recv()
        total = held[phase, 0]
        for at in range(1, GROUP):
            total = total + held[phase, at]
        return total

    def side_copy(source, at, device):
        return pltpu.make_async_remote_copy(
            src_ref=source,
            dst_ref=back.at[at],
            send_sem=side_sems.at[0, at],
            recv_sem=side_sems.at[1, at],
            device_id=device,
            device_id_type=pl.DeviceIdType.MESH,
        )

    to_x = side_copy(side_x_hbm, 0, next_x)
    to_y = side_copy(side_y_hbm, 1, next_y)
    send_all(0, gram_ref)
    to_x.start()

    @pl.when(b < n_py - 1)
    def _():
        to_y.start()

    sums[0] = sum_all(0, gram_ref)
    send_all(1, sums.at[0])
    for read in reads:
        read.wait()
    sums[1] = sum_all(1, sums.at[0])
    send_all(2, sums.at[1])
    to_x.wait_recv()
    for op in range(2):
        low[op, :, :face] += back[0, ROWS * op : ROWS * op + ROWS, :]

    @pl.when(b > 0)
    def _():
        to_y.wait_recv()
        for op in range(2):
            low[op, :, face:] += back[1, ROWS * op : ROWS * op + ROWS, :]

    write.start()
    whole = sum_all(2, sums.at[1])
    for op in range(2):
        for part in range(2):
            at = 16 * op + 8 * part
            gram_out[op, part] = whole[:, at : at + 8] / float(n_px * n_py * owned)
    to_x.wait_send()

    @pl.when(b < n_py - 1)
    def _():
        to_y.wait_send()

    for phase, source in enumerate((gram_ref, sums.at[0], sums.at[1])):
        me = groups[phase][1]
        for to in others(me):
            tile_copy(phase, source, to, me).wait_send()
    write.wait()


def exchange(side_x, side_y, curl, mass, gram):
    shape = jax.ShapeDtypeStruct
    f32 = jnp.float32
    dma = pltpu.SemaphoreType.DMA
    face = side_x.shape[1]
    return pl.pallas_call(
        exchange_kernel,
        out_shape=(shape((2, ROWS, 2 * face), f32), shape((2, 2, 8, 8), f32)),
        in_specs=[ANY] * 4 + [VMEM],
        out_specs=(ANY, VMEM),
        scratch_shapes=[
            pltpu.VMEM((2, 2 * ROWS, face), f32),
            pltpu.VMEM((2, ROWS, 2 * face), f32),
            pltpu.VMEM((3, GROUP, 8, LANES), f32),
            pltpu.VMEM((2, 8, LANES), f32),
            dma((3,)),
            dma((2, 2)),
            dma((3, GROUP)),
            dma((3, GROUP)),
        ],
        compiler_params=pltpu.CompilerParams(
            collective_id=0, has_side_effects=True, vmem_limit_bytes=VMEM_BYTES
        ),
        name="exchange",
    )(side_x, side_y, curl, mass, gram)


def finish_kernel(curl_in, mass_in, lows, gram_ref, curl_out, mass_out, gram_out, sems):
    width = lows.shape[2]
    writes = [
        pltpu.make_async_copy(lows.at[op], image.at[:, pl.ds(image.shape[1] - width, width)], sems.at[op])
        for op, image in enumerate((curl_out, mass_out))
    ]
    for write in writes:
        write.start()
    gram_out[...] = gram_ref[...]
    for write in writes:
        write.wait()


def finish(curl, mass, lows, gram):
    shape = jax.ShapeDtypeStruct
    return pl.pallas_call(
        finish_kernel,
        out_shape=tuple(shape(value.shape, jnp.float32) for value in (curl, mass, gram)),
        in_specs=[ANY, ANY, ANY, VMEM],
        out_specs=(ANY, ANY, VMEM),
        scratch_shapes=[pltpu.SemaphoreType.DMA((2,))],
        input_output_aliases={0: 0, 1: 1},
        compiler_params=pltpu.CompilerParams(vmem_limit_bytes=VMEM_BYTES),
        name="finish",
    )(curl, mass, lows, gram)


def on_device(
    trial_block,
    stiff_coef,
    mass_coef,
    elem_count,
    elem_dofs,
    pairing,
    bloch_fraction,
    stiff_mat,
    mass_mat,
):
    owned = trial_block.shape[-1]
    own = trial_block.reshape(ROWS, owned)
    high_x, high_y, phase, idx, kh, kl = begin(
        bloch_fraction,
        own,
        elem_dofs[0, 0].T.reshape(-1, LANES),
        pairing.reshape(-1, LANES),
        stiff_mat,
        mass_mat,
    )
    curl, mass, side_x, side_y, gram = part_images(
        elem_count, phase, idx, own, high_x, high_y, stiff_coef[0], mass_coef[0], kh, kl
    )
    lows, gram = exchange(side_x, side_y, curl, mass, gram)
    curl, mass, gram = finish(curl, mass, lows, gram)
    return curl.reshape(trial_block.shape), mass.reshape(trial_block.shape), gram


def solution(mesh):
    return jax.shard_map(
        on_device,
        mesh=mesh,
        in_specs=(
            P("px", "py", None, None, None),
            P("px", "py", None),
            P("px", "py", None),
            P("px", "py"),
            P("px", "py", None, None),
            P(),
            P(),
            P(),
            P(),
        ),
        out_specs=(P("px", "py", None, None, None), P("px", "py", None, None, None), P()),
        check_vma=False,
    )
```

```python
import functools
import math

import jax
import jax.numpy as jnp
from jax import lax
from jax.experimental import pallas as pl
from jax.experimental.pallas import tpu as pltpu
from jax.sharding import PartitionSpec as P

HIGH = lax.Precision.HIGHEST
LANES = 128
ROWS = 16
NLOC = 20
HALO_SLOTS = 128
BLOCK = 256
TILES = 5
GTILES = 3
LANE_SETS = 4

VMEM = pl.BlockSpec(memory_space=pltpu.VMEM)
SMEM = pl.BlockSpec(memory_space=pltpu.SMEM)
ANY = pl.BlockSpec(memory_space=pl.ANY)
VMEM_BYTES = 56 * 2**20
OUT_CHUNKS = 2
GROUP = 8


def split_bf16(value):
    high = value.astype(jnp.bfloat16)
    low = (value - high.astype(jnp.float32)).astype(jnp.bfloat16)
    return high, low


def dot_split(a, b):
    (ah, al), (bh, bl) = a, b
    dot = functools.partial(jnp.dot, preferred_element_type=jnp.float32)
    both = dot(jnp.concatenate([ah, al], axis=0), bh)
    rows = ah.shape[0]
    return both[:rows] + (both[rows:] + dot(ah, bl))


def begin_kernel(
    fraction_ref,
    idx_hbm,
    own_ref,
    dofs_ref,
    pairing_ref,
    stiff_ref,
    mass_ref,
    phase_out,
    idx_out,
    kh_out,
    kl_out,
    high_out,
    gathered,
    ext,
    idx_all,
    head_v,
    head_s,
    high_in,
    sems,
):
    face = pairing_ref.shape[0] * LANES
    owned = own_ref.shape[1]
    capacity = idx_all.shape[0] // NLOC
    n_px, n_py = lax.axis_size("px"), lax.axis_size("py")
    a, b = lax.axis_index("px"), lax.axis_index("py")
    below_x, above_x = lax.rem(a + n_px - 1, n_px), lax.rem(a + 1, n_px)
    below_y, above_y = lax.rem(b + n_py - 1, n_py), lax.rem(b + 1, n_py)

    barrier = pltpu.get_barrier_semaphore()

    def greet(axis, to):
        pl.semaphore_signal(barrier, 1, device_id={axis: to}, device_id_type=pl.DeviceIdType.MESH)

    greet("px", below_x)
    greet("px", above_x)

    @pl.when(b > 0)
    def _():
        greet("py", below_y)

    @pl.when(b < n_py - 1)
    def _():
        greet("py", above_y)

    def face_copy(first, at, axis, to):
        return pltpu.make_async_remote_copy(
            src_ref=own_ref.at[:, pl.ds(first, face)],
            dst_ref=high_in.at[at],
            send_sem=sems.at[2 * at],
            recv_sem=sems.at[2 * at + 1],
            device_id={axis: to},
            device_id_type=pl.DeviceIdType.MESH,
        )

    to_x = face_copy(owned - 2 * face, 0, "px", below_x)
    to_y = face_copy(owned - face, 1, "py", below_y)
    idx_in = pltpu.make_async_copy(idx_hbm, idx_all, sems.at[4])
    idx_in.start()

    at_end = jnp.broadcast_to(a, (1, LANES)) == n_px - 1
    above = jnp.broadcast_to(fraction_ref[0], (1, LANES)).astype(jnp.float32)
    below = jnp.broadcast_to(fraction_ref[1], (1, LANES)).astype(jnp.float32)
    angle = 2.0 * math.pi * above / below
    cosine = jnp.where(at_end, jnp.cos(angle), 1.0)
    sine = jnp.where(at_end, jnp.sin(angle), 0.0)
    phase_out[0:1, :] = cosine
    phase_out[1:2, :] = sine

    blocks = dofs_ref.shape[0] // NLOC
    idx_out[...] = dofs_ref[...]
    heads = pl.ds(0, NLOC, stride=blocks)
    head = dofs_ref[heads, :]
    spot = head - owned
    local = spot & (LANES - 1)
    found = jnp.zeros_like(head)
    for row in range(pairing_ref.shape[0]):
        values = jnp.broadcast_to(pairing_ref[row : row + 1, :], head.shape)
        here = jnp.take_along_axis(values, local, axis=1)
        found = jnp.where((spot >> 7) == row, here + owned, found)
    wraps = (spot >= 0) & (spot < face) & (jnp.broadcast_to(a, head.shape) == n_px - 1)
    head = jnp.where(wraps, found, head)
    idx_out[heads, :] = head
    head_v[:NLOC, :] = head
    head_v[NLOC:, :] = jnp.zeros_like(head_v[NLOC:, :])
    head_in = pltpu.make_async_copy(head_v, head_s, sems.at[5])
    head_in.start()

    grow = lax.broadcasted_iota(jnp.int32, (GTILES * LANES, NLOC), 0)
    gcol = lax.broadcasted_iota(jnp.int32, (GTILES * LANES, NLOC), 1)
    spread_i = ((grow >> 4) == gcol).astype(jnp.float32)
    trow = lax.broadcasted_iota(jnp.int32, (NLOC, TILES * LANES), 0)
    tcol = lax.broadcasted_iota(jnp.int32, (NLOC, TILES * LANES), 1)
    spread_j = ((tcol >> 5) == trow).astype(jnp.float32)
    dot = functools.partial(jnp.dot, precision=HIGH, preferred_element_type=jnp.float32)
    stiff = dot(dot(spread_i, stiff_ref[...].T), spread_j)
    mass = dot(dot(spread_i, mass_ref[...].T), spread_j)
    krow = lax.broadcasted_iota(jnp.int32, (GTILES * LANES, TILES * LANES), 0)
    kcol = lax.broadcasted_iota(jnp.int32, (GTILES * LANES, TILES * LANES), 1)
    both = jnp.where(((kcol >> 4) & 1) == 0, stiff, mass)
    both = jnp.where((krow & 15) == (kcol & 15), both, 0.0)
    kh_out[...], kl_out[...] = split_bf16(both)

    def put_rows(at, block):
        ext[pl.ds(at, LANES), :] = jnp.concatenate([block] * (LANES // ROWS), axis=0).T

    @pl.loop(0, owned // LANES, unroll=8)
    def _(block):
        at = pl.multiple_of(block * LANES, LANES)
        put_rows(at, own_ref[:, pl.ds(at, LANES)])

    lane_set = lax.broadcasted_iota(jnp.int32, (1, LANES), 1) >> 4

    def gather(slot, index):
        for tile in range(GTILES):
            row = None
            for i in range(8 * tile, min(8 * tile + 8, NLOC)):
                got = ext[pl.ds(index(i, slot), 1), :]
                row = got if row is None else jnp.where(lane_set == i % 8, got, row)
            gathered[tile, pl.ds(slot, 1), :] = row

    idx_s = [idx_all.at[pl.ds(j * capacity, capacity)] for j in range(NLOC)]
    idx_in.wait()

    def gather_slots(first, last):
        @pl.loop(first, last, unroll=4)
        def _(slot):
            gather(slot, lambda i, slot: idx_s[i][slot])

    middle = HALO_SLOTS + (capacity - HALO_SLOTS) // 2
    gather_slots(HALO_SLOTS, middle)

    pl.semaphore_wait(barrier, 2 + jnp.minimum(b, 1) + jnp.minimum(n_py - 1 - b, 1))
    to_x.start()

    @pl.when(b > 0)
    def _():
        to_y.start()

    gather_slots(middle, capacity)
    to_x.wait()

    @pl.when(b > 0)
    def _():
        to_y.wait_send()

    @pl.when(b < n_py - 1)
    def _():
        to_y.wait_recv()

    @pl.when(b == n_py - 1)
    def _():
        high_in[1] = jnp.zeros_like(high_in[1])

    @pl.loop(0, face // LANES, unroll=4)
    def _(block):
        at = pl.multiple_of(block * LANES, LANES)
        got = high_in[0, :, pl.ds(at, LANES)]
        real, imag = got[: ROWS // 2], got[ROWS // 2 :]
        turned = jnp.concatenate([cosine * real - sine * imag, sine * real + cosine * imag], axis=0)
        along_y = high_in[1, :, pl.ds(at, LANES)]
        high_out[0, :, pl.ds(at, LANES)] = turned
        high_out[1, :, pl.ds(at, LANES)] = along_y
        put_rows(owned + at, turned)
        put_rows(owned + face + at, along_y)

    head_in.wait()

    @pl.loop(0, HALO_SLOTS, unroll=4)
    def _(slot):
        gather(slot, lambda i, slot: head_s[i, slot])


def begin(fraction, own, dofs, pairing, stiff_mat, mass_mat):
    shape = jax.ShapeDtypeStruct
    f32 = jnp.float32
    face, owned = pairing.size, own.shape[1]
    spread = shape((GTILES * LANES, TILES * LANES), jnp.bfloat16)
    return pl.pallas_call(
        begin_kernel,
        out_shape=(
            shape((2, LANES), f32),
            shape(dofs.shape, jnp.int32),
            spread,
            spread,
            shape((2, ROWS, face), f32),
            shape((GTILES, dofs.size // NLOC, LANES), f32),
        ),
        in_specs=[SMEM, ANY] + [VMEM] * 5,
        out_specs=(VMEM,) * 6,
        scratch_shapes=[
            pltpu.VMEM((owned + 2 * face, LANES), f32),
            pltpu.SMEM((dofs.size,), jnp.int32),
            pltpu.VMEM((24, LANES), jnp.int32),
            pltpu.SMEM((24, LANES), jnp.int32),
            pltpu.VMEM((2, ROWS, face), f32),
            pltpu.SemaphoreType.DMA((6,)),
        ],
        compiler_params=pltpu.CompilerParams(
            collective_id=1, has_side_effects=True, vmem_limit_bytes=VMEM_BYTES
        ),
        name="begin",
    )(fraction, dofs.reshape(-1), own, dofs, pairing, stiff_mat, mass_mat)


def part_kernel(
    count_ref,
    idx_hbm,
    own_hbm,
    high_hbm,
    gathered_hbm,
    phase_ref,
    idx_v,
    stiff_ref,
    mass_ref,
    kh_ref,
    kl_ref,
    curl_out,
    mass_out,
    side_x_out,
    side_y_out,
    gram_out,
    acc0,
    acc1,
    acc2,
    acc3,
    gathered,
    terms,
    gram,
    idx_all,
    own_v,
    high_v,
    images,
    in_sems,
    out_sems,
):
    accs = (acc0, acc1, acc2, acc3)
    owned = own_v.shape[1]
    face = high_v.shape[2]
    cosine, sine = phase_ref[0:1, :], phase_ref[1:2, :]
    count = count_ref[0, 0]
    capacity = stiff_ref.shape[1]
    idx_s = [idx_all.at[pl.ds(j * capacity, capacity)] for j in range(NLOC)]

    own_in = pltpu.make_async_copy(own_hbm, own_v, in_sems.at[0])
    high_in = pltpu.make_async_copy(high_hbm, high_v, in_sems.at[1])
    gathered_in = pltpu.make_async_copy(gathered_hbm, gathered, in_sems.at[2])
    idx_in = pltpu.make_async_copy(idx_hbm, idx_all, in_sems.at[3])
    gathered_in.start()
    idx_in.start()
    own_in.start()
    high_in.start()

    zero_rows = jnp.zeros((LANES, LANES), jnp.float32)

    @pl.loop(0, acc0.shape[0] // LANES)
    def _(b):
        at = pl.multiple_of(b * LANES, LANES)
        for acc in accs:
            acc[pl.ds(at, LANES), :] = zero_rows

    gram[...] = jnp.zeros_like(gram)

    def idx_row(j, block_id, part):
        row = j * (capacity // LANES) + block_id * (BLOCK // LANES) + part
        return jnp.broadcast_to(idx_v[pl.ds(row, 1), :], (LANES // LANE_SETS, LANES))

    gathered_in.wait()
    idx_in.wait()

    @pl.loop(0, (count + BLOCK - 1) // BLOCK)
    def _(block_id):
        first = pl.multiple_of(block_id * BLOCK, BLOCK)

        values = jnp.concatenate([gathered[tile, pl.ds(first, BLOCK), :] for tile in range(GTILES)], axis=1)
        products = dot_split(split_bf16(values), (kh_ref[...], kl_ref[...]))
        slots = first + lax.broadcasted_iota(jnp.int32, (1, BLOCK), 1)
        live = slots < count
        stiff = jnp.where(live, stiff_ref[:, pl.ds(first, BLOCK)], 0.0)
        mass = jnp.where(live, mass_ref[:, pl.ds(first, BLOCK)], 0.0)
        pair = [jnp.broadcast_to(stiff, (ROWS, BLOCK)), jnp.broadcast_to(mass, (ROWS, BLOCK))]
        coef = jnp.concatenate(pair * LANE_SETS, axis=0).T
        scaled = [products[:, t * LANES : (t + 1) * LANES] * coef for t in range(TILES)]

        names = []
        for t in range(TILES):
            rows = [
                jnp.concatenate([idx_row(j, block_id, part) for part in range(BLOCK // LANES)], axis=1)
                for j in range(LANE_SETS * t, LANE_SETS * t + LANE_SETS)
            ]
            names.append(jnp.concatenate(rows, axis=0).astype(jnp.float32).T)
        for t in range(TILES):
            total = scaled[t]
            for s in range(t):
                total = total + jnp.where(names[s] == names[t], scaled[s], 0.0)
            terms[t] = total

        @pl.loop(0, BLOCK, unroll=4)
        def _(e):
            slot = first + e
            added = [terms[t, pl.ds(e, 1), :] for t in range(TILES)]
            places = [[idx_s[LANE_SETS * t + g][slot] for t in range(TILES)] for g in range(LANE_SETS)]
            held = [[accs[g][pl.ds(places[g][t], 1), :] for t in range(TILES)] for g in range(LANE_SETS)]
            for t in range(TILES):
                for g in range(LANE_SETS):
                    accs[g][pl.ds(places[g][t], 1), :] = held[g][t] + added[t]

    own_in.wait()
    high_in.wait()
    quarter = lax.broadcasted_iota(jnp.int32, (LANES, LANES), 1) >> 5

    def summed(at):
        rows = accs[0][pl.ds(at, LANES), :]
        for g in range(1, LANE_SETS):
            rows = jnp.where(quarter == g, accs[g][pl.ds(at, LANES), :], rows)
        rows = rows.T
        return (rows[:32] + rows[32:64]) + (rows[64:96] + rows[96:])

    def wide(at):
        return jnp.concatenate([summed(at), summed(at + LANES)], axis=1)

    across = (((1,), (1,)), ((), ()))
    dot = functools.partial(lax.dot_general, dimension_numbers=across, preferred_element_type=jnp.float32)

    def add_gram(left, both):
        (lh, ll), (bh, bl) = split_bf16(left), split_bf16(both)
        pieces = dot(jnp.concatenate([lh, ll], axis=0), bh)
        gram[:, : 2 * ROWS] += pieces[:ROWS] + (pieces[ROWS:] + dot(lh, bl))

    step = 2 * LANES

    @pl.loop(0, face // step, unroll=2)
    def _(b):
        at = pl.multiple_of(b * step, step)
        both = wide(owned + at)
        add_gram(high_v[0, :, pl.ds(at, step)], both)
        cos2, sin2 = (jnp.concatenate([row, row], axis=1) for row in (cosine, sine))
        for op in range(2):
            real, imag = both[ROWS * op : ROWS * op + 8], both[ROWS * op + 8 : ROWS * op + ROWS]
            side_x_out[ROWS * op : ROWS * op + 8, pl.ds(at, step)] = cos2 * real + sin2 * imag
            side_x_out[ROWS * op + 8 : ROWS * op + ROWS, pl.ds(at, step)] = cos2 * imag - sin2 * real
        both = wide(owned + face + at)
        add_gram(high_v[1, :, pl.ds(at, step)], both)
        side_y_out[:, pl.ds(at, step)] = both

    chunk = owned // OUT_CHUNKS

    def out_copies(c):
        cols = pl.ds(c * chunk, chunk)
        return (
            pltpu.make_async_copy(images.at[pl.ds(0, ROWS), cols], curl_out.at[:, cols], out_sems.at[0, c]),
            pltpu.make_async_copy(images.at[pl.ds(ROWS, ROWS), cols], mass_out.at[:, cols], out_sems.at[1, c]),
        )

    for c in range(OUT_CHUNKS):

        @pl.loop(0, chunk // step, unroll=4)
        def _(b):
            at = pl.multiple_of(c * chunk + b * step, step)
            both = wide(at)
            add_gram(own_v[:, pl.ds(at, step)], both)
            images[:, pl.ds(at, step)] = both

        for copy in out_copies(c):
            copy.start()

    total = gram[...]
    of_real, of_imag = total[:8], total[8:]
    odd = ((lax.broadcasted_iota(jnp.int32, (8, LANES), 1) >> 3) & 1) == 1
    gram_out[...] = jnp.where(
        odd, of_real - pltpu.roll(of_imag, 8, 1), of_real + pltpu.roll(of_imag, LANES - 8, 1)
    )
    for c in range(OUT_CHUNKS):
        for copy in out_copies(c):
            copy.wait()


def part_images(count, phase, idx, own, high, gathered, stiff, mass, kh, kl):
    shape = jax.ShapeDtypeStruct
    owned, face = own.shape[1], high.shape[2]
    extent = owned + 2 * face
    f32 = jnp.float32
    dma = pltpu.SemaphoreType.DMA
    return pl.pallas_call(
        part_kernel,
        out_shape=(
            shape((ROWS, owned), f32),
            shape((ROWS, owned), f32),
            shape((2 * ROWS, face), f32),
            shape((2 * ROWS, face), f32),
            shape((8, LANES), f32),
        ),
        in_specs=[SMEM, ANY, ANY, ANY, ANY] + [VMEM] * 6,
        out_specs=(ANY, ANY, VMEM, VMEM, VMEM),
        scratch_shapes=[pltpu.VMEM((extent, LANES), f32)] * 4
        + [
            pltpu.VMEM(gathered.shape, f32),
            pltpu.VMEM((TILES, BLOCK, LANES), f32),
            pltpu.VMEM((ROWS, LANES), f32),
            pltpu.SMEM((idx.size,), jnp.int32),
            pltpu.VMEM((ROWS, owned), f32),
            pltpu.VMEM((2, ROWS, face), f32),
            pltpu.VMEM((2 * ROWS, owned), f32),
            dma((4,)),
            dma((2, OUT_CHUNKS)),
        ],
        compiler_params=pltpu.CompilerParams(vmem_limit_bytes=VMEM_BYTES),
        name="part_images",
    )(count, idx.reshape(-1), own, high, gathered, phase, idx, stiff, mass, kh, kl)


def exchange_kernel(
    side_x_hbm,
    side_y_hbm,
    curl_hbm,
    mass_hbm,
    gram_ref,
    lows_out,
    gram_out,
    back,
    low,
    held,
    sums,
    low_sems,
    side_sems,
    send_sems,
    recv_sems,
):
    face = side_x_hbm.shape[1]
    owned = curl_hbm.shape[1]
    n_px, n_py = lax.axis_size("px"), lax.axis_size("py")
    a, b = lax.axis_index("px"), lax.axis_index("py")
    core, at_y, high = lax.rem(a, 2), lax.rem(a // 2, GROUP), a // (2 * GROUP)
    at_z, side = lax.rem(b, GROUP), b // GROUP

    def along_y(k):
        return {"px": high * (2 * GROUP) + k * 2 + core}

    def along_z(k):
        return {"py": side * GROUP + k}

    def over_rest(k):
        return {"px": (k // 4) * (2 * GROUP) + at_y * 2 + lax.rem(k, 2), "py": lax.rem(k // 2, 2) * GROUP + at_z}

    groups = ((along_y, at_y), (along_z, at_z), (over_rest, high * 4 + side * 2 + core))
    next_x, last_x = {"px": lax.rem(a + 1, n_px)}, {"px": lax.rem(a + n_px - 1, n_px)}
    next_y, last_y = {"py": lax.rem(b + 1, n_py)}, {"py": lax.rem(b + n_py - 1, n_py)}
    barrier = pltpu.get_barrier_semaphore()

    def greet(device):
        pl.semaphore_signal(barrier, 1, device_id=device, device_id_type=pl.DeviceIdType.MESH)

    for place, me in groups:
        for k in range(1, GROUP):
            greet(place(lax.rem(me + k, GROUP)))
    greet(next_x)
    greet(last_x)

    @pl.when(b < n_py - 1)
    def _():
        greet(next_y)

    @pl.when(b > 0)
    def _():
        greet(last_y)

    reads = [
        pltpu.make_async_copy(image.at[:, pl.ds(owned - 2 * face, 2 * face)], low.at[op], low_sems.at[op])
        for op, image in enumerate((curl_hbm, mass_hbm))
    ]
    write = pltpu.make_async_copy(low, lows_out, low_sems.at[2])
    for read in reads:
        read.start()
    peers = 3 * (GROUP - 1) + 2
    pl.semaphore_wait(barrier, peers + jnp.minimum(b, 1) + jnp.minimum(n_py - 1 - b, 1))

    def tile_copy(phase, source, to, at):
        return pltpu.make_async_remote_copy(
            src_ref=source,
            dst_ref=held.at[phase, at],
            send_sem=send_sems.at[phase, to],
            recv_sem=recv_sems.at[phase, at],
            device_id=groups[phase][0](to),
            device_id_type=pl.DeviceIdType.MESH,
        )

    def others(me):
        return [lax.rem(me + k, GROUP) for k in range(1, GROUP)]

    def send_all(phase, source):
        me = groups[phase][1]
        for to in others(me):
            tile_copy(phase, source, to, me).start()
        held[phase, pl.ds(me, 1)] = source[...][None]

    def sum_all(phase, source):
        me = groups[phase][1]
        for other in others(me):
            tile_copy(phase, source, other, other).wait_recv()
        total = held[phase, 0]
        for at in range(1, GROUP):
            total = total + held[phase, at]
        return total

    def side_copy(source, at, device):
        return pltpu.make_async_remote_copy(
            src_ref=source,
            dst_ref=back.at[at],
            send_sem=side_sems.at[0, at],
            recv_sem=side_sems.at[1, at],
            device_id=device,
            device_id_type=pl.DeviceIdType.MESH,
        )

    to_x = side_copy(side_x_hbm, 0, next_x)
    to_y = side_copy(side_y_hbm, 1, next_y)
    send_all(0, gram_ref)
    to_x.start()

    @pl.when(b < n_py - 1)
    def _():
        to_y.start()

    sums[0] = sum_all(0, gram_ref)
    send_all(1, sums.at[0])
    for read in reads:
        read.wait()
    sums[1] = sum_all(1, sums.at[0])
    send_all(2, sums.at[1])
    to_x.wait_recv()
    for op in range(2):
        low[op, :, :face] += back[0, ROWS * op : ROWS * op + ROWS, :]

    @pl.when(b > 0)
    def _():
        to_y.wait_recv()
        for op in range(2):
            low[op, :, face:] += back[1, ROWS * op : ROWS * op + ROWS, :]

    write.start()
    whole = sum_all(2, sums.at[1])
    for op in range(2):
        for part in range(2):
            at = 16 * op + 8 * part
            gram_out[op, part] = whole[:, at : at + 8] / float(n_px * n_py * owned)
    to_x.wait_send()

    @pl.when(b < n_py - 1)
    def _():
        to_y.wait_send()

    for phase, source in enumerate((gram_ref, sums.at[0], sums.at[1])):
        me = groups[phase][1]
        for to in others(me):
            tile_copy(phase, source, to, me).wait_send()
    write.wait()


def exchange(side_x, side_y, curl, mass, gram):
    shape = jax.ShapeDtypeStruct
    f32 = jnp.float32
    dma = pltpu.SemaphoreType.DMA
    face = side_x.shape[1]
    return pl.pallas_call(
        exchange_kernel,
        out_shape=(shape((2, ROWS, 2 * face), f32), shape((2, 2, 8, 8), f32)),
        in_specs=[ANY] * 4 + [VMEM],
        out_specs=(ANY, VMEM),
        scratch_shapes=[
            pltpu.VMEM((2, 2 * ROWS, face), f32),
            pltpu.VMEM((2, ROWS, 2 * face), f32),
            pltpu.VMEM((3, GROUP, 8, LANES), f32),
            pltpu.VMEM((2, 8, LANES), f32),
            dma((3,)),
            dma((2, 2)),
            dma((3, GROUP)),
            dma((3, GROUP)),
        ],
        compiler_params=pltpu.CompilerParams(
            collective_id=0, has_side_effects=True, vmem_limit_bytes=VMEM_BYTES
        ),
        name="exchange",
    )(side_x, side_y, curl, mass, gram)


def finish_kernel(curl_in, mass_in, lows, gram_ref, curl_out, mass_out, gram_out, sems):
    width = lows.shape[2]
    writes = [
        pltpu.make_async_copy(lows.at[op], image.at[:, pl.ds(image.shape[1] - width, width)], sems.at[op])
        for op, image in enumerate((curl_out, mass_out))
    ]
    for write in writes:
        write.start()
    gram_out[...] = gram_ref[...]
    for write in writes:
        write.wait()


def finish(curl, mass, lows, gram):
    shape = jax.ShapeDtypeStruct
    return pl.pallas_call(
        finish_kernel,
        out_shape=tuple(shape(value.shape, jnp.float32) for value in (curl, mass, gram)),
        in_specs=[ANY, ANY, VMEM, VMEM],
        out_specs=(ANY, ANY, VMEM),
        scratch_shapes=[pltpu.SemaphoreType.DMA((2,))],
        input_output_aliases={0: 0, 1: 1},
        compiler_params=pltpu.CompilerParams(vmem_limit_bytes=VMEM_BYTES),
        name="finish",
    )(curl, mass, lows, gram)


def on_device(
    trial_block,
    stiff_coef,
    mass_coef,
    elem_count,
    elem_dofs,
    pairing,
    bloch_fraction,
    stiff_mat,
    mass_mat,
):
    owned = trial_block.shape[-1]
    own = trial_block.reshape(ROWS, owned)
    phase, idx, kh, kl, high, gathered = begin(
        bloch_fraction,
        own,
        elem_dofs[0, 0].T.reshape(-1, LANES),
        pairing.reshape(-1, LANES),
        stiff_mat,
        mass_mat,
    )
    curl, mass, side_x, side_y, gram = part_images(
        elem_count, phase, idx, own, high, gathered, stiff_coef[0], mass_coef[0], kh, kl
    )
    lows, gram = exchange(side_x, side_y, curl, mass, gram)
    curl, mass, gram = finish(curl, mass, lows, gram)
    return curl.reshape(trial_block.shape), mass.reshape(trial_block.shape), gram


def solution(mesh):
    return jax.shard_map(
        on_device,
        mesh=mesh,
        in_specs=(
            P("px", "py", None, None, None),
            P("px", "py", None),
            P("px", "py", None),
            P("px", "py"),
            P("px", "py", None, None),
            P(),
            P(),
            P(),
            P(),
        ),
        out_specs=(P("px", "py", None, None, None), P("px", "py", None, None, None), P()),
        check_vma=False,
    )
```

```python
import functools
import math

import jax
import jax.numpy as jnp
from jax import lax
from jax.experimental import pallas as pl
from jax.experimental.pallas import tpu as pltpu
from jax.sharding import PartitionSpec as P

HIGH = lax.Precision.HIGHEST
LANES = 128
ROWS = 16
NLOC = 20
HALO_SLOTS = 128
BLOCK = 512
TILES = 5
GTILES = 3
LANE_SETS = 4

VMEM = pl.BlockSpec(memory_space=pltpu.VMEM)
SMEM = pl.BlockSpec(memory_space=pltpu.SMEM)
ANY = pl.BlockSpec(memory_space=pl.ANY)
VMEM_BYTES = 56 * 2**20
OUT_CHUNKS = 2
GROUP = 8


def split_bf16(value):
    high = value.astype(jnp.bfloat16)
    low = (value - high.astype(jnp.float32)).astype(jnp.bfloat16)
    return high, low


def dot_split(a, b):
    (ah, al), (bh, bl) = a, b
    dot = functools.partial(jnp.dot, preferred_element_type=jnp.float32)
    both = dot(jnp.concatenate([ah, al], axis=0), bh)
    rows = ah.shape[0]
    return both[:rows] + (both[rows:] + dot(ah, bl))


def begin_kernel(
    fraction_ref,
    own_hbm,
    dofs_ref,
    pairing_ref,
    stiff_ref,
    mass_ref,
    high_x,
    high_y,
    phase_out,
    idx_out,
    kh_out,
    kl_out,
    zeros,
    sems,
):
    face = pairing_ref.shape[0] * LANES
    owned = own_hbm.shape[1]
    n_px, n_py = lax.axis_size("px"), lax.axis_size("py")
    a, b = lax.axis_index("px"), lax.axis_index("py")
    below_x, above_x = lax.rem(a + n_px - 1, n_px), lax.rem(a + 1, n_px)
    below_y, above_y = lax.rem(b + n_py - 1, n_py), lax.rem(b + 1, n_py)

    barrier = pltpu.get_barrier_semaphore()

    def greet(axis, to):
        pl.semaphore_signal(barrier, 1, device_id={axis: to}, device_id_type=pl.DeviceIdType.MESH)

    greet("px", below_x)
    greet("px", above_x)

    @pl.when(b > 0)
    def _():
        greet("py", below_y)

    @pl.when(b < n_py - 1)
    def _():
        greet("py", above_y)

    pl.semaphore_wait(barrier, 2 + jnp.minimum(b, 1) + jnp.minimum(n_py - 1 - b, 1))

    def face_copy(first, target, at, axis, to):
        return pltpu.make_async_remote_copy(
            src_ref=own_hbm.at[:, pl.ds(first, face)],
            dst_ref=target,
            send_sem=sems.at[2 * at],
            recv_sem=sems.at[2 * at + 1],
            device_id={axis: to},
            device_id_type=pl.DeviceIdType.MESH,
        )

    to_x = face_copy(owned - 2 * face, high_x, 0, "px", below_x)
    to_y = face_copy(owned - face, high_y, 1, "py", below_y)
    no_y = pltpu.make_async_copy(zeros, high_y, sems.at[4])
    to_x.start()

    @pl.when(b > 0)
    def _():
        to_y.start()

    @pl.when(b == n_py - 1)
    def _():
        zeros[...] = jnp.zeros_like(zeros)
        no_y.start()

    at_end = jnp.broadcast_to(a, (1, LANES)) == n_px - 1
    above = jnp.broadcast_to(fraction_ref[0], (1, LANES)).astype(jnp.float32)
    below = jnp.broadcast_to(fraction_ref[1], (1, LANES)).astype(jnp.float32)
    angle = 2.0 * math.pi * above / below
    phase_out[0:1, :] = jnp.where(at_end, jnp.cos(angle), 1.0)
    phase_out[1:2, :] = jnp.where(at_end, jnp.sin(angle), 0.0)

    blocks = idx_out.shape[0] // NLOC
    for j in range(NLOC):
        for block in range(blocks):
            row = j * blocks + block
            idx_out[row : row + 1, :] = dofs_ref[j, :, block * LANES : (block + 1) * LANES]
    heads = pl.ds(0, NLOC, stride=blocks)
    head = idx_out[heads, :]
    spot = head - owned
    local = spot & (LANES - 1)
    found = jnp.zeros_like(head)
    for row in range(pairing_ref.shape[0]):
        values = jnp.broadcast_to(pairing_ref[row : row + 1, :], head.shape)
        here = jnp.take_along_axis(values, local, axis=1)
        found = jnp.where((spot >> 7) == row, here + owned, found)
    wraps = (spot >= 0) & (spot < face) & (jnp.broadcast_to(a, head.shape) == n_px - 1)
    idx_out[heads, :] = jnp.where(wraps, found, head)

    grow = lax.broadcasted_iota(jnp.int32, (GTILES * LANES, NLOC), 0)
    gcol = lax.broadcasted_iota(jnp.int32, (GTILES * LANES, NLOC), 1)
    spread_i = ((grow >> 4) == gcol).astype(jnp.float32)
    trow = lax.broadcasted_iota(jnp.int32, (NLOC, TILES * LANES), 0)
    tcol = lax.broadcasted_iota(jnp.int32, (NLOC, TILES * LANES), 1)
    spread_j = ((tcol >> 5) == trow).astype(jnp.float32)
    dot = functools.partial(jnp.dot, precision=HIGH, preferred_element_type=jnp.float32)
    stiff = dot(dot(spread_i, stiff_ref[...].T), spread_j)
    mass = dot(dot(spread_i, mass_ref[...].T), spread_j)
    krow = lax.broadcasted_iota(jnp.int32, (GTILES * LANES, TILES * LANES), 0)
    kcol = lax.broadcasted_iota(jnp.int32, (GTILES * LANES, TILES * LANES), 1)
    both = jnp.where(((kcol >> 4) & 1) == 0, stiff, mass)
    both = jnp.where((krow & 15) == (kcol & 15), both, 0.0)
    kh_out[...], kl_out[...] = split_bf16(both)

    to_x.wait()

    @pl.when(b > 0)
    def _():
        to_y.wait_send()

    @pl.when(b < n_py - 1)
    def _():
        to_y.wait_recv()

    @pl.when(b == n_py - 1)
    def _():
        no_y.wait()


def begin(fraction, own, dofs, pairing, stiff_mat, mass_mat):
    shape = jax.ShapeDtypeStruct
    high = shape((ROWS, pairing.size), jnp.float32)
    spread = shape((GTILES * LANES, TILES * LANES), jnp.bfloat16)
    return pl.pallas_call(
        begin_kernel,
        out_shape=(high, high, shape((2, LANES), jnp.float32), shape((dofs.size // LANES, LANES), jnp.int32), spread, spread),
        in_specs=[SMEM, ANY, VMEM, VMEM, VMEM, VMEM],
        out_specs=(ANY, ANY, VMEM, VMEM, VMEM, VMEM),
        scratch_shapes=[
            pltpu.VMEM(high.shape, jnp.float32),
            pltpu.SemaphoreType.DMA((5,)),
        ],
        compiler_params=pltpu.CompilerParams(
            collective_id=1, has_side_effects=True, vmem_limit_bytes=VMEM_BYTES
        ),
        name="begin",
    )(fraction, own, dofs, pairing, stiff_mat, mass_mat)


def part_kernel(
    count_ref,
    idx_hbm,
    own_hbm,
    high_x_hbm,
    high_y_hbm,
    phase_ref,
    idx_v,
    stiff_ref,
    mass_ref,
    kh_hbm,
    kl_hbm,
    curl_out,
    mass_out,
    side_x_hbm,
    side_y_hbm,
    gram_out,
    ext,
    acc0,
    acc1,
    acc2,
    acc3,
    gathered,
    terms,
    gram,
    idx_all,
    own_v,
    high_v,
    images,
    kh_ref,
    kl_ref,
    side_x_out,
    side_y_out,
    in_sems,
    out_sems,
):
    accs = (acc0, acc1, acc2, acc3)
    owned = own_v.shape[1]
    face = high_v.shape[2]
    cosine, sine = phase_ref[0:1, :], phase_ref[1:2, :]
    count = count_ref[0, 0]
    capacity = stiff_ref.shape[1]
    idx_s = [idx_all.at[pl.ds(j * capacity, capacity)] for j in range(NLOC)]

    own_in = pltpu.make_async_copy(own_hbm, own_v, in_sems.at[0])
    high_x_in = pltpu.make_async_copy(high_x_hbm, high_v.at[0], in_sems.at[1])
    high_y_in = pltpu.make_async_copy(high_y_hbm, high_v.at[1], in_sems.at[2])
    idx_in = pltpu.make_async_copy(idx_hbm, idx_all, in_sems.at[3])
    own_in.start()
    idx_in.start()
    high_x_in.start()
    high_y_in.start()
    kh_in = pltpu.make_async_copy(kh_hbm, kh_ref, in_sems.at[4])
    kl_in = pltpu.make_async_copy(kl_hbm, kl_ref, in_sems.at[5])
    kh_in.start()
    kl_in.start()

    zero_rows = jnp.zeros((LANES, LANES), jnp.float32)

    @pl.loop(0, ext.shape[0] // LANES)
    def _(b):
        at = pl.multiple_of(b * LANES, LANES)
        for acc in accs:
            acc[pl.ds(at, LANES), :] = zero_rows

    gram[...] = jnp.zeros_like(gram)

    def put_rows(at, block):
        ext[pl.ds(at, LANES), :] = jnp.concatenate([block] * (LANES // ROWS), axis=0).T

    own_in.wait()

    @pl.loop(0, owned // LANES, unroll=8)
    def _(b):
        at = pl.multiple_of(b * LANES, LANES)
        put_rows(at, own_v[:, pl.ds(at, LANES)])

    high_x_in.wait()
    high_y_in.wait()

    @pl.loop(0, face // LANES, unroll=4)
    def _(b):
        at = pl.multiple_of(b * LANES, LANES)
        got = high_v[0, :, pl.ds(at, LANES)]
        real, imag = got[: ROWS // 2], got[ROWS // 2 :]
        turned = jnp.concatenate([cosine * real - sine * imag, sine * real + cosine * imag], axis=0)
        high_v[0, :, pl.ds(at, LANES)] = turned
        put_rows(owned + at, turned)
        put_rows(owned + face + at, high_v[1, :, pl.ds(at, LANES)])

    def idx_row(j, block_id, part):
        row = j * (capacity // LANES) + block_id * (BLOCK // LANES) + part
        return jnp.broadcast_to(idx_v[pl.ds(row, 1), :], (LANES // LANE_SETS, LANES))

    lane_set = lax.broadcasted_iota(jnp.int32, (1, LANES), 1) >> 4
    idx_in.wait()
    kh_in.wait()
    kl_in.wait()

    @pl.loop(0, (count + BLOCK - 1) // BLOCK)
    def _(block_id):
        first = pl.multiple_of(block_id * BLOCK, BLOCK)

        @pl.loop(0, BLOCK, unroll=4)
        def _(e):
            slot = first + e
            for tile in range(GTILES):
                inside = range(8 * tile, min(8 * tile + 8, NLOC))
                row = None
                for i in inside:
                    got = ext[pl.ds(idx_s[i][slot], 1), :]
                    row = got if row is None else jnp.where(lane_set == i % 8, got, row)
                gathered[tile, pl.ds(e, 1), :] = row

        values = jnp.concatenate([gathered[tile] for tile in range(GTILES)], axis=1)
        products = dot_split(split_bf16(values), (kh_ref[...], kl_ref[...]))
        slots = first + lax.broadcasted_iota(jnp.int32, (1, BLOCK), 1)
        live = slots < count
        stiff = jnp.where(live, stiff_ref[:, pl.ds(first, BLOCK)], 0.0)
        mass = jnp.where(live, mass_ref[:, pl.ds(first, BLOCK)], 0.0)
        pair = [jnp.broadcast_to(stiff, (ROWS, BLOCK)), jnp.broadcast_to(mass, (ROWS, BLOCK))]
        coef = jnp.concatenate(pair * LANE_SETS, axis=0).T
        scaled = [products[:, t * LANES : (t + 1) * LANES] * coef for t in range(TILES)]

        names = []
        for t in range(TILES):
            rows = [
                jnp.concatenate([idx_row(j, block_id, part) for part in range(BLOCK // LANES)], axis=1)
                for j in range(LANE_SETS * t, LANE_SETS * t + LANE_SETS)
            ]
            names.append(jnp.concatenate(rows, axis=0).astype(jnp.float32).T)
        for t in range(TILES):
            total = scaled[t]
            for s in range(t):
                total = total + jnp.where(names[s] == names[t], scaled[s], 0.0)
            terms[t] = total

        @pl.loop(0, BLOCK, unroll=8)
        def _(e):
            slot = first + e
            added = [terms[t, pl.ds(e, 1), :] for t in range(TILES)]
            places = [[idx_s[LANE_SETS * t + g][slot] for t in range(TILES)] for g in range(LANE_SETS)]
            held = [[accs[g][pl.ds(places[g][t], 1), :] for t in range(TILES)] for g in range(LANE_SETS)]
            for t in range(TILES):
                for g in range(LANE_SETS):
                    accs[g][pl.ds(places[g][t], 1), :] = held[g][t] + added[t]

    quarter = lax.broadcasted_iota(jnp.int32, (LANES, LANES), 1) >> 5

    def summed(at):
        rows = accs[0][pl.ds(at, LANES), :]
        for g in range(1, LANE_SETS):
            rows = jnp.where(quarter == g, accs[g][pl.ds(at, LANES), :], rows)
        rows = rows.T
        return (rows[:32] + rows[32:64]) + (rows[64:96] + rows[96:])

    def wide(at):
        return jnp.concatenate([summed(at), summed(at + LANES)], axis=1)

    across = (((1,), (1,)), ((), ()))
    dot = functools.partial(lax.dot_general, dimension_numbers=across, preferred_element_type=jnp.float32)

    def add_gram(left, both):
        (lh, ll), (bh, bl) = split_bf16(left), split_bf16(both)
        pieces = dot(jnp.concatenate([lh, ll], axis=0), bh)
        gram[:, : 2 * ROWS] += pieces[:ROWS] + (pieces[ROWS:] + dot(lh, bl))

    step = 2 * LANES

    @pl.loop(0, face // step, unroll=2)
    def _(b):
        at = pl.multiple_of(b * step, step)
        both = wide(owned + at)
        add_gram(high_v[0, :, pl.ds(at, step)], both)
        cos2, sin2 = (jnp.concatenate([row, row], axis=1) for row in (cosine, sine))
        for op in range(2):
            real, imag = both[ROWS * op : ROWS * op + 8], both[ROWS * op + 8 : ROWS * op + ROWS]
            side_x_out[ROWS * op : ROWS * op + 8, pl.ds(at, step)] = cos2 * real + sin2 * imag
            side_x_out[ROWS * op + 8 : ROWS * op + ROWS, pl.ds(at, step)] = cos2 * imag - sin2 * real
        both = wide(owned + face + at)
        add_gram(high_v[1, :, pl.ds(at, step)], both)
        side_y_out[:, pl.ds(at, step)] = both

    side_x_put = pltpu.make_async_copy(side_x_out, side_x_hbm, in_sems.at[6])
    side_y_put = pltpu.make_async_copy(side_y_out, side_y_hbm, in_sems.at[7])
    side_x_put.start()
    side_y_put.start()
    chunk = owned // OUT_CHUNKS

    def out_copies(c):
        cols = pl.ds(c * chunk, chunk)
        return (
            pltpu.make_async_copy(images.at[pl.ds(0, ROWS), cols], curl_out.at[:, cols], out_sems.at[0, c]),
            pltpu.make_async_copy(images.at[pl.ds(ROWS, ROWS), cols], mass_out.at[:, cols], out_sems.at[1, c]),
        )

    for c in range(OUT_CHUNKS):

        @pl.loop(0, chunk // step, unroll=8)
        def _(b):
            at = pl.multiple_of(c * chunk + b * step, step)
            both = wide(at)
            add_gram(own_v[:, pl.ds(at, step)], both)
            images[:, pl.ds(at, step)] = both

        for copy in out_copies(c):
            copy.start()

    total = gram[...]
    of_real, of_imag = total[:8], total[8:]
    odd = ((lax.broadcasted_iota(jnp.int32, (8, LANES), 1) >> 3) & 1) == 1
    gram_out[...] = jnp.where(
        odd, of_real - pltpu.roll(of_imag, 8, 1), of_real + pltpu.roll(of_imag, LANES - 8, 1)
    )
    side_x_put.wait()
    side_y_put.wait()
    for c in range(OUT_CHUNKS):
        for copy in out_copies(c):
            copy.wait()


def part_images(count, phase, idx, own, high_x, high_y, stiff, mass, kh, kl):
    shape = jax.ShapeDtypeStruct
    owned, face = own.shape[1], high_x.shape[1]
    extent = owned + 2 * face
    f32 = jnp.float32
    dma = pltpu.SemaphoreType.DMA
    return pl.pallas_call(
        part_kernel,
        out_shape=(
            shape((ROWS, owned), f32),
            shape((ROWS, owned), f32),
            shape((2 * ROWS, face), f32),
            shape((2 * ROWS, face), f32),
            shape((8, LANES), f32),
        ),
        in_specs=[SMEM, ANY, ANY, ANY, ANY] + [VMEM] * 4 + [ANY] * 2,
        out_specs=(ANY, ANY, ANY, ANY, VMEM),
        scratch_shapes=[pltpu.VMEM((extent, LANES), f32)] * 5
        + [
            pltpu.VMEM((GTILES, BLOCK, LANES), f32),
            pltpu.VMEM((TILES, BLOCK, LANES), f32),
            pltpu.VMEM((ROWS, LANES), f32),
            pltpu.SMEM((idx.size,), jnp.int32),
            pltpu.VMEM((ROWS, owned), f32),
            pltpu.VMEM((2, ROWS, face), f32),
            pltpu.VMEM((2 * ROWS, owned), f32),
            pltpu.VMEM(kh.shape, kh.dtype),
            pltpu.VMEM(kl.shape, kl.dtype),
            pltpu.VMEM((2 * ROWS, face), f32),
            pltpu.VMEM((2 * ROWS, face), f32),
            dma((8,)),
            dma((2, OUT_CHUNKS)),
        ],
        compiler_params=pltpu.CompilerParams(vmem_limit_bytes=VMEM_BYTES),
        name="part_images",
    )(count, idx.reshape(-1), own, high_x, high_y, phase, idx, stiff, mass, kh, kl)


def exchange_kernel(
    side_x_hbm,
    side_y_hbm,
    curl_hbm,
    mass_hbm,
    gram_hbm,
    lows_out,
    gram_out,
    back,
    low,
    held,
    gram_ref,
    sums,
    low_sems,
    side_sems,
    send_sems,
    recv_sems,
):
    face = side_x_hbm.shape[1]
    owned = curl_hbm.shape[1]
    n_px, n_py = lax.axis_size("px"), lax.axis_size("py")
    a, b = lax.axis_index("px"), lax.axis_index("py")
    core, at_y, high = lax.rem(a, 2), lax.rem(a // 2, GROUP), a // (2 * GROUP)
    at_z, side = lax.rem(b, GROUP), b // GROUP

    def along_y(k):
        return {"px": high * (2 * GROUP) + k * 2 + core}

    def along_z(k):
        return {"py": side * GROUP + k}

    def over_rest(k):
        return {"px": (k // 4) * (2 * GROUP) + at_y * 2 + lax.rem(k, 2), "py": lax.rem(k // 2, 2) * GROUP + at_z}

    groups = ((along_y, at_y), (along_z, at_z), (over_rest, high * 4 + side * 2 + core))
    next_x, last_x = {"px": lax.rem(a + 1, n_px)}, {"px": lax.rem(a + n_px - 1, n_px)}
    next_y, last_y = {"py": lax.rem(b + 1, n_py)}, {"py": lax.rem(b + n_py - 1, n_py)}
    gram_in = pltpu.make_async_copy(gram_hbm, gram_ref, low_sems.at[3])
    gram_in.start()
    barrier = pltpu.get_barrier_semaphore()

    def greet(device):
        pl.semaphore_signal(barrier, 1, device_id=device, device_id_type=pl.DeviceIdType.MESH)

    for place, me in groups:
        for k in range(1, GROUP):
            greet(place(lax.rem(me + k, GROUP)))
    greet(next_x)
    greet(last_x)

    @pl.when(b < n_py - 1)
    def _():
        greet(next_y)

    @pl.when(b > 0)
    def _():
        greet(last_y)

    reads = [
        pltpu.make_async_copy(image.at[:, pl.ds(owned - 2 * face, 2 * face)], low.at[op], low_sems.at[op])
        for op, image in enumerate((curl_hbm, mass_hbm))
    ]
    write = pltpu.make_async_copy(low, lows_out, low_sems.at[2])
    for read in reads:
        read.start()
    gram_in.wait()
    peers = 3 * (GROUP - 1) + 2
    pl.semaphore_wait(barrier, peers + jnp.minimum(b, 1) + jnp.minimum(n_py - 1 - b, 1))

    def tile_copy(phase, source, to, at):
        return pltpu.make_async_remote_copy(
            src_ref=source,
            dst_ref=held.at[phase, at],
            send_sem=send_sems.at[phase, to],
            recv_sem=recv_sems.at[phase, at],
            device_id=groups[phase][0](to),
            device_id_type=pl.DeviceIdType.MESH,
        )

    def others(me):
        return [lax.rem(me + k, GROUP) for k in range(1, GROUP)]

    def send_all(phase, source):
        me = groups[phase][1]
        for to in others(me):
            tile_copy(phase, source, to, me).start()
        held[phase, pl.ds(me, 1)] = source[...][None]

    def sum_all(phase, source):
        me = groups[phase][1]
        for other in others(me):
            tile_copy(phase, source, other, other).wait_recv()
        total = held[phase, 0]
        for at in range(1, GROUP):
            total = total + held[phase, at]
        return total

    def side_copy(source, at, device):
        return pltpu.make_async_remote_copy(
            src_ref=source,
            dst_ref=back.at[at],
            send_sem=side_sems.at[0, at],
            recv_sem=side_sems.at[1, at],
            device_id=device,
            device_id_type=pl.DeviceIdType.MESH,
        )

    to_x = side_copy(side_x_hbm, 0, next_x)
    to_y = side_copy(side_y_hbm, 1, next_y)
    send_all(0, gram_ref)
    to_x.start()

    @pl.when(b < n_py - 1)
    def _():
        to_y.start()

    sums[0] = sum_all(0, gram_ref)
    send_all(1, sums.at[0])
    for read in reads:
        read.wait()
    sums[1] = sum_all(1, sums.at[0])
    send_all(2, sums.at[1])
    to_x.wait_recv()
    for op in range(2):
        low[op, :, :face] += back[0, ROWS * op : ROWS * op + ROWS, :]

    @pl.when(b > 0)
    def _():
        to_y.wait_recv()
        for op in range(2):
            low[op, :, face:] += back[1, ROWS * op : ROWS * op + ROWS, :]

    write.start()
    whole = sum_all(2, sums.at[1])
    for op in range(2):
        for part in range(2):
            at = 16 * op + 8 * part
            gram_out[op, part] = whole[:, at : at + 8] / float(n_px * n_py * owned)
    to_x.wait_send()

    @pl.when(b < n_py - 1)
    def _():
        to_y.wait_send()

    for phase, source in enumerate((gram_ref, sums.at[0], sums.at[1])):
        me = groups[phase][1]
        for to in others(me):
            tile_copy(phase, source, to, me).wait_send()
    write.wait()


def exchange(side_x, side_y, curl, mass, gram):
    shape = jax.ShapeDtypeStruct
    f32 = jnp.float32
    dma = pltpu.SemaphoreType.DMA
    face = side_x.shape[1]
    return pl.pallas_call(
        exchange_kernel,
        out_shape=(shape((2, ROWS, 2 * face), f32), shape((2, 2, 8, 8), f32)),
        in_specs=[ANY] * 5,
        out_specs=(ANY, VMEM),
        scratch_shapes=[
            pltpu.VMEM((2, 2 * ROWS, face), f32),
            pltpu.VMEM((2, ROWS, 2 * face), f32),
            pltpu.VMEM((3, GROUP, 8, LANES), f32),
            pltpu.VMEM((8, LANES), f32),
            pltpu.VMEM((2, 8, LANES), f32),
            dma((4,)),
            dma((2, 2)),
            dma((3, GROUP)),
            dma((3, GROUP)),
        ],
        compiler_params=pltpu.CompilerParams(
            collective_id=0, has_side_effects=True, vmem_limit_bytes=VMEM_BYTES
        ),
        name="exchange",
    )(side_x, side_y, curl, mass, gram)


def finish_kernel(curl_in, mass_in, lows, gram_ref, curl_out, mass_out, gram_out, sems):
    width = lows.shape[2]
    writes = [
        pltpu.make_async_copy(lows.at[op], image.at[:, pl.ds(image.shape[1] - width, width)], sems.at[op])
        for op, image in enumerate((curl_out, mass_out))
    ]
    for write in writes:
        write.start()
    gram_out[...] = gram_ref[...]
    for write in writes:
        write.wait()


def finish(curl, mass, lows, gram):
    shape = jax.ShapeDtypeStruct
    return pl.pallas_call(
        finish_kernel,
        out_shape=tuple(shape(value.shape, jnp.float32) for value in (curl, mass, gram)),
        in_specs=[ANY, ANY, VMEM, VMEM],
        out_specs=(ANY, ANY, VMEM),
        scratch_shapes=[pltpu.SemaphoreType.DMA((2,))],
        input_output_aliases={0: 0, 1: 1},
        compiler_params=pltpu.CompilerParams(vmem_limit_bytes=VMEM_BYTES),
        name="finish",
    )(curl, mass, lows, gram)


def on_device(
    trial_block,
    stiff_coef,
    mass_coef,
    elem_count,
    elem_dofs,
    pairing,
    bloch_fraction,
    stiff_mat,
    mass_mat,
):
    owned = trial_block.shape[-1]
    own = trial_block.reshape(ROWS, owned)
    high_x, high_y, phase, idx, kh, kl = begin(
        bloch_fraction,
        own,
        elem_dofs[0].transpose(2, 0, 1),
        pairing.reshape(-1, LANES),
        stiff_mat,
        mass_mat,
    )
    curl, mass, side_x, side_y, gram = part_images(
        elem_count, phase, idx, own, high_x, high_y, stiff_coef[0], mass_coef[0], kh, kl
    )
    lows, gram = exchange(side_x, side_y, curl, mass, gram)
    curl, mass, gram = finish(curl, mass, lows, gram)
    return curl.reshape(trial_block.shape), mass.reshape(trial_block.shape), gram


def solution(mesh):
    return jax.shard_map(
        on_device,
        mesh=mesh,
        in_specs=(
            P("px", "py", None, None, None),
            P("px", "py", None),
            P("px", "py", None),
            P("px", "py"),
            P("px", "py", None, None),
            P(),
            P(),
            P(),
            P(),
        ),
        out_specs=(P("px", "py", None, None, None), P("px", "py", None, None, None), P()),
        check_vma=False,
    )
```

```python
import functools
import math

import jax
import jax.numpy as jnp
from jax import lax
from jax.experimental import pallas as pl
from jax.experimental.pallas import tpu as pltpu
from jax.sharding import PartitionSpec as P

HIGH = lax.Precision.HIGHEST
LANES = 128
ROWS = 16
NLOC = 20
HALO_SLOTS = 128
BLOCK = 512
TILES = 5
GTILES = 3
LANE_SETS = 4

VMEM = pl.BlockSpec(memory_space=pltpu.VMEM)
SMEM = pl.BlockSpec(memory_space=pltpu.SMEM)
ANY = pl.BlockSpec(memory_space=pl.ANY)
VMEM_BYTES = 56 * 2**20
OUT_CHUNKS = 2
GROUP = 8


def split_bf16(value):
    high = value.astype(jnp.bfloat16)
    low = (value - high.astype(jnp.float32)).astype(jnp.bfloat16)
    return high, low


def dot_split(a, b):
    (ah, al), (bh, bl) = a, b
    dot = functools.partial(jnp.dot, preferred_element_type=jnp.float32)
    both = dot(jnp.concatenate([ah, al], axis=0), bh)
    rows = ah.shape[0]
    return both[:rows] + (both[rows:] + dot(ah, bl))


def begin_kernel(
    fraction_ref,
    own_hbm,
    dofs_ref,
    pairing_ref,
    stiff_ref,
    mass_ref,
    high_x,
    high_y,
    phase_out,
    idx_out,
    kh_out,
    kl_out,
    zeros,
    sems,
):
    face = pairing_ref.shape[0] * LANES
    owned = own_hbm.shape[1]
    n_px, n_py = lax.axis_size("px"), lax.axis_size("py")
    a, b = lax.axis_index("px"), lax.axis_index("py")
    below_x, above_x = lax.rem(a + n_px - 1, n_px), lax.rem(a + 1, n_px)
    below_y, above_y = lax.rem(b + n_py - 1, n_py), lax.rem(b + 1, n_py)

    barrier = pltpu.get_barrier_semaphore()

    def greet(axis, to):
        pl.semaphore_signal(barrier, 1, device_id={axis: to}, device_id_type=pl.DeviceIdType.MESH)

    greet("px", below_x)
    greet("px", above_x)

    @pl.when(b > 0)
    def _():
        greet("py", below_y)

    @pl.when(b < n_py - 1)
    def _():
        greet("py", above_y)

    pl.semaphore_wait(barrier, 2 + jnp.minimum(b, 1) + jnp.minimum(n_py - 1 - b, 1))

    def face_copy(first, target, at, axis, to):
        return pltpu.make_async_remote_copy(
            src_ref=own_hbm.at[:, pl.ds(first, face)],
            dst_ref=target,
            send_sem=sems.at[2 * at],
            recv_sem=sems.at[2 * at + 1],
            device_id={axis: to},
            device_id_type=pl.DeviceIdType.MESH,
        )

    to_x = face_copy(owned - 2 * face, high_x, 0, "px", below_x)
    to_y = face_copy(owned - face, high_y, 1, "py", below_y)
    no_y = pltpu.make_async_copy(zeros, high_y, sems.at[4])
    to_x.start()

    @pl.when(b > 0)
    def _():
        to_y.start()

    @pl.when(b == n_py - 1)
    def _():
        zeros[...] = jnp.zeros_like(zeros)
        no_y.start()

    at_end = jnp.broadcast_to(a, (1, LANES)) == n_px - 1
    above = jnp.broadcast_to(fraction_ref[0], (1, LANES)).astype(jnp.float32)
    below = jnp.broadcast_to(fraction_ref[1], (1, LANES)).astype(jnp.float32)
    angle = 2.0 * math.pi * above / below
    phase_out[0:1, :] = jnp.where(at_end, jnp.cos(angle), 1.0)
    phase_out[1:2, :] = jnp.where(at_end, jnp.sin(angle), 0.0)

    blocks = idx_out.shape[0] // NLOC
    for j in range(NLOC):
        for block in range(blocks):
            row = j * blocks + block
            idx_out[row : row + 1, :] = dofs_ref[j, :, block * LANES : (block + 1) * LANES]
    heads = pl.ds(0, NLOC, stride=blocks)
    head = idx_out[heads, :]
    spot = head - owned
    local = spot & (LANES - 1)
    found = jnp.zeros_like(head)
    for row in range(pairing_ref.shape[0]):
        values = jnp.broadcast_to(pairing_ref[row : row + 1, :], head.shape)
        here = jnp.take_along_axis(values, local, axis=1)
        found = jnp.where((spot >> 7) == row, here + owned, found)
    wraps = (spot >= 0) & (spot < face) & (jnp.broadcast_to(a, head.shape) == n_px - 1)
    idx_out[heads, :] = jnp.where(wraps, found, head)

    grow = lax.broadcasted_iota(jnp.int32, (GTILES * LANES, NLOC), 0)
    gcol = lax.broadcasted_iota(jnp.int32, (GTILES * LANES, NLOC), 1)
    spread_i = ((grow >> 4) == gcol).astype(jnp.float32)
    trow = lax.broadcasted_iota(jnp.int32, (NLOC, TILES * LANES), 0)
    tcol = lax.broadcasted_iota(jnp.int32, (NLOC, TILES * LANES), 1)
    spread_j = ((tcol >> 5) == trow).astype(jnp.float32)
    dot = functools.partial(jnp.dot, precision=HIGH, preferred_element_type=jnp.float32)
    stiff = dot(dot(spread_i, stiff_ref[...].T), spread_j)
    mass = dot(dot(spread_i, mass_ref[...].T), spread_j)
    krow = lax.broadcasted_iota(jnp.int32, (GTILES * LANES, TILES * LANES), 0)
    kcol = lax.broadcasted_iota(jnp.int32, (GTILES * LANES, TILES * LANES), 1)
    both = jnp.where(((kcol >> 4) & 1) == 0, stiff, mass)
    both = jnp.where((krow & 15) == (kcol & 15), both, 0.0)
    kh_out[...], kl_out[...] = split_bf16(both)

    to_x.wait()

    @pl.when(b > 0)
    def _():
        to_y.wait_send()

    @pl.when(b < n_py - 1)
    def _():
        to_y.wait_recv()

    @pl.when(b == n_py - 1)
    def _():
        no_y.wait()


def begin(fraction, own, dofs, pairing, stiff_mat, mass_mat):
    shape = jax.ShapeDtypeStruct
    high = shape((ROWS, pairing.size), jnp.float32)
    spread = shape((GTILES * LANES, TILES * LANES), jnp.bfloat16)
    return pl.pallas_call(
        begin_kernel,
        out_shape=(high, high, shape((2, LANES), jnp.float32), shape((dofs.size // LANES, LANES), jnp.int32), spread, spread),
        in_specs=[SMEM, ANY, VMEM, VMEM, VMEM, VMEM],
        out_specs=(ANY, ANY, VMEM, VMEM, VMEM, VMEM),
        scratch_shapes=[
            pltpu.VMEM(high.shape, jnp.float32),
            pltpu.SemaphoreType.DMA((5,)),
        ],
        compiler_params=pltpu.CompilerParams(
            collective_id=1, has_side_effects=True, vmem_limit_bytes=VMEM_BYTES
        ),
        name="begin",
    )(fraction, own, dofs, pairing, stiff_mat, mass_mat)


def part_kernel(
    count_ref,
    idx_hbm,
    own_hbm,
    high_x_hbm,
    high_y_hbm,
    phase_ref,
    idx_v,
    stiff_ref,
    mass_ref,
    kh_hbm,
    kl_hbm,
    curl_out,
    mass_out,
    side_x_hbm,
    side_y_hbm,
    gram_out,
    ext,
    acc0,
    acc1,
    acc2,
    acc3,
    gathered,
    terms,
    gram,
    idx_all,
    own_v,
    high_v,
    images,
    kh_ref,
    kl_ref,
    side_x_out,
    side_y_out,
    in_sems,
    out_sems,
):
    accs = (acc0, acc1, acc2, acc3)
    owned = own_v.shape[1]
    face = high_v.shape[2]
    cosine, sine = phase_ref[0:1, :], phase_ref[1:2, :]
    count = count_ref[0, 0]
    capacity = stiff_ref.shape[1]
    idx_s = [idx_all.at[pl.ds(j * capacity, capacity)] for j in range(NLOC)]

    own_in = pltpu.make_async_copy(own_hbm, own_v, in_sems.at[0])
    high_x_in = pltpu.make_async_copy(high_x_hbm, high_v.at[0], in_sems.at[1])
    high_y_in = pltpu.make_async_copy(high_y_hbm, high_v.at[1], in_sems.at[2])
    idx_in = pltpu.make_async_copy(idx_hbm, idx_all, in_sems.at[3])
    own_in.start()
    idx_in.start()
    high_x_in.start()
    high_y_in.start()
    kh_in = pltpu.make_async_copy(kh_hbm, kh_ref, in_sems.at[4])
    kl_in = pltpu.make_async_copy(kl_hbm, kl_ref, in_sems.at[5])
    kh_in.start()
    kl_in.start()

    zero_rows = jnp.zeros((LANES, LANES), jnp.float32)

    @pl.loop(0, ext.shape[0] // LANES, unroll=4)
    def _(b):
        at = pl.multiple_of(b * LANES, LANES)
        for acc in accs:
            acc[pl.ds(at, LANES), :] = zero_rows

    gram[...] = jnp.zeros_like(gram)

    def put_rows(at, block):
        ext[pl.ds(at, LANES), :] = jnp.concatenate([block] * (LANES // ROWS), axis=0).T

    own_in.wait()

    @pl.loop(0, owned // LANES, unroll=16)
    def _(b):
        at = pl.multiple_of(b * LANES, LANES)
        put_rows(at, own_v[:, pl.ds(at, LANES)])

    high_x_in.wait()
    high_y_in.wait()

    @pl.loop(0, face // LANES, unroll=8)
    def _(b):
        at = pl.multiple_of(b * LANES, LANES)
        got = high_v[0, :, pl.ds(at, LANES)]
        real, imag = got[: ROWS // 2], got[ROWS // 2 :]
        turned = jnp.concatenate([cosine * real - sine * imag, sine * real + cosine * imag], axis=0)
        high_v[0, :, pl.ds(at, LANES)] = turned
        put_rows(owned + at, turned)
        put_rows(owned + face + at, high_v[1, :, pl.ds(at, LANES)])

    def idx_row(j, block_id, part):
        row = j * (capacity // LANES) + block_id * (BLOCK // LANES) + part
        return jnp.broadcast_to(idx_v[pl.ds(row, 1), :], (LANES // LANE_SETS, LANES))

    lane_set = lax.broadcasted_iota(jnp.int32, (1, LANES), 1) >> 4
    idx_in.wait()
    kh_in.wait()
    kl_in.wait()

    @pl.loop(0, (count + BLOCK - 1) // BLOCK)
    def _(block_id):
        first = pl.multiple_of(block_id * BLOCK, BLOCK)

        @pl.loop(0, BLOCK, unroll=4)
        def _(e):
            slot = first + e
            for tile in range(GTILES):
                inside = range(8 * tile, min(8 * tile + 8, NLOC))
                row = None
                for i in inside:
                    got = ext[pl.ds(idx_s[i][slot], 1), :]
                    row = got if row is None else jnp.where(lane_set == i % 8, got, row)
                gathered[tile, pl.ds(e, 1), :] = row

        values = jnp.concatenate([gathered[tile] for tile in range(GTILES)], axis=1)
        products = dot_split(split_bf16(values), (kh_ref[...], kl_ref[...]))
        slots = first + lax.broadcasted_iota(jnp.int32, (1, BLOCK), 1)
        live = slots < count
        stiff = jnp.where(live, stiff_ref[:, pl.ds(first, BLOCK)], 0.0)
        mass = jnp.where(live, mass_ref[:, pl.ds(first, BLOCK)], 0.0)
        pair = [jnp.broadcast_to(stiff, (ROWS, BLOCK)), jnp.broadcast_to(mass, (ROWS, BLOCK))]
        coef = jnp.concatenate(pair * LANE_SETS, axis=0).T
        scaled = [products[:, t * LANES : (t + 1) * LANES] * coef for t in range(TILES)]

        names = []
        for t in range(TILES):
            rows = [
                jnp.concatenate([idx_row(j, block_id, part) for part in range(BLOCK // LANES)], axis=1)
                for j in range(LANE_SETS * t, LANE_SETS * t + LANE_SETS)
            ]
            names.append(jnp.concatenate(rows, axis=0).astype(jnp.float32).T)
        for t in range(TILES):
            total = scaled[t]
            for s in range(t):
                total = total + jnp.where(names[s] == names[t], scaled[s], 0.0)
            terms[t] = total

        @pl.loop(0, BLOCK, unroll=16)
        def _(e):
            slot = first + e
            added = [terms[t, pl.ds(e, 1), :] for t in range(TILES)]
            places = [[idx_s[LANE_SETS * t + g][slot] for t in range(TILES)] for g in range(LANE_SETS)]
            held = [[accs[g][pl.ds(places[g][t], 1), :] for t in range(TILES)] for g in range(LANE_SETS)]
            for t in range(TILES):
                for g in range(LANE_SETS):
                    accs[g][pl.ds(places[g][t], 1), :] = held[g][t] + added[t]

    quarter = lax.broadcasted_iota(jnp.int32, (LANES, LANES), 1) >> 5

    def summed(at):
        rows = accs[0][pl.ds(at, LANES), :]
        for g in range(1, LANE_SETS):
            rows = jnp.where(quarter == g, accs[g][pl.ds(at, LANES), :], rows)
        rows = rows.T
        return (rows[:32] + rows[32:64]) + (rows[64:96] + rows[96:])

    def wide(at):
        return jnp.concatenate([summed(at), summed(at + LANES)], axis=1)

    across = (((1,), (1,)), ((), ()))
    dot = functools.partial(lax.dot_general, dimension_numbers=across, preferred_element_type=jnp.float32)

    def add_gram(left, both):
        (lh, ll), (bh, bl) = split_bf16(left), split_bf16(both)
        pieces = dot(jnp.concatenate([lh, ll], axis=0), bh)
        gram[:, : 2 * ROWS] += pieces[:ROWS] + (pieces[ROWS:] + dot(lh, bl))

    step = 2 * LANES

    @pl.loop(0, face // step, unroll=4)
    def _(b):
        at = pl.multiple_of(b * step, step)
        both = wide(owned + at)
        add_gram(high_v[0, :, pl.ds(at, step)], both)
        cos2, sin2 = (jnp.concatenate([row, row], axis=1) for row in (cosine, sine))
        for op in range(2):
            real, imag = both[ROWS * op : ROWS * op + 8], both[ROWS * op + 8 : ROWS * op + ROWS]
            side_x_out[ROWS * op : ROWS * op + 8, pl.ds(at, step)] = cos2 * real + sin2 * imag
            side_x_out[ROWS * op + 8 : ROWS * op + ROWS, pl.ds(at, step)] = cos2 * imag - sin2 * real
        both = wide(owned + face + at)
        add_gram(high_v[1, :, pl.ds(at, step)], both)
        side_y_out[:, pl.ds(at, step)] = both

    side_x_put = pltpu.make_async_copy(side_x_out, side_x_hbm, in_sems.at[6])
    side_y_put = pltpu.make_async_copy(side_y_out, side_y_hbm, in_sems.at[7])
    side_x_put.start()
    side_y_put.start()
    chunk = owned // OUT_CHUNKS

    def out_copies(c):
        cols = pl.ds(c * chunk, chunk)
        return (
            pltpu.make_async_copy(images.at[pl.ds(0, ROWS), cols], curl_out.at[:, cols], out_sems.at[0, c]),
            pltpu.make_async_copy(images.at[pl.ds(ROWS, ROWS), cols], mass_out.at[:, cols], out_sems.at[1, c]),
        )

    for c in range(OUT_CHUNKS):

        @pl.loop(0, chunk // step, unroll=16)
        def _(b):
            at = pl.multiple_of(c * chunk + b * step, step)
            both = wide(at)
            add_gram(own_v[:, pl.ds(at, step)], both)
            images[:, pl.ds(at, step)] = both

        for copy in out_copies(c):
            copy.start()

    total = gram[...]
    of_real, of_imag = total[:8], total[8:]
    odd = ((lax.broadcasted_iota(jnp.int32, (8, LANES), 1) >> 3) & 1) == 1
    gram_out[...] = jnp.where(
        odd, of_real - pltpu.roll(of_imag, 8, 1), of_real + pltpu.roll(of_imag, LANES - 8, 1)
    )
    side_x_put.wait()
    side_y_put.wait()
    for c in range(OUT_CHUNKS):
        for copy in out_copies(c):
            copy.wait()


def part_images(count, phase, idx, own, high_x, high_y, stiff, mass, kh, kl):
    shape = jax.ShapeDtypeStruct
    owned, face = own.shape[1], high_x.shape[1]
    extent = owned + 2 * face
    f32 = jnp.float32
    dma = pltpu.SemaphoreType.DMA
    return pl.pallas_call(
        part_kernel,
        out_shape=(
            shape((ROWS, owned), f32),
            shape((ROWS, owned), f32),
            shape((2 * ROWS, face), f32),
            shape((2 * ROWS, face), f32),
            shape((8, LANES), f32),
        ),
        in_specs=[SMEM, ANY, ANY, ANY, ANY] + [VMEM] * 4 + [ANY] * 2,
        out_specs=(ANY, ANY, ANY, ANY, VMEM),
        scratch_shapes=[pltpu.VMEM((extent, LANES), f32)] * 5
        + [
            pltpu.VMEM((GTILES, BLOCK, LANES), f32),
            pltpu.VMEM((TILES, BLOCK, LANES), f32),
            pltpu.VMEM((ROWS, LANES), f32),
            pltpu.SMEM((idx.size,), jnp.int32),
            pltpu.VMEM((ROWS, owned), f32),
            pltpu.VMEM((2, ROWS, face), f32),
            pltpu.VMEM((2 * ROWS, owned), f32),
            pltpu.VMEM(kh.shape, kh.dtype),
            pltpu.VMEM(kl.shape, kl.dtype),
            pltpu.VMEM((2 * ROWS, face), f32),
            pltpu.VMEM((2 * ROWS, face), f32),
            dma((8,)),
            dma((2, OUT_CHUNKS)),
        ],
        compiler_params=pltpu.CompilerParams(vmem_limit_bytes=VMEM_BYTES),
        name="part_images",
    )(count, idx.reshape(-1), own, high_x, high_y, phase, idx, stiff, mass, kh, kl)


def exchange_kernel(
    side_x_hbm,
    side_y_hbm,
    curl_hbm,
    mass_hbm,
    gram_hbm,
    lows_out,
    gram_out,
    back,
    low,
    held,
    gram_ref,
    sums,
    low_sems,
    side_sems,
    send_sems,
    recv_sems,
):
    face = side_x_hbm.shape[1]
    owned = curl_hbm.shape[1]
    n_px, n_py = lax.axis_size("px"), lax.axis_size("py")
    a, b = lax.axis_index("px"), lax.axis_index("py")
    core, at_y, high = lax.rem(a, 2), lax.rem(a // 2, GROUP), a // (2 * GROUP)
    at_z, side = lax.rem(b, GROUP), b // GROUP

    def along_y(k):
        return {"px": high * (2 * GROUP) + k * 2 + core}

    def along_z(k):
        return {"py": side * GROUP + k}

    def over_rest(k):
        return {"px": (k // 4) * (2 * GROUP) + at_y * 2 + lax.rem(k, 2), "py": lax.rem(k // 2, 2) * GROUP + at_z}

    groups = ((over_rest, high * 4 + side * 2 + core), (along_y, at_y), (along_z, at_z))
    next_x, last_x = {"px": lax.rem(a + 1, n_px)}, {"px": lax.rem(a + n_px - 1, n_px)}
    next_y, last_y = {"py": lax.rem(b + 1, n_py)}, {"py": lax.rem(b + n_py - 1, n_py)}
    gram_in = pltpu.make_async_copy(gram_hbm, gram_ref, low_sems.at[3])
    gram_in.start()
    barrier = pltpu.get_barrier_semaphore()

    def greet(device):
        pl.semaphore_signal(barrier, 1, device_id=device, device_id_type=pl.DeviceIdType.MESH)

    for place, me in groups:
        for k in range(1, GROUP):
            greet(place(lax.rem(me + k, GROUP)))
    greet(next_x)
    greet(last_x)

    @pl.when(b < n_py - 1)
    def _():
        greet(next_y)

    @pl.when(b > 0)
    def _():
        greet(last_y)

    reads = [
        pltpu.make_async_copy(image.at[:, pl.ds(owned - 2 * face, 2 * face)], low.at[op], low_sems.at[op])
        for op, image in enumerate((curl_hbm, mass_hbm))
    ]
    write = pltpu.make_async_copy(low, lows_out, low_sems.at[2])
    for read in reads:
        read.start()
    gram_in.wait()
    peers = 3 * (GROUP - 1) + 2
    pl.semaphore_wait(barrier, peers + jnp.minimum(b, 1) + jnp.minimum(n_py - 1 - b, 1))

    def tile_copy(phase, source, to, at):
        return pltpu.make_async_remote_copy(
            src_ref=source,
            dst_ref=held.at[phase, at],
            send_sem=send_sems.at[phase, to],
            recv_sem=recv_sems.at[phase, at],
            device_id=groups[phase][0](to),
            device_id_type=pl.DeviceIdType.MESH,
        )

    def others(me):
        return [lax.rem(me + k, GROUP) for k in range(1, GROUP)]

    def send_all(phase, source):
        me = groups[phase][1]
        for to in others(me):
            tile_copy(phase, source, to, me).start()
        held[phase, pl.ds(me, 1)] = source[...][None]

    def sum_all(phase, source):
        me = groups[phase][1]
        for other in others(me):
            tile_copy(phase, source, other, other).wait_recv()
        total = held[phase, 0]
        for at in range(1, GROUP):
            total = total + held[phase, at]
        return total

    def side_copy(source, at, device):
        return pltpu.make_async_remote_copy(
            src_ref=source,
            dst_ref=back.at[at],
            send_sem=side_sems.at[0, at],
            recv_sem=side_sems.at[1, at],
            device_id=device,
            device_id_type=pl.DeviceIdType.MESH,
        )

    to_x = side_copy(side_x_hbm, 0, next_x)
    to_y = side_copy(side_y_hbm, 1, next_y)
    send_all(0, gram_ref)
    to_x.start()

    @pl.when(b < n_py - 1)
    def _():
        to_y.start()

    sums[0] = sum_all(0, gram_ref)
    send_all(1, sums.at[0])
    for read in reads:
        read.wait()
    sums[1] = sum_all(1, sums.at[0])
    send_all(2, sums.at[1])
    to_x.wait_recv()
    for op in range(2):
        low[op, :, :face] += back[0, ROWS * op : ROWS * op + ROWS, :]

    @pl.when(b > 0)
    def _():
        to_y.wait_recv()
        for op in range(2):
            low[op, :, face:] += back[1, ROWS * op : ROWS * op + ROWS, :]

    write.start()
    whole = sum_all(2, sums.at[1])
    for op in range(2):
        for part in range(2):
            at = 16 * op + 8 * part
            gram_out[op, part] = whole[:, at : at + 8] / float(n_px * n_py * owned)
    to_x.wait_send()

    @pl.when(b < n_py - 1)
    def _():
        to_y.wait_send()

    for phase, source in enumerate((gram_ref, sums.at[0], sums.at[1])):
        me = groups[phase][1]
        for to in others(me):
            tile_copy(phase, source, to, me).wait_send()
    write.wait()


def exchange(side_x, side_y, curl, mass, gram):
    shape = jax.ShapeDtypeStruct
    f32 = jnp.float32
    dma = pltpu.SemaphoreType.DMA
    face = side_x.shape[1]
    return pl.pallas_call(
        exchange_kernel,
        out_shape=(shape((2, ROWS, 2 * face), f32), shape((2, 2, 8, 8), f32)),
        in_specs=[ANY] * 5,
        out_specs=(ANY, VMEM),
        scratch_shapes=[
            pltpu.VMEM((2, 2 * ROWS, face), f32),
            pltpu.VMEM((2, ROWS, 2 * face), f32),
            pltpu.VMEM((3, GROUP, 8, LANES), f32),
            pltpu.VMEM((8, LANES), f32),
            pltpu.VMEM((2, 8, LANES), f32),
            dma((4,)),
            dma((2, 2)),
            dma((3, GROUP)),
            dma((3, GROUP)),
        ],
        compiler_params=pltpu.CompilerParams(
            collective_id=0, has_side_effects=True, vmem_limit_bytes=VMEM_BYTES
        ),
        name="exchange",
    )(side_x, side_y, curl, mass, gram)


def finish_kernel(curl_in, mass_in, lows_hbm, gram_ref, curl_out, mass_out, gram_out, lows, sems):
    width = lows.shape[2]
    reads = [pltpu.make_async_copy(lows_hbm.at[op], lows.at[op], sems.at[0, op]) for op in range(2)]
    writes = [
        pltpu.make_async_copy(lows.at[op], image.at[:, pl.ds(image.shape[1] - width, width)], sems.at[1, op])
        for op, image in enumerate((curl_out, mass_out))
    ]
    for read in reads:
        read.start()
    gram_out[...] = gram_ref[...]
    for read, write in zip(reads, writes):
        read.wait()
        write.start()
    for write in writes:
        write.wait()


def finish(curl, mass, lows, gram):
    shape = jax.ShapeDtypeStruct
    return pl.pallas_call(
        finish_kernel,
        out_shape=tuple(shape(value.shape, jnp.float32) for value in (curl, mass, gram)),
        in_specs=[ANY, ANY, ANY, VMEM],
        out_specs=(ANY, ANY, VMEM),
        scratch_shapes=[pltpu.VMEM(lows.shape, jnp.float32), pltpu.SemaphoreType.DMA((2, 2))],
        input_output_aliases={0: 0, 1: 1},
        compiler_params=pltpu.CompilerParams(vmem_limit_bytes=VMEM_BYTES),
        name="finish",
    )(curl, mass, lows, gram)


def on_device(
    trial_block,
    stiff_coef,
    mass_coef,
    elem_count,
    elem_dofs,
    pairing,
    bloch_fraction,
    stiff_mat,
    mass_mat,
):
    owned = trial_block.shape[-1]
    own = trial_block.reshape(ROWS, owned)
    high_x, high_y, phase, idx, kh, kl = begin(
        bloch_fraction,
        own,
        elem_dofs[0].transpose(2, 0, 1),
        pairing.reshape(-1, LANES),
        stiff_mat,
        mass_mat,
    )
    curl, mass, side_x, side_y, gram = part_images(
        elem_count, phase, idx, own, high_x, high_y, stiff_coef[0], mass_coef[0], kh, kl
    )
    lows, gram = exchange(side_x, side_y, curl, mass, gram)
    curl, mass, gram = finish(curl, mass, lows, gram)
    return curl.reshape(trial_block.shape), mass.reshape(trial_block.shape), gram


def solution(mesh):
    return jax.shard_map(
        on_device,
        mesh=mesh,
        in_specs=(
            P("px", "py", None, None, None),
            P("px", "py", None),
            P("px", "py", None),
            P("px", "py"),
            P("px", "py", None, None),
            P(),
            P(),
            P(),
            P(),
        ),
        out_specs=(P("px", "py", None, None, None), P("px", "py", None, None, None), P()),
        check_vma=False,
    )
```

```python
import functools
import math

import jax
import jax.numpy as jnp
from jax import lax
from jax.experimental import pallas as pl
from jax.experimental.pallas import tpu as pltpu
from jax.sharding import PartitionSpec as P

HIGH = lax.Precision.HIGHEST
LANES = 128
ROWS = 16
NLOC = 20
HALO_SLOTS = 128
BLOCK = 512
TILES = 5
GTILES = 3
LANE_SETS = 4

VMEM = pl.BlockSpec(memory_space=pltpu.VMEM)
SMEM = pl.BlockSpec(memory_space=pltpu.SMEM)
ANY = pl.BlockSpec(memory_space=pl.ANY)
VMEM_BYTES = 56 * 2**20
OUT_CHUNKS = 2
GROUP = 8


def split_bf16(value):
    high = value.astype(jnp.bfloat16)
    low = (value - high.astype(jnp.float32)).astype(jnp.bfloat16)
    return high, low


def dot_split(a, b):
    (ah, al), (bh, bl) = a, b
    dot = functools.partial(jnp.dot, preferred_element_type=jnp.float32)
    both = dot(jnp.concatenate([ah, al], axis=0), bh)
    rows = ah.shape[0]
    return both[:rows] + (both[rows:] + dot(ah, bl))


def begin_kernel(
    fraction_ref,
    own_hbm,
    dofs_ref,
    pairing_ref,
    stiff_ref,
    mass_ref,
    high_x,
    high_y,
    phase_out,
    idx_out,
    kh_out,
    kl_out,
    zeros,
    sems,
):
    face = pairing_ref.shape[0] * LANES
    owned = own_hbm.shape[1]
    n_px, n_py = lax.axis_size("px"), lax.axis_size("py")
    a, b = lax.axis_index("px"), lax.axis_index("py")
    below_x, above_x = lax.rem(a + n_px - 1, n_px), lax.rem(a + 1, n_px)
    below_y, above_y = lax.rem(b + n_py - 1, n_py), lax.rem(b + 1, n_py)

    barrier = pltpu.get_barrier_semaphore()

    def greet(axis, to):
        pl.semaphore_signal(barrier, 1, device_id={axis: to}, device_id_type=pl.DeviceIdType.MESH)

    greet("px", below_x)
    greet("px", above_x)

    @pl.when(b > 0)
    def _():
        greet("py", below_y)

    @pl.when(b < n_py - 1)
    def _():
        greet("py", above_y)

    pl.semaphore_wait(barrier, 2 + jnp.minimum(b, 1) + jnp.minimum(n_py - 1 - b, 1))

    def face_copy(first, target, at, axis, to):
        return pltpu.make_async_remote_copy(
            src_ref=own_hbm.at[:, pl.ds(first, face)],
            dst_ref=target,
            send_sem=sems.at[2 * at],
            recv_sem=sems.at[2 * at + 1],
            device_id={axis: to},
            device_id_type=pl.DeviceIdType.MESH,
        )

    to_x = face_copy(owned - 2 * face, high_x, 0, "px", below_x)
    to_y = face_copy(owned - face, high_y, 1, "py", below_y)
    no_y = pltpu.make_async_copy(zeros, high_y, sems.at[4])
    to_x.start()

    @pl.when(b > 0)
    def _():
        to_y.start()

    @pl.when(b == n_py - 1)
    def _():
        zeros[...] = jnp.zeros_like(zeros)
        no_y.start()

    at_end = jnp.broadcast_to(a, (1, LANES)) == n_px - 1
    above = jnp.broadcast_to(fraction_ref[0], (1, LANES)).astype(jnp.float32)
    below = jnp.broadcast_to(fraction_ref[1], (1, LANES)).astype(jnp.float32)
    angle = 2.0 * math.pi * above / below
    phase_out[0:1, :] = jnp.where(at_end, jnp.cos(angle), 1.0)
    phase_out[1:2, :] = jnp.where(at_end, jnp.sin(angle), 0.0)

    blocks = idx_out.shape[0] // NLOC
    for j in range(NLOC):
        for block in range(blocks):
            row = j * blocks + block
            idx_out[row : row + 1, :] = dofs_ref[j, :, block * LANES : (block + 1) * LANES]
    heads = pl.ds(0, NLOC, stride=blocks)
    head = idx_out[heads, :]
    spot = head - owned
    local = spot & (LANES - 1)
    found = jnp.zeros_like(head)
    for row in range(pairing_ref.shape[0]):
        values = jnp.broadcast_to(pairing_ref[row : row + 1, :], head.shape)
        here = jnp.take_along_axis(values, local, axis=1)
        found = jnp.where((spot >> 7) == row, here + owned, found)
    wraps = (spot >= 0) & (spot < face) & (jnp.broadcast_to(a, head.shape) == n_px - 1)
    idx_out[heads, :] = jnp.where(wraps, found, head)

    grow = lax.broadcasted_iota(jnp.int32, (GTILES * LANES, NLOC), 0)
    gcol = lax.broadcasted_iota(jnp.int32, (GTILES * LANES, NLOC), 1)
    spread_i = ((grow >> 4) == gcol).astype(jnp.float32)
    trow = lax.broadcasted_iota(jnp.int32, (NLOC, TILES * LANES), 0)
    tcol = lax.broadcasted_iota(jnp.int32, (NLOC, TILES * LANES), 1)
    spread_j = ((tcol >> 5) == trow).astype(jnp.float32)
    dot = functools.partial(jnp.dot, precision=HIGH, preferred_element_type=jnp.float32)
    stiff = dot(dot(spread_i, stiff_ref[...].T), spread_j)
    mass = dot(dot(spread_i, mass_ref[...].T), spread_j)
    krow = lax.broadcasted_iota(jnp.int32, (GTILES * LANES, TILES * LANES), 0)
    kcol = lax.broadcasted_iota(jnp.int32, (GTILES * LANES, TILES * LANES), 1)
    both = jnp.where(((kcol >> 4) & 1) == 0, stiff, mass)
    both = jnp.where((krow & 15) == (kcol & 15), both, 0.0)
    kh_out[...], kl_out[...] = split_bf16(both)

    to_x.wait()

    @pl.when(b > 0)
    def _():
        to_y.wait_send()

    @pl.when(b < n_py - 1)
    def _():
        to_y.wait_recv()

    @pl.when(b == n_py - 1)
    def _():
        no_y.wait()


def begin(fraction, own, dofs, pairing, stiff_mat, mass_mat):
    shape = jax.ShapeDtypeStruct
    high = shape((ROWS, pairing.size), jnp.float32)
    spread = shape((GTILES * LANES, TILES * LANES), jnp.bfloat16)
    return pl.pallas_call(
        begin_kernel,
        out_shape=(high, high, shape((2, LANES), jnp.float32), shape((dofs.size // LANES, LANES), jnp.int32), spread, spread),
        in_specs=[SMEM, ANY, VMEM, VMEM, VMEM, VMEM],
        out_specs=(ANY, ANY, VMEM, VMEM, VMEM, VMEM),
        scratch_shapes=[
            pltpu.VMEM(high.shape, jnp.float32),
            pltpu.SemaphoreType.DMA((5,)),
        ],
        compiler_params=pltpu.CompilerParams(
            collective_id=1, has_side_effects=True, vmem_limit_bytes=VMEM_BYTES
        ),
        name="begin",
    )(fraction, own, dofs, pairing, stiff_mat, mass_mat)


def part_kernel(
    count_ref,
    idx_hbm,
    own_hbm,
    high_x_hbm,
    high_y_hbm,
    phase_ref,
    idx_v,
    stiff_ref,
    mass_ref,
    kh_hbm,
    kl_hbm,
    curl_out,
    mass_out,
    side_x_hbm,
    side_y_hbm,
    gram_out,
    ext,
    acc0,
    acc1,
    acc2,
    acc3,
    gathered,
    terms,
    gram,
    idx_all,
    own_v,
    high_v,
    images,
    kh_ref,
    kl_ref,
    side_x_out,
    side_y_out,
    in_sems,
    out_sems,
):
    accs = (acc0, acc1, acc2, acc3)
    owned = own_v.shape[1]
    face = high_v.shape[2]
    cosine, sine = phase_ref[0:1, :], phase_ref[1:2, :]
    count = count_ref[0, 0]
    capacity = stiff_ref.shape[1]
    idx_s = [idx_all.at[pl.ds(j * capacity, capacity)] for j in range(NLOC)]

    own_in = pltpu.make_async_copy(own_hbm, own_v, in_sems.at[0])
    high_x_in = pltpu.make_async_copy(high_x_hbm, high_v.at[0], in_sems.at[1])
    high_y_in = pltpu.make_async_copy(high_y_hbm, high_v.at[1], in_sems.at[2])
    idx_in = pltpu.make_async_copy(idx_hbm, idx_all, in_sems.at[3])
    own_in.start()
    idx_in.start()
    high_x_in.start()
    high_y_in.start()
    kh_in = pltpu.make_async_copy(kh_hbm, kh_ref, in_sems.at[4])
    kl_in = pltpu.make_async_copy(kl_hbm, kl_ref, in_sems.at[5])
    kh_in.start()
    kl_in.start()

    zero_rows = jnp.zeros((LANES, LANES), jnp.float32)

    @pl.loop(0, ext.shape[0] // LANES, unroll=4)
    def _(b):
        at = pl.multiple_of(b * LANES, LANES)
        for acc in accs:
            acc[pl.ds(at, LANES), :] = zero_rows

    gram[...] = jnp.zeros_like(gram)

    def put_rows(at, block):
        ext[pl.ds(at, LANES), :] = jnp.concatenate([block] * (LANES // ROWS), axis=0).T

    own_in.wait()

    @pl.loop(0, owned // LANES, unroll=16)
    def _(b):
        at = pl.multiple_of(b * LANES, LANES)
        put_rows(at, own_v[:, pl.ds(at, LANES)])

    high_x_in.wait()
    high_y_in.wait()

    @pl.loop(0, face // LANES, unroll=8)
    def _(b):
        at = pl.multiple_of(b * LANES, LANES)
        got = high_v[0, :, pl.ds(at, LANES)]
        real, imag = got[: ROWS // 2], got[ROWS // 2 :]
        turned = jnp.concatenate([cosine * real - sine * imag, sine * real + cosine * imag], axis=0)
        high_v[0, :, pl.ds(at, LANES)] = turned
        put_rows(owned + at, turned)
        put_rows(owned + face + at, high_v[1, :, pl.ds(at, LANES)])

    def idx_row(j, block_id, part):
        row = j * (capacity // LANES) + block_id * (BLOCK // LANES) + part
        return jnp.broadcast_to(idx_v[pl.ds(row, 1), :], (LANES // LANE_SETS, LANES))

    lane_set = lax.broadcasted_iota(jnp.int32, (1, LANES), 1) >> 4
    idx_in.wait()
    kh_in.wait()
    kl_in.wait()

    @pl.loop(0, (count + BLOCK - 1) // BLOCK)
    def _(block_id):
        first = pl.multiple_of(block_id * BLOCK, BLOCK)

        @pl.loop(0, BLOCK, unroll=4)
        def _(e):
            slot = first + e
            for tile in range(GTILES):
                inside = range(8 * tile, min(8 * tile + 8, NLOC))
                row = None
                for i in inside:
                    got = ext[pl.ds(idx_s[i][slot], 1), :]
                    row = got if row is None else jnp.where(lane_set == i % 8, got, row)
                gathered[tile, pl.ds(e, 1), :] = row

        values = jnp.concatenate([gathered[tile] for tile in range(GTILES)], axis=1)
        products = dot_split(split_bf16(values), (kh_ref[...], kl_ref[...]))
        slots = first + lax.broadcasted_iota(jnp.int32, (1, BLOCK), 1)
        live = slots < count
        stiff = jnp.where(live, stiff_ref[:, pl.ds(first, BLOCK)], 0.0)
        mass = jnp.where(live, mass_ref[:, pl.ds(first, BLOCK)], 0.0)
        pair = [jnp.broadcast_to(stiff, (ROWS, BLOCK)), jnp.broadcast_to(mass, (ROWS, BLOCK))]
        coef = jnp.concatenate(pair * LANE_SETS, axis=0).T
        scaled = [products[:, t * LANES : (t + 1) * LANES] * coef for t in range(TILES)]

        names = []
        for t in range(TILES):
            rows = [
                jnp.concatenate([idx_row(j, block_id, part) for part in range(BLOCK // LANES)], axis=1)
                for j in range(LANE_SETS * t, LANE_SETS * t + LANE_SETS)
            ]
            names.append(jnp.concatenate(rows, axis=0).astype(jnp.float32).T)
        for t in range(TILES):
            total = scaled[t]
            for s in range(t):
                total = total + jnp.where(names[s] == names[t], scaled[s], 0.0)
            terms[t] = total

        @pl.loop(0, BLOCK, unroll=16)
        def _(e):
            slot = first + e
            added = [terms[t, pl.ds(e, 1), :] for t in range(TILES)]
            places = [[idx_s[LANE_SETS * t + g][slot] for t in range(TILES)] for g in range(LANE_SETS)]
            held = [[accs[g][pl.ds(places[g][t], 1), :] for t in range(TILES)] for g in range(LANE_SETS)]
            for t in range(TILES):
                for g in range(LANE_SETS):
                    accs[g][pl.ds(places[g][t], 1), :] = held[g][t] + added[t]

    quarter = lax.broadcasted_iota(jnp.int32, (LANES, LANES), 1) >> 5

    def summed(at):
        rows = accs[0][pl.ds(at, LANES), :]
        for g in range(1, LANE_SETS):
            rows = jnp.where(quarter == g, accs[g][pl.ds(at, LANES), :], rows)
        rows = rows.T
        return (rows[:32] + rows[32:64]) + (rows[64:96] + rows[96:])

    def wide(at):
        return jnp.concatenate([summed(at), summed(at + LANES)], axis=1)

    across = (((1,), (1,)), ((), ()))
    dot = functools.partial(lax.dot_general, dimension_numbers=across, preferred_element_type=jnp.float32)

    def add_gram(left, both):
        (lh, ll), (bh, bl) = split_bf16(left), split_bf16(both)
        pieces = dot(jnp.concatenate([lh, ll], axis=0), bh)
        gram[:, : 2 * ROWS] += pieces[:ROWS] + (pieces[ROWS:] + dot(lh, bl))

    step = 2 * LANES

    @pl.loop(0, face // step, unroll=4)
    def _(b):
        at = pl.multiple_of(b * step, step)
        both = wide(owned + at)
        add_gram(high_v[0, :, pl.ds(at, step)], both)
        cos2, sin2 = (jnp.concatenate([row, row], axis=1) for row in (cosine, sine))
        for op in range(2):
            real, imag = both[ROWS * op : ROWS * op + 8], both[ROWS * op + 8 : ROWS * op + ROWS]
            side_x_out[ROWS * op : ROWS * op + 8, pl.ds(at, step)] = cos2 * real + sin2 * imag
            side_x_out[ROWS * op + 8 : ROWS * op + ROWS, pl.ds(at, step)] = cos2 * imag - sin2 * real
        both = wide(owned + face + at)
        add_gram(high_v[1, :, pl.ds(at, step)], both)
        side_y_out[:, pl.ds(at, step)] = both

    side_x_put = pltpu.make_async_copy(side_x_out, side_x_hbm, in_sems.at[6])
    side_y_put = pltpu.make_async_copy(side_y_out, side_y_hbm, in_sems.at[7])
    side_x_put.start()
    side_y_put.start()
    chunk = owned // OUT_CHUNKS

    def out_copies(c):
        cols = pl.ds(c * chunk, chunk)
        return (
            pltpu.make_async_copy(images.at[pl.ds(0, ROWS), cols], curl_out.at[:, cols], out_sems.at[0, c]),
            pltpu.make_async_copy(images.at[pl.ds(ROWS, ROWS), cols], mass_out.at[:, cols], out_sems.at[1, c]),
        )

    for c in range(OUT_CHUNKS):

        @pl.loop(0, chunk // step, unroll=16)
        def _(b):
            at = pl.multiple_of(c * chunk + b * step, step)
            both = wide(at)
            add_gram(own_v[:, pl.ds(at, step)], both)
            images[:, pl.ds(at, step)] = both

        for copy in out_copies(c):
            copy.start()

    total = gram[...]
    of_real, of_imag = total[:8], total[8:]
    odd = ((lax.broadcasted_iota(jnp.int32, (8, LANES), 1) >> 3) & 1) == 1
    gram_out[...] = jnp.where(
        odd, of_real - pltpu.roll(of_imag, 8, 1), of_real + pltpu.roll(of_imag, LANES - 8, 1)
    )
    side_x_put.wait()
    side_y_put.wait()
    for c in range(OUT_CHUNKS):
        for copy in out_copies(c):
            copy.wait()


def part_images(count, phase, idx, own, high_x, high_y, stiff, mass, kh, kl):
    shape = jax.ShapeDtypeStruct
    owned, face = own.shape[1], high_x.shape[1]
    extent = owned + 2 * face
    f32 = jnp.float32
    dma = pltpu.SemaphoreType.DMA
    return pl.pallas_call(
        part_kernel,
        out_shape=(
            shape((ROWS, owned), f32),
            shape((ROWS, owned), f32),
            shape((2 * ROWS, face), f32),
            shape((2 * ROWS, face), f32),
            shape((8, LANES), f32),
        ),
        in_specs=[SMEM, ANY, ANY, ANY, ANY] + [VMEM] * 4 + [ANY] * 2,
        out_specs=(ANY, ANY, ANY, ANY, VMEM),
        scratch_shapes=[pltpu.VMEM((extent, LANES), f32)] * 5
        + [
            pltpu.VMEM((GTILES, BLOCK, LANES), f32),
            pltpu.VMEM((TILES, BLOCK, LANES), f32),
            pltpu.VMEM((ROWS, LANES), f32),
            pltpu.SMEM((idx.size,), jnp.int32),
            pltpu.VMEM((ROWS, owned), f32),
            pltpu.VMEM((2, ROWS, face), f32),
            pltpu.VMEM((2 * ROWS, owned), f32),
            pltpu.VMEM(kh.shape, kh.dtype),
            pltpu.VMEM(kl.shape, kl.dtype),
            pltpu.VMEM((2 * ROWS, face), f32),
            pltpu.VMEM((2 * ROWS, face), f32),
            dma((8,)),
            dma((2, OUT_CHUNKS)),
        ],
        compiler_params=pltpu.CompilerParams(vmem_limit_bytes=VMEM_BYTES),
        name="part_images",
    )(count, idx.reshape(-1), own, high_x, high_y, phase, idx, stiff, mass, kh, kl)


def exchange_kernel(
    side_x_hbm,
    side_y_hbm,
    curl_hbm,
    mass_hbm,
    gram_hbm,
    lows_out,
    gram_out,
    back,
    low,
    held,
    gram_ref,
    sums,
    low_sems,
    side_sems,
    send_sems,
    recv_sems,
):
    face = side_x_hbm.shape[1]
    owned = curl_hbm.shape[1]
    n_px, n_py = lax.axis_size("px"), lax.axis_size("py")
    a, b = lax.axis_index("px"), lax.axis_index("py")
    core, at_y, high = lax.rem(a, 2), lax.rem(a // 2, GROUP), a // (2 * GROUP)
    at_z, side = lax.rem(b, GROUP), b // GROUP

    def along_y(k):
        return {"px": high * (2 * GROUP) + k * 2 + core}

    def along_z(k):
        return {"py": side * GROUP + k}

    def over_rest(k):
        return {"px": (k // 4) * (2 * GROUP) + at_y * 2 + lax.rem(k, 2), "py": lax.rem(k // 2, 2) * GROUP + at_z}

    groups = ((over_rest, high * 4 + side * 2 + core), (along_y, at_y), (along_z, at_z))
    next_x, last_x = {"px": lax.rem(a + 1, n_px)}, {"px": lax.rem(a + n_px - 1, n_px)}
    next_y, last_y = {"py": lax.rem(b + 1, n_py)}, {"py": lax.rem(b + n_py - 1, n_py)}
    gram_in = pltpu.make_async_copy(gram_hbm, gram_ref, low_sems.at[3])
    gram_in.start()
    barrier = pltpu.get_barrier_semaphore()

    def greet(device):
        pl.semaphore_signal(barrier, 1, device_id=device, device_id_type=pl.DeviceIdType.MESH)

    for place, me in groups:
        for k in range(1, GROUP):
            greet(place(lax.rem(me + k, GROUP)))
    greet(next_x)
    greet(last_x)

    @pl.when(b < n_py - 1)
    def _():
        greet(next_y)

    @pl.when(b > 0)
    def _():
        greet(last_y)

    reads = [
        pltpu.make_async_copy(image.at[:, pl.ds(owned - 2 * face, 2 * face)], low.at[op], low_sems.at[op])
        for op, image in enumerate((curl_hbm, mass_hbm))
    ]
    write = pltpu.make_async_copy(low, lows_out, low_sems.at[2])
    for read in reads:
        read.start()
    gram_in.wait()
    peers = 3 * (GROUP - 1) + 2
    pl.semaphore_wait(barrier, peers + jnp.minimum(b, 1) + jnp.minimum(n_py - 1 - b, 1))

    def tile_copy(phase, source, to, at):
        return pltpu.make_async_remote_copy(
            src_ref=source,
            dst_ref=held.at[phase, at],
            send_sem=send_sems.at[phase, to],
            recv_sem=recv_sems.at[phase, at],
            device_id=groups[phase][0](to),
            device_id_type=pl.DeviceIdType.MESH,
        )

    def others(me):
        return [lax.rem(me + k, GROUP) for k in range(1, GROUP)]

    def send_all(phase, source):
        me = groups[phase][1]
        for to in others(me):
            tile_copy(phase, source, to, me).start()
        held[phase, pl.ds(me, 1)] = source[...][None]

    def sum_all(phase, source):
        me = groups[phase][1]
        for other in others(me):
            tile_copy(phase, source, other, other).wait_recv()
        total = held[phase, 0]
        for at in range(1, GROUP):
            total = total + held[phase, at]
        return total

    def side_copy(source, at, device):
        return pltpu.make_async_remote_copy(
            src_ref=source,
            dst_ref=back.at[at],
            send_sem=side_sems.at[0, at],
            recv_sem=side_sems.at[1, at],
            device_id=device,
            device_id_type=pl.DeviceIdType.MESH,
        )

    to_x = side_copy(side_x_hbm, 0, next_x)
    to_y = side_copy(side_y_hbm, 1, next_y)
    send_all(0, gram_ref)
    to_x.start()

    @pl.when(b < n_py - 1)
    def _():
        to_y.start()

    sums[0] = sum_all(0, gram_ref)
    send_all(1, sums.at[0])
    for read in reads:
        read.wait()
    sums[1] = sum_all(1, sums.at[0])
    send_all(2, sums.at[1])
    to_x.wait_recv()
    for op in range(2):
        low[op, :, :face] += back[0, ROWS * op : ROWS * op + ROWS, :]

    @pl.when(b > 0)
    def _():
        to_y.wait_recv()
        for op in range(2):
            low[op, :, face:] += back[1, ROWS * op : ROWS * op + ROWS, :]

    write.start()
    whole = sum_all(2, sums.at[1])
    for op in range(2):
        for part in range(2):
            at = 16 * op + 8 * part
            gram_out[op, part] = whole[:, at : at + 8] / float(n_px * n_py * owned)
    to_x.wait_send()

    @pl.when(b < n_py - 1)
    def _():
        to_y.wait_send()

    for phase, source in enumerate((gram_ref, sums.at[0], sums.at[1])):
        me = groups[phase][1]
        for to in others(me):
            tile_copy(phase, source, to, me).wait_send()
    write.wait()


def exchange(side_x, side_y, curl, mass, gram):
    shape = jax.ShapeDtypeStruct
    f32 = jnp.float32
    dma = pltpu.SemaphoreType.DMA
    face = side_x.shape[1]
    return pl.pallas_call(
        exchange_kernel,
        out_shape=(shape((2, ROWS, 2 * face), f32), shape((2, 2, 8, 8), f32)),
        in_specs=[ANY] * 5,
        out_specs=(ANY, VMEM),
        scratch_shapes=[
            pltpu.VMEM((2, 2 * ROWS, face), f32),
            pltpu.VMEM((2, ROWS, 2 * face), f32),
            pltpu.VMEM((3, GROUP, 8, LANES), f32),
            pltpu.VMEM((8, LANES), f32),
            pltpu.VMEM((2, 8, LANES), f32),
            dma((4,)),
            dma((2, 2)),
            dma((3, GROUP)),
            dma((3, GROUP)),
        ],
        compiler_params=pltpu.CompilerParams(
            collective_id=0, has_side_effects=True, vmem_limit_bytes=VMEM_BYTES
        ),
        name="exchange",
    )(side_x, side_y, curl, mass, gram)


def finish_kernel(curl_in, mass_in, lows, gram_ref, curl_out, mass_out, gram_out, sems):
    width = lows.shape[2]
    writes = [
        pltpu.make_async_copy(lows.at[op], image.at[:, pl.ds(image.shape[1] - width, width)], sems.at[op])
        for op, image in enumerate((curl_out, mass_out))
    ]
    for write in writes:
        write.start()
    gram_out[...] = gram_ref[...]
    for write in writes:
        write.wait()


def finish(curl, mass, lows, gram):
    shape = jax.ShapeDtypeStruct
    return pl.pallas_call(
        finish_kernel,
        out_shape=tuple(shape(value.shape, jnp.float32) for value in (curl, mass, gram)),
        in_specs=[ANY, ANY, VMEM, VMEM],
        out_specs=(ANY, ANY, VMEM),
        scratch_shapes=[pltpu.SemaphoreType.DMA((2,))],
        input_output_aliases={0: 0, 1: 1},
        compiler_params=pltpu.CompilerParams(vmem_limit_bytes=VMEM_BYTES),
        name="finish",
    )(curl, mass, lows, gram)


def on_device(
    trial_block,
    stiff_coef,
    mass_coef,
    elem_count,
    elem_dofs,
    pairing,
    bloch_fraction,
    stiff_mat,
    mass_mat,
):
    owned = trial_block.shape[-1]
    own = trial_block.reshape(ROWS, owned)
    high_x, high_y, phase, idx, kh, kl = begin(
        bloch_fraction,
        own,
        elem_dofs[0].transpose(2, 0, 1),
        pairing.reshape(-1, LANES),
        stiff_mat,
        mass_mat,
    )
    curl, mass, side_x, side_y, gram = part_images(
        elem_count, phase, idx, own, high_x, high_y, stiff_coef[0], mass_coef[0], kh, kl
    )
    lows, gram = exchange(side_x, side_y, curl, mass, gram)
    curl, mass, gram = finish(curl, mass, lows, gram)
    return curl.reshape(trial_block.shape), mass.reshape(trial_block.shape), gram


def solution(mesh):
    return jax.shard_map(
        on_device,
        mesh=mesh,
        in_specs=(
            P("px", "py", None, None, None),
            P("px", "py", None),
            P("px", "py", None),
            P("px", "py"),
            P("px", "py", None, None),
            P(),
            P(),
            P(),
            P(),
        ),
        out_specs=(P("px", "py", None, None, None), P("px", "py", None, None, None), P()),
        check_vma=False,
    )
```

```python
import functools
import math

import jax
import jax.numpy as jnp
from jax import lax
from jax.experimental import pallas as pl
from jax.experimental.pallas import tpu as pltpu
from jax.sharding import PartitionSpec as P

HIGH = lax.Precision.HIGHEST
LANES = 128
ROWS = 16
NLOC = 20
HALO_SLOTS = 128
BLOCK = 512
TILES = 5
GTILES = 3
LANE_SETS = 4

VMEM = pl.BlockSpec(memory_space=pltpu.VMEM)
SMEM = pl.BlockSpec(memory_space=pltpu.SMEM)
ANY = pl.BlockSpec(memory_space=pl.ANY)
VMEM_BYTES = 56 * 2**20
OUT_CHUNKS = 2
GROUP = 8


def split_bf16(value):
    high = value.astype(jnp.bfloat16)
    low = (value - high.astype(jnp.float32)).astype(jnp.bfloat16)
    return high, low


def dot_split(a, b):
    (ah, al), (bh, bl) = a, b
    dot = functools.partial(jnp.dot, preferred_element_type=jnp.float32)
    both = dot(jnp.concatenate([ah, al], axis=0), bh)
    rows = ah.shape[0]
    return both[:rows] + (both[rows:] + dot(ah, bl))


def begin_kernel(
    fraction_ref,
    own_hbm,
    dofs_ref,
    pairing_ref,
    stiff_ref,
    mass_ref,
    high_x,
    high_y,
    phase_out,
    idx_out,
    kh_out,
    kl_out,
    zeros,
    sems,
):
    face = pairing_ref.shape[0] * LANES
    owned = own_hbm.shape[1]
    n_px, n_py = lax.axis_size("px"), lax.axis_size("py")
    a, b = lax.axis_index("px"), lax.axis_index("py")
    below_x, above_x = lax.rem(a + n_px - 1, n_px), lax.rem(a + 1, n_px)
    below_y, above_y = lax.rem(b + n_py - 1, n_py), lax.rem(b + 1, n_py)

    barrier = pltpu.get_barrier_semaphore()

    def greet(axis, to):
        pl.semaphore_signal(barrier, 1, device_id={axis: to}, device_id_type=pl.DeviceIdType.MESH)

    greet("px", below_x)
    greet("px", above_x)

    @pl.when(b > 0)
    def _():
        greet("py", below_y)

    @pl.when(b < n_py - 1)
    def _():
        greet("py", above_y)

    pl.semaphore_wait(barrier, 2 + jnp.minimum(b, 1) + jnp.minimum(n_py - 1 - b, 1))

    def face_copy(first, target, at, axis, to):
        return pltpu.make_async_remote_copy(
            src_ref=own_hbm.at[:, pl.ds(first, face)],
            dst_ref=target,
            send_sem=sems.at[2 * at],
            recv_sem=sems.at[2 * at + 1],
            device_id={axis: to},
            device_id_type=pl.DeviceIdType.MESH,
        )

    to_x = face_copy(owned - 2 * face, high_x, 0, "px", below_x)
    to_y = face_copy(owned - face, high_y, 1, "py", below_y)
    no_y = pltpu.make_async_copy(zeros, high_y, sems.at[4])
    to_x.start()

    @pl.when(b > 0)
    def _():
        to_y.start()

    @pl.when(b == n_py - 1)
    def _():
        zeros[...] = jnp.zeros_like(zeros)
        no_y.start()

    at_end = jnp.broadcast_to(a, (1, LANES)) == n_px - 1
    above = jnp.broadcast_to(fraction_ref[0], (1, LANES)).astype(jnp.float32)
    below = jnp.broadcast_to(fraction_ref[1], (1, LANES)).astype(jnp.float32)
    angle = 2.0 * math.pi * above / below
    phase_out[0:1, :] = jnp.where(at_end, jnp.cos(angle), 1.0)
    phase_out[1:2, :] = jnp.where(at_end, jnp.sin(angle), 0.0)

    blocks = idx_out.shape[0] // NLOC
    for j in range(NLOC):
        for block in range(blocks):
            row = j * blocks + block
            idx_out[row : row + 1, :] = dofs_ref[j, :, block * LANES : (block + 1) * LANES]
    heads = pl.ds(0, NLOC, stride=blocks)
    head = idx_out[heads, :]
    spot = head - owned
    local = spot & (LANES - 1)
    found = jnp.zeros_like(head)
    for row in range(pairing_ref.shape[0]):
        values = jnp.broadcast_to(pairing_ref[row : row + 1, :], head.shape)
        here = jnp.take_along_axis(values, local, axis=1)
        found = jnp.where((spot >> 7) == row, here + owned, found)
    wraps = (spot >= 0) & (spot < face) & (jnp.broadcast_to(a, head.shape) == n_px - 1)
    idx_out[heads, :] = jnp.where(wraps, found, head)

    grow = lax.broadcasted_iota(jnp.int32, (GTILES * LANES, NLOC), 0)
    gcol = lax.broadcasted_iota(jnp.int32, (GTILES * LANES, NLOC), 1)
    spread_i = ((grow >> 4) == gcol).astype(jnp.float32)
    trow = lax.broadcasted_iota(jnp.int32, (NLOC, TILES * LANES), 0)
    tcol = lax.broadcasted_iota(jnp.int32, (NLOC, TILES * LANES), 1)
    spread_j = ((tcol >> 5) == trow).astype(jnp.float32)
    dot = functools.partial(jnp.dot, precision=HIGH, preferred_element_type=jnp.float32)
    stiff = dot(dot(spread_i, stiff_ref[...].T), spread_j)
    mass = dot(dot(spread_i, mass_ref[...].T), spread_j)
    krow = lax.broadcasted_iota(jnp.int32, (GTILES * LANES, TILES * LANES), 0)
    kcol = lax.broadcasted_iota(jnp.int32, (GTILES * LANES, TILES * LANES), 1)
    both = jnp.where(((kcol >> 4) & 1) == 0, stiff, mass)
    both = jnp.where((krow & 15) == (kcol & 15), both, 0.0)
    kh_out[...], kl_out[...] = split_bf16(both)

    to_x.wait()

    @pl.when(b > 0)
    def _():
        to_y.wait_send()

    @pl.when(b < n_py - 1)
    def _():
        to_y.wait_recv()

    @pl.when(b == n_py - 1)
    def _():
        no_y.wait()


def begin(fraction, own, dofs, pairing, stiff_mat, mass_mat):
    shape = jax.ShapeDtypeStruct
    high = shape((ROWS, pairing.size), jnp.float32)
    spread = shape((GTILES * LANES, TILES * LANES), jnp.bfloat16)
    return pl.pallas_call(
        begin_kernel,
        out_shape=(high, high, shape((2, LANES), jnp.float32), shape((dofs.size // LANES, LANES), jnp.int32), spread, spread),
        in_specs=[SMEM, ANY, VMEM, VMEM, VMEM, VMEM],
        out_specs=(ANY, ANY, VMEM, VMEM, VMEM, VMEM),
        scratch_shapes=[
            pltpu.VMEM(high.shape, jnp.float32),
            pltpu.SemaphoreType.DMA((5,)),
        ],
        compiler_params=pltpu.CompilerParams(
            collective_id=1, has_side_effects=True, vmem_limit_bytes=VMEM_BYTES
        ),
        name="begin",
    )(fraction, own, dofs, pairing, stiff_mat, mass_mat)


def part_kernel(
    count_ref,
    idx_hbm,
    own_hbm,
    high_x_hbm,
    high_y_hbm,
    phase_ref,
    idx_v,
    stiff_ref,
    mass_ref,
    kh_hbm,
    kl_hbm,
    curl_out,
    mass_out,
    side_x_hbm,
    side_y_hbm,
    gram_out,
    ext,
    acc0,
    acc1,
    acc2,
    acc3,
    gathered,
    terms,
    gram,
    idx_all,
    own_v,
    high_v,
    images,
    kh_ref,
    kl_ref,
    side_x_out,
    side_y_out,
    in_sems,
    out_sems,
):
    accs = (acc0, acc1, acc2, acc3)
    owned = own_v.shape[1]
    face = high_v.shape[2]
    cosine, sine = phase_ref[0:1, :], phase_ref[1:2, :]
    count = count_ref[0, 0]
    capacity = stiff_ref.shape[1]
    idx_s = [idx_all.at[pl.ds(j * capacity, capacity)] for j in range(NLOC)]

    own_in = pltpu.make_async_copy(own_hbm, own_v, in_sems.at[0])
    high_x_in = pltpu.make_async_copy(high_x_hbm, high_v.at[0], in_sems.at[1])
    high_y_in = pltpu.make_async_copy(high_y_hbm, high_v.at[1], in_sems.at[2])
    idx_in = pltpu.make_async_copy(idx_hbm, idx_all, in_sems.at[3])
    own_in.start()
    idx_in.start()
    high_x_in.start()
    high_y_in.start()
    kh_in = pltpu.make_async_copy(kh_hbm, kh_ref, in_sems.at[4])
    kl_in = pltpu.make_async_copy(kl_hbm, kl_ref, in_sems.at[5])
    kh_in.start()
    kl_in.start()

    zero_rows = jnp.zeros((LANES, LANES), jnp.float32)

    @pl.loop(0, ext.shape[0] // LANES, unroll=4)
    def _(b):
        at = pl.multiple_of(b * LANES, LANES)
        for acc in accs:
            acc[pl.ds(at, LANES), :] = zero_rows

    gram[...] = jnp.zeros_like(gram)

    def put_rows(at, block):
        ext[pl.ds(at, LANES), :] = jnp.concatenate([block] * (LANES // ROWS), axis=0).T

    own_in.wait()

    @pl.loop(0, owned // LANES, unroll=16)
    def _(b):
        at = pl.multiple_of(b * LANES, LANES)
        put_rows(at, own_v[:, pl.ds(at, LANES)])

    high_x_in.wait()
    high_y_in.wait()

    @pl.loop(0, face // LANES, unroll=8)
    def _(b):
        at = pl.multiple_of(b * LANES, LANES)
        got = high_v[0, :, pl.ds(at, LANES)]
        real, imag = got[: ROWS // 2], got[ROWS // 2 :]
        turned = jnp.concatenate([cosine * real - sine * imag, sine * real + cosine * imag], axis=0)
        high_v[0, :, pl.ds(at, LANES)] = turned
        put_rows(owned + at, turned)
        put_rows(owned + face + at, high_v[1, :, pl.ds(at, LANES)])

    def idx_row(j, block_id, part):
        row = j * (capacity // LANES) + block_id * (BLOCK // LANES) + part
        return jnp.broadcast_to(idx_v[pl.ds(row, 1), :], (LANES // LANE_SETS, LANES))

    lane_set = lax.broadcasted_iota(jnp.int32, (1, LANES), 1) >> 4
    idx_in.wait()
    kh_in.wait()
    kl_in.wait()

    @pl.loop(0, (count + BLOCK - 1) // BLOCK)
    def _(block_id):
        first = pl.multiple_of(block_id * BLOCK, BLOCK)

        @pl.loop(0, BLOCK, unroll=4)
        def _(e):
            slot = first + e
            for tile in range(GTILES):
                inside = range(8 * tile, min(8 * tile + 8, NLOC))
                row = None
                for i in inside:
                    got = ext[pl.ds(idx_s[i][slot], 1), :]
                    row = got if row is None else jnp.where(lane_set == i % 8, got, row)
                gathered[tile, pl.ds(e, 1), :] = row

        values = jnp.concatenate([gathered[tile] for tile in range(GTILES)], axis=1)
        products = dot_split(split_bf16(values), (kh_ref[...], kl_ref[...]))
        slots = first + lax.broadcasted_iota(jnp.int32, (1, BLOCK), 1)
        live = slots < count
        stiff = jnp.where(live, stiff_ref[:, pl.ds(first, BLOCK)], 0.0)
        mass = jnp.where(live, mass_ref[:, pl.ds(first, BLOCK)], 0.0)
        pair = [jnp.broadcast_to(stiff, (ROWS, BLOCK)), jnp.broadcast_to(mass, (ROWS, BLOCK))]
        coef = jnp.concatenate(pair * LANE_SETS, axis=0).T
        scaled = [products[:, t * LANES : (t + 1) * LANES] * coef for t in range(TILES)]

        names = []
        for t in range(TILES):
            rows = [
                jnp.concatenate([idx_row(j, block_id, part) for part in range(BLOCK // LANES)], axis=1)
                for j in range(LANE_SETS * t, LANE_SETS * t + LANE_SETS)
            ]
            names.append(jnp.concatenate(rows, axis=0).astype(jnp.float32).T)
        for t in range(TILES):
            total = scaled[t]
            for s in range(t):
                total = total + jnp.where(names[s] == names[t], scaled[s], 0.0)
            terms[t] = total

        @pl.loop(0, BLOCK, unroll=16)
        def _(e):
            slot = first + e
            added = [terms[t, pl.ds(e, 1), :] for t in range(TILES)]
            places = [[idx_s[LANE_SETS * t + g][slot] for t in range(TILES)] for g in range(LANE_SETS)]
            held = [[accs[g][pl.ds(places[g][t], 1), :] for t in range(TILES)] for g in range(LANE_SETS)]
            for t in range(TILES):
                for g in range(LANE_SETS):
                    accs[g][pl.ds(places[g][t], 1), :] = held[g][t] + added[t]

    quarter = lax.broadcasted_iota(jnp.int32, (LANES, LANES), 1) >> 5

    def summed(at):
        rows = accs[0][pl.ds(at, LANES), :]
        for g in range(1, LANE_SETS):
            rows = jnp.where(quarter == g, accs[g][pl.ds(at, LANES), :], rows)
        rows = rows.T
        return (rows[:32] + rows[32:64]) + (rows[64:96] + rows[96:])

    def wide(at):
        return jnp.concatenate([summed(at), summed(at + LANES)], axis=1)

    across = (((1,), (1,)), ((), ()))
    dot = functools.partial(lax.dot_general, dimension_numbers=across, preferred_element_type=jnp.float32)

    def add_gram(left, both):
        (lh, ll), (bh, bl) = split_bf16(left), split_bf16(both)
        pieces = dot(jnp.concatenate([lh, ll], axis=0), bh)
        gram[:, : 2 * ROWS] += pieces[:ROWS] + (pieces[ROWS:] + dot(lh, bl))

    step = 2 * LANES

    @pl.loop(0, face // step, unroll=4)
    def _(b):
        at = pl.multiple_of(b * step, step)
        both = wide(owned + at)
        add_gram(high_v[0, :, pl.ds(at, step)], both)
        cos2, sin2 = (jnp.concatenate([row, row], axis=1) for row in (cosine, sine))
        for op in range(2):
            real, imag = both[ROWS * op : ROWS * op + 8], both[ROWS * op + 8 : ROWS * op + ROWS]
            side_x_out[ROWS * op : ROWS * op + 8, pl.ds(at, step)] = cos2 * real + sin2 * imag
            side_x_out[ROWS * op + 8 : ROWS * op + ROWS, pl.ds(at, step)] = cos2 * imag - sin2 * real
        both = wide(owned + face + at)
        add_gram(high_v[1, :, pl.ds(at, step)], both)
        side_y_out[:, pl.ds(at, step)] = both

    side_x_put = pltpu.make_async_copy(side_x_out, side_x_hbm, in_sems.at[6])
    side_y_put = pltpu.make_async_copy(side_y_out, side_y_hbm, in_sems.at[7])
    side_x_put.start()
    side_y_put.start()
    chunk = owned // OUT_CHUNKS

    def out_copies(c):
        cols = pl.ds(c * chunk, chunk)
        return (
            pltpu.make_async_copy(images.at[pl.ds(0, ROWS), cols], curl_out.at[:, cols], out_sems.at[0, c]),
            pltpu.make_async_copy(images.at[pl.ds(ROWS, ROWS), cols], mass_out.at[:, cols], out_sems.at[1, c]),
        )

    for c in range(OUT_CHUNKS):

        @pl.loop(0, chunk // step, unroll=16)
        def _(b):
            at = pl.multiple_of(c * chunk + b * step, step)
            both = wide(at)
            add_gram(own_v[:, pl.ds(at, step)], both)
            images[:, pl.ds(at, step)] = both

        for copy in out_copies(c):
            copy.start()

    total = gram[...]
    of_real, of_imag = total[:8], total[8:]
    odd = ((lax.broadcasted_iota(jnp.int32, (8, LANES), 1) >> 3) & 1) == 1
    gram_out[...] = jnp.where(
        odd, of_real - pltpu.roll(of_imag, 8, 1), of_real + pltpu.roll(of_imag, LANES - 8, 1)
    )
    side_x_put.wait()
    side_y_put.wait()
    for c in range(OUT_CHUNKS):
        for copy in out_copies(c):
            copy.wait()


def part_images(count, phase, idx, own, high_x, high_y, stiff, mass, kh, kl):
    shape = jax.ShapeDtypeStruct
    owned, face = own.shape[1], high_x.shape[1]
    extent = owned + 2 * face
    f32 = jnp.float32
    dma = pltpu.SemaphoreType.DMA
    return pl.pallas_call(
        part_kernel,
        out_shape=(
            shape((ROWS, owned), f32),
            shape((ROWS, owned), f32),
            shape((2 * ROWS, face), f32),
            shape((2 * ROWS, face), f32),
            shape((8, LANES), f32),
        ),
        in_specs=[SMEM, ANY, ANY, ANY, ANY] + [VMEM] * 4 + [ANY] * 2,
        out_specs=(ANY, ANY, ANY, ANY, VMEM),
        scratch_shapes=[pltpu.VMEM((extent, LANES), f32)] * 5
        + [
            pltpu.VMEM((GTILES, BLOCK, LANES), f32),
            pltpu.VMEM((TILES, BLOCK, LANES), f32),
            pltpu.VMEM((ROWS, LANES), f32),
            pltpu.SMEM((idx.size,), jnp.int32),
            pltpu.VMEM((ROWS, owned), f32),
            pltpu.VMEM((2, ROWS, face), f32),
            pltpu.VMEM((2 * ROWS, owned), f32),
            pltpu.VMEM(kh.shape, kh.dtype),
            pltpu.VMEM(kl.shape, kl.dtype),
            pltpu.VMEM((2 * ROWS, face), f32),
            pltpu.VMEM((2 * ROWS, face), f32),
            dma((8,)),
            dma((2, OUT_CHUNKS)),
        ],
        compiler_params=pltpu.CompilerParams(vmem_limit_bytes=VMEM_BYTES),
        name="part_images",
    )(count, idx.reshape(-1), own, high_x, high_y, phase, idx, stiff, mass, kh, kl)


def exchange_kernel(
    side_x_hbm,
    side_y_hbm,
    curl_hbm,
    mass_hbm,
    gram_hbm,
    lows_out,
    gram_out,
    back,
    low,
    held,
    gram_ref,
    sums,
    low_sems,
    side_sems,
    send_sems,
    recv_sems,
):
    face = side_x_hbm.shape[1]
    owned = curl_hbm.shape[1]
    n_px, n_py = lax.axis_size("px"), lax.axis_size("py")
    a, b = lax.axis_index("px"), lax.axis_index("py")
    core, at_y, high = lax.rem(a, 2), lax.rem(a // 2, GROUP), a // (2 * GROUP)
    at_z, side = lax.rem(b, GROUP), b // GROUP

    def along_y(k):
        return {"px": high * (2 * GROUP) + k * 2 + core}

    def along_z(k):
        return {"py": side * GROUP + k}

    def over_rest(k):
        return {"px": (k // 4) * (2 * GROUP) + at_y * 2 + lax.rem(k, 2), "py": lax.rem(k // 2, 2) * GROUP + at_z}

    groups = ((over_rest, high * 4 + side * 2 + core), (along_y, at_y), (along_z, at_z))
    next_x, last_x = {"px": lax.rem(a + 1, n_px)}, {"px": lax.rem(a + n_px - 1, n_px)}
    next_y, last_y = {"py": lax.rem(b + 1, n_py)}, {"py": lax.rem(b + n_py - 1, n_py)}
    gram_in = pltpu.make_async_copy(gram_hbm, gram_ref, low_sems.at[3])
    gram_in.start()
    barrier = pltpu.get_barrier_semaphore()

    def greet(device):
        pl.semaphore_signal(barrier, 1, device_id=device, device_id_type=pl.DeviceIdType.MESH)

    far_first = sorted(range(1, GROUP), key=lambda k: -min(k, GROUP - k))
    for place, me in reversed(groups):
        for k in far_first:
            greet(place(lax.rem(me + k, GROUP)))
    greet(next_x)
    greet(last_x)

    @pl.when(b < n_py - 1)
    def _():
        greet(next_y)

    @pl.when(b > 0)
    def _():
        greet(last_y)

    reads = [
        pltpu.make_async_copy(image.at[:, pl.ds(owned - 2 * face, 2 * face)], low.at[op], low_sems.at[op])
        for op, image in enumerate((curl_hbm, mass_hbm))
    ]
    write = pltpu.make_async_copy(low, lows_out, low_sems.at[2])
    for read in reads:
        read.start()
    gram_in.wait()
    peers = 3 * (GROUP - 1) + 2
    pl.semaphore_wait(barrier, peers + jnp.minimum(b, 1) + jnp.minimum(n_py - 1 - b, 1))

    def tile_copy(phase, source, to, at):
        return pltpu.make_async_remote_copy(
            src_ref=source,
            dst_ref=held.at[phase, at],
            send_sem=send_sems.at[phase, to],
            recv_sem=recv_sems.at[phase, at],
            device_id=groups[phase][0](to),
            device_id_type=pl.DeviceIdType.MESH,
        )

    def others(me):
        return [lax.rem(me + k, GROUP) for k in far_first]

    def send_all(phase, source):
        me = groups[phase][1]
        for to in others(me):
            tile_copy(phase, source, to, me).start()
        held[phase, pl.ds(me, 1)] = source[...][None]

    def sum_all(phase, source):
        me = groups[phase][1]
        for other in others(me):
            tile_copy(phase, source, other, other).wait_recv()
        total = held[phase, 0]
        for at in range(1, GROUP):
            total = total + held[phase, at]
        return total

    def side_copy(source, at, device):
        return pltpu.make_async_remote_copy(
            src_ref=source,
            dst_ref=back.at[at],
            send_sem=side_sems.at[0, at],
            recv_sem=side_sems.at[1, at],
            device_id=device,
            device_id_type=pl.DeviceIdType.MESH,
        )

    to_x = side_copy(side_x_hbm, 0, next_x)
    to_y = side_copy(side_y_hbm, 1, next_y)
    send_all(0, gram_ref)
    to_x.start()

    @pl.when(b < n_py - 1)
    def _():
        to_y.start()

    sums[0] = sum_all(0, gram_ref)
    send_all(1, sums.at[0])
    for read in reads:
        read.wait()
    sums[1] = sum_all(1, sums.at[0])
    send_all(2, sums.at[1])
    to_x.wait_recv()
    for op in range(2):
        low[op, :, :face] += back[0, ROWS * op : ROWS * op + ROWS, :]

    @pl.when(b > 0)
    def _():
        to_y.wait_recv()
        for op in range(2):
            low[op, :, face:] += back[1, ROWS * op : ROWS * op + ROWS, :]

    write.start()
    whole = sum_all(2, sums.at[1])
    for op in range(2):
        for part in range(2):
            at = 16 * op + 8 * part
            gram_out[op, part] = whole[:, at : at + 8] / float(n_px * n_py * owned)
    to_x.wait_send()

    @pl.when(b < n_py - 1)
    def _():
        to_y.wait_send()

    for phase, source in enumerate((gram_ref, sums.at[0], sums.at[1])):
        me = groups[phase][1]
        for to in others(me):
            tile_copy(phase, source, to, me).wait_send()
    write.wait()


def exchange(side_x, side_y, curl, mass, gram):
    shape = jax.ShapeDtypeStruct
    f32 = jnp.float32
    dma = pltpu.SemaphoreType.DMA
    face = side_x.shape[1]
    return pl.pallas_call(
        exchange_kernel,
        out_shape=(shape((2, ROWS, 2 * face), f32), shape((2, 2, 8, 8), f32)),
        in_specs=[ANY] * 5,
        out_specs=(ANY, VMEM),
        scratch_shapes=[
            pltpu.VMEM((2, 2 * ROWS, face), f32),
            pltpu.VMEM((2, ROWS, 2 * face), f32),
            pltpu.VMEM((3, GROUP, 8, LANES), f32),
            pltpu.VMEM((8, LANES), f32),
            pltpu.VMEM((2, 8, LANES), f32),
            dma((4,)),
            dma((2, 2)),
            dma((3, GROUP)),
            dma((3, GROUP)),
        ],
        compiler_params=pltpu.CompilerParams(
            collective_id=0, has_side_effects=True, vmem_limit_bytes=VMEM_BYTES
        ),
        name="exchange",
    )(side_x, side_y, curl, mass, gram)


def finish_kernel(curl_in, mass_in, lows, gram_ref, curl_out, mass_out, gram_out, sems):
    width = lows.shape[2]
    writes = [
        pltpu.make_async_copy(lows.at[op], image.at[:, pl.ds(image.shape[1] - width, width)], sems.at[op])
        for op, image in enumerate((curl_out, mass_out))
    ]
    for write in writes:
        write.start()
    gram_out[...] = gram_ref[...]
    for write in writes:
        write.wait()


def finish(curl, mass, lows, gram):
    shape = jax.ShapeDtypeStruct
    return pl.pallas_call(
        finish_kernel,
        out_shape=tuple(shape(value.shape, jnp.float32) for value in (curl, mass, gram)),
        in_specs=[ANY, ANY, VMEM, VMEM],
        out_specs=(ANY, ANY, VMEM),
        scratch_shapes=[pltpu.SemaphoreType.DMA((2,))],
        input_output_aliases={0: 0, 1: 1},
        compiler_params=pltpu.CompilerParams(vmem_limit_bytes=VMEM_BYTES),
        name="finish",
    )(curl, mass, lows, gram)


def on_device(
    trial_block,
    stiff_coef,
    mass_coef,
    elem_count,
    elem_dofs,
    pairing,
    bloch_fraction,
    stiff_mat,
    mass_mat,
):
    owned = trial_block.shape[-1]
    own = trial_block.reshape(ROWS, owned)
    high_x, high_y, phase, idx, kh, kl = begin(
        bloch_fraction,
        own,
        elem_dofs[0].transpose(2, 0, 1),
        pairing.reshape(-1, LANES),
        stiff_mat,
        mass_mat,
    )
    curl, mass, side_x, side_y, gram = part_images(
        elem_count, phase, idx, own, high_x, high_y, stiff_coef[0], mass_coef[0], kh, kl
    )
    lows, gram = exchange(side_x, side_y, curl, mass, gram)
    curl, mass, gram = finish(curl, mass, lows, gram)
    return curl.reshape(trial_block.shape), mass.reshape(trial_block.shape), gram


def solution(mesh):
    return jax.shard_map(
        on_device,
        mesh=mesh,
        in_specs=(
            P("px", "py", None, None, None),
            P("px", "py", None),
            P("px", "py", None),
            P("px", "py"),
            P("px", "py", None, None),
            P(),
            P(),
            P(),
            P(),
        ),
        out_specs=(P("px", "py", None, None, None), P("px", "py", None, None, None), P()),
        check_vma=False,
    )
```
